32 devices in a mesh: dp: 16 (over z, x, core), head: 2 (over y).
Axes of the slice: x: 2, y: 2, z: 4, core: 2. Of those that a mesh axis runs over, the one named last changes fastest.
Arguments:
- tokens: bfloat16 [128, 608, 256], P(('dp', 'head')), may hold values from -6 to 6
- crop_side: int32 [128, 8], P(('dp', 'head')), may hold values from 6 to 14, as said below
- cotangent: bfloat16 [128, 608, 256], P(('dp', 'head')), may hold values from -6 to 6
- ln1_gain: float32 [2, 256], replicated, may hold values from 0.25 to 1.75
- ln1_bias: float32 [2, 256], replicated, may hold values from -1.75 to 1.75
- qkv_weight: bfloat16 [2, 256, 768], replicated, may hold values from -0.5 to 0.5
- lepe_weight: float32 [2, 9, 256], replicated, may hold values from -1.5 to 1.5
- lepe_bias: float32 [2, 256], replicated, may hold values from -3 to 3
- proj_weight: bfloat16 [2, 256, 256], replicated, may hold values from -0.5 to 0.5
- proj_bias: float32 [2, 256], replicated, may hold values from -3 to 3
- ln2_gain: float32 [2, 256], replicated, may hold values from 0.25 to 1.75
- ln2_bias: float32 [2, 256], replicated, may hold values from -1.75 to 1.75
- fc1_weight: bfloat16 [2, 256, 1024], replicated, may hold values from -0.375 to 0.375
- fc1_bias: float32 [2, 1024], replicated, may hold values from -3 to 3
- fc2_weight: bfloat16 [2, 1024, 256], replicated, may hold values from -0.25 to 0.25
- fc2_bias: float32 [2, 256], replicated, may hold values from -3 to 3
Outputs:
- out: bfloat16 [128, 608, 256], P(('dp', 'head'))
- input_grad: float32 [128, 608, 256], P(('dp', 'head'))
- ln1_gain_grad: float32 [2, 256], replicated
- ln1_bias_grad: float32 [2, 256], replicated
- qkv_weight_grad: float32 [2, 256, 768], replicated
- lepe_weight_grad: float32 [2, 9, 256], replicated
- lepe_bias_grad: float32 [2, 256], replicated
- proj_weight_grad: float32 [2, 256, 256], replicated
- proj_bias_grad: float32 [2, 256], replicated
- ln2_gain_grad: float32 [2, 256], replicated
- ln2_bias_grad: float32 [2, 256], replicated
- fc1_weight_grad: float32 [2, 256, 1024], replicated
- fc1_bias_grad: float32 [2, 1024], replicated
- fc2_weight_grad: float32 [2, 1024, 256], replicated
- fc2_bias_grad: float32 [2, 256], replicated
The draws below stay inside these ranges and needn't reach their ends.
Inputs may be any that keep to these rules, and one draw needn't show every extreme that they name: `crop_side`: each image has 2 crops of side 14 and 6 crops of side 6, in an order drawn for each image.
All inputs are finite; a program needn't handle non-finite values.
Results may differ from the reference program's by a relative error of at most 0.017.
Values may be sent and summed in bfloat16 or wider, within the bound.
A program may use at most 192 MiB of HBM per device.

```python
import math
import jax
import jax.numpy as jnp
from jax import lax

D = 256
HEADS = 8
HEAD_DIM = 32
FF = 1024
SW = 7
BIG = 14
SMALL = 6
CROPS = 8
BIG_CROPS = 2
LAYERS = 2
TOK_IMG = 608
IMAGES = 128
TOKENS = 77824


def draw_crop_side(key, part):
    key = jax.random.fold_in(key, 11)
    scores = jax.random.randint(key, (IMAGES, CROPS), 0, 1 << 20) * CROPS + jnp.arange(CROPS, dtype=jnp.int32)[None, :]
    ranking = jnp.argsort(scores, axis=1, stable=True)
    return jnp.where(ranking < BIG_CROPS, BIG, SMALL).astype(jnp.int32)


def levels(key, dims, cuts, low, largest):
    level = 1.0
    for position, parts in cuts:
        draws = jax.random.uniform(jax.random.fold_in(jax.random.fold_in(key, 6), position), (parts,), jnp.float32, low / len(cuts), largest / len(cuts))
        level = level * jnp.repeat(jnp.exp(draws), dims[position] // parts).reshape((-1,) + (1,) * (len(dims) - 1 - position))
    return level


def scatter_about(key, extent, scale, most, split=(), held_as=jnp.bfloat16):
    drawn = scale * jax.random.normal(key, extent, jnp.float32)
    if split:
        drawn = drawn * levels(key, extent, split, -0.22, 0.18)
    return jnp.clip(drawn, -most, most).astype(held_as)


def setup_inputs(seed: int = 0) -> dict:
    seeds = jax.random.split(jax.random.key(seed), 17)
    tokens = scatter_about(seeds[0], (IMAGES, TOK_IMG, D), 1.0, 6.0, ((0, 32),))
    crop_side = draw_crop_side(jax.random.fold_in(seeds[16], 71), 0)
    cotangent = scatter_about(seeds[2], (IMAGES, TOK_IMG, D), 1.0, 6.0, ((0, 32),))
    ln1_gain = jnp.clip(1.0 + 0.15 * jax.random.normal(seeds[3], (LAYERS, D), jnp.float32), 0.25, 1.75)
    ln1_bias = scatter_about(seeds[4], (LAYERS, D), 0.3, 1.75, (), jnp.float32)
    qkv_weight = scatter_about(seeds[5], (LAYERS, D, 3 * D), (D // 2) ** -0.5, 0.5)
    lepe_weight = scatter_about(seeds[6], (LAYERS, 9, D), 0.25, 1.5, (), jnp.float32)
    lepe_bias = scatter_about(seeds[7], (LAYERS, D), 0.5, 3.0, (), jnp.float32)
    proj_weight = scatter_about(seeds[8], (LAYERS, D, D), (D // 2) ** -0.5, 0.5)
    proj_bias = scatter_about(seeds[9], (LAYERS, D), 0.5, 3.0, (), jnp.float32)
    ln2_gain = jnp.clip(1.0 + 0.15 * jax.random.normal(seeds[10], (LAYERS, D), jnp.float32), 0.25, 1.75)
    ln2_bias = scatter_about(seeds[11], (LAYERS, D), 0.3, 1.75, (), jnp.float32)
    fc1_weight = scatter_about(seeds[12], (LAYERS, D, FF), D ** -0.5, 0.375)
    fc1_bias = scatter_about(seeds[13], (LAYERS, FF), 0.5, 3.0, (), jnp.float32)
    fc2_weight = scatter_about(seeds[14], (LAYERS, FF, D), (FF // 2) ** -0.5, 0.25)
    fc2_bias = scatter_about(seeds[15], (LAYERS, D), 0.5, 3.0, (), jnp.float32)
    return dict(tokens=tokens, crop_side=crop_side, cotangent=cotangent, ln1_gain=ln1_gain, ln1_bias=ln1_bias, qkv_weight=qkv_weight, lepe_weight=lepe_weight, lepe_bias=lepe_bias, proj_weight=proj_weight, proj_bias=proj_bias, ln2_gain=ln2_gain, ln2_bias=ln2_bias, fc1_weight=fc1_weight, fc1_bias=fc1_bias, fc2_weight=fc2_weight, fc2_bias=fc2_bias)


HIGHEST = lax.Precision.HIGHEST
EPSILON = 1e-05

@jax.custom_vjp
def low(v):
    return lax.optimization_barrier(v.astype(jnp.bfloat16)).astype(jnp.float32)

@jax.custom_vjp
def low_back(v):
    return v

def low_keep(v):
    return (low(v), None)

def low_pass(kept, grad):
    return (grad,)

def back_keep(v):
    return (v, None)

def back_low(kept, grad):
    return (low(grad),)
low.defvjp(low_keep, low_pass)
low_back.defvjp(back_keep, back_low)

def normalize(values, gain_vec, shift_vec):
    center = values - lax.optimization_barrier(jnp.mean(values, axis=-1, keepdims=True))
    spread = lax.optimization_barrier(jnp.mean(center * center, axis=-1, keepdims=True))
    return center * lax.rsqrt(spread + EPSILON) * gain_vec + shift_vec

def layout(sides):
    crop_area = sides * sides
    crop_ends = jnp.cumsum(crop_area).astype(jnp.int32)
    crop_starts = crop_ends - crop_area
    positions = jnp.arange(TOK_IMG, dtype=jnp.int32)
    crop_of = lax.optimization_barrier(jnp.sum((positions[:, None] >= crop_ends[None, :]).astype(jnp.int32), axis=1)).astype(jnp.int32)
    chosen = (crop_of[:, None] == jnp.arange(CROPS, dtype=jnp.int32)[None, :]).astype(jnp.int32)
    start_of = lax.optimization_barrier(jnp.sum(chosen * crop_starts[None, :], axis=1)).astype(jnp.int32)
    side_of = lax.optimization_barrier(jnp.sum(chosen * sides[None, :], axis=1)).astype(jnp.int32)
    offset = positions - start_of
    return (positions, crop_of, offset // side_of, offset % side_of, side_of, start_of)

def windows(sides, vertical):
    positions, crop_of, row_of, column_of, side_of, start_of = layout(sides)
    stripe_of = jnp.where(vertical, column_of // SW, row_of // SW)
    window = crop_of * TOK_IMG + stripe_of
    places = []
    usable = []
    for step_row in (-1, 0, 1):
        for step_col in (-1, 0, 1):
            row_to = row_of + step_row
            column_to = column_of + step_col
            inside = (row_to >= 0) & (row_to < side_of) & (column_to >= 0) & (column_to < side_of)
            stripe_to = jnp.where(vertical, column_to // SW, row_to // SW)
            usable_now = inside & (stripe_to == stripe_of)
            places.append(jnp.where(usable_now, start_of + row_to * side_of + column_to, positions).astype(jnp.int32))
            usable.append(usable_now)
    return (window, jnp.stack(places), jnp.stack(usable).astype(jnp.float32))

def attend_image(packed, sides, w_lepe, b_lepe):
    group_width = D // 2
    group_heads = HEADS // 2
    outputs = []
    for group_index in range(2):
        low_edge = group_index * group_width
        group_part = packed[:, :, low_edge:low_edge + group_width]
        window, places, usable = windows(sides, group_index == 1)
        queries = group_part[:, 0].reshape(TOK_IMG, group_heads, HEAD_DIM)
        keys_in = group_part[:, 1].reshape(TOK_IMG, group_heads, HEAD_DIM)
        values_in = group_part[:, 2]
        raw = jnp.einsum('thd,uhd->htu', queries, keys_in, precision=HIGHEST)
        scores = low_back(raw * HEAD_DIM ** (-0.5))
        allowed = window[:, None] == window[None, :]
        scores = jnp.where(allowed[None], scores, -1e+30)
        probabilities = low(jax.nn.softmax(scores, axis=-1))
        mixed = jnp.einsum('htu,uhd->thd', probabilities, values_in.reshape(TOK_IMG, group_heads, HEAD_DIM), precision=HIGHEST)
        neighbours_v = jnp.take(values_in, places, axis=0)
        lepe_term = lax.optimization_barrier(jnp.sum(w_lepe[:, None, low_edge:low_edge + group_width] * neighbours_v * usable[:, :, None], axis=0))
        outputs.append(mixed.reshape(TOK_IMG, group_width) + lepe_term + b_lepe[low_edge:low_edge + group_width])
    return jnp.concatenate(outputs, axis=1)

def forward(current, params, crop_side):
    for layer_index in range(LAYERS):
        gain_one, shift_one, w_qkv, w_lepe, b_lepe, w_proj, b_proj, gain_two, shift_two, w_up, b_up, w_down, b_down = [member[layer_index] for member in params]
        normed = low(normalize(current, gain_one, shift_one))
        packed = low_back(low(jnp.einsum('itd,de->ite', normed, w_qkv, precision=HIGHEST)))
        packed = packed.reshape(IMAGES, TOK_IMG, 3, D)

        def one_image(item_pair):
            return attend_image(item_pair[0], item_pair[1], w_lepe, b_lepe)
        heads_out = lax.map(jax.checkpoint(one_image), (packed, crop_side))
        sent = low_back(low(heads_out))
        branch = low_back(jnp.einsum('itd,de->ite', sent, w_proj, precision=HIGHEST) + b_proj)
        middle = current + branch
        normed_two = low(normalize(middle, gain_two, shift_two))
        hidden = low_back(jnp.einsum('itd,df->itf', normed_two, w_up, precision=HIGHEST) + b_up)
        active = low(jax.nn.gelu(hidden, approximate=False))
        current = middle + low_back(jnp.einsum('itf,fd->itd', active, w_down, precision=HIGHEST) + b_down)
    return current

def reference(tokens, crop_side, cotangent, ln1_gain, ln1_bias, qkv_weight, lepe_weight, lepe_bias, proj_weight, proj_bias, ln2_gain, ln2_bias, fc1_weight, fc1_bias, fc2_weight, fc2_bias):
    params = tuple((member.astype(jnp.float32) for member in (ln1_gain, ln1_bias, qkv_weight, lepe_weight, lepe_bias, proj_weight, proj_bias, ln2_gain, ln2_bias, fc1_weight, fc1_bias, fc2_weight, fc2_bias)))

    def run(inputs, weights):
        return forward(inputs, weights, crop_side)
    result, pull_back = jax.vjp(run, tokens.astype(jnp.float32), params)
    input_grad, gradients = pull_back(cotangent.astype(jnp.float32))
    factor = 1.0 / math.sqrt(TOKENS)
    return (result.astype(jnp.bfloat16), input_grad, gradients[0] * factor, gradients[1] * factor, gradients[2] * factor, gradients[3] * factor, gradients[4] * factor, gradients[5] * factor, gradients[6] * factor, gradients[7] * factor, gradients[8] * factor, gradients[9] * factor, gradients[10] * factor, gradients[11] * factor, gradients[12] * factor)
```

```python
from functools import partial
import math

import jax
import jax.numpy as jnp
import numpy as np
from jax import lax
from jax.experimental import pallas as pl
from jax.experimental.pallas import tpu as pltpu
from jax.sharding import PartitionSpec as P

HEADS_GROUP = 4
HEAD_DIM = 32
SW = 7
BIG = 14
SMALL = 6
BIG_CROPS = 2
SMALL_CROPS = 6
GROUP = 128
EPSILON = 1e-05

BIG_ROWS = BIG * 16
WIN = SW * 16
SMALL_ROWS = SMALL * 8
SMALL_BASE = BIG_CROPS * BIG_ROWS
ROWS = SMALL_BASE + SMALL_CROPS * SMALL_ROWS
CHUNK = ROWS // 2

SCALE = HEAD_DIM**-0.5
LOG2E = math.log2(math.e)
NEG = -1e30

bf16 = jnp.bfloat16
f32 = jnp.float32

NN = (((1,), (0,)), ((), ()))
NT = (((1,), (1,)), ((), ()))
TN = (((0,), (0,)), ((), ()))


def mm(a, b, dims=NN):
    return lax.dot_general(a, b, dims, preferred_element_type=f32)


def iota(shape, dim):
    return lax.broadcasted_iota(jnp.int32, shape, dim)


def to_vertical(x):
    x4 = x.reshape(BIG, 2, 8, x.shape[1])
    return jnp.concatenate([x4[:, 0].reshape(WIN, -1), x4[:, 1].reshape(WIN, -1)], axis=0)


def from_vertical(y):
    y4 = y.reshape(2, BIG, 8, y.shape[1])
    return jnp.stack([y4[0], y4[1]], axis=1).reshape(BIG_ROWS, -1)


def real_big():
    sub = iota((BIG_ROWS, GROUP), 0) % 16
    return ((sub != 0) & (sub != 15)).astype(f32)


def real_small(rows):
    return ((iota((rows, GROUP), 0) % 8) < SMALL).astype(f32)


def partial_rows(x):
    return jnp.sum(x.reshape(x.shape[0] // 8, 8, x.shape[1]), axis=0)


def head_mask(h):
    lane = iota((1, GROUP), 1)
    return ((lane >= h * HEAD_DIM) & (lane < (h + 1) * HEAD_DIM)).astype(f32)


def block_heads(x, keys):
    rows = x.shape[0]
    parts = []
    for h in range(HEADS_GROUP):
        part = x * head_mask(h).astype(x.dtype)
        parts.append(part)
        if keys > rows:
            parts.append(jnp.zeros((keys - rows, GROUP), x.dtype))
    return jnp.concatenate(parts, axis=0)


def ones_heads(keys):
    row_head = iota((HEADS_GROUP * keys, GROUP), 0) // keys
    lane_head = iota((HEADS_GROUP * keys, GROUP), 1) // HEAD_DIM
    return (row_head == lane_head).astype(f32).astype(bf16)


def sum_heads(x, keys, rows):
    total = None
    for h in range(HEADS_GROUP):
        part = x[h * keys : h * keys + rows] * head_mask(h)
        total = part if total is None else total + part
    return total


def kernel(
    crop_side,
    tokens,
    cotangent,
    ln1_gain,
    ln1_bias,
    qkv_w,
    lepe_w,
    lepe_b,
    proj_w,
    proj_b,
    ln2_gain,
    ln2_bias,
    fc1_w,
    fc1_b,
    fc2_w,
    fc2_b,
    out,
    input_grad,
    g_gain1,
    g_bias1,
    g_qkv,
    g_lepe_w,
    g_lepe_b,
    g_proj,
    g_proj_b,
    g_gain2,
    g_bias2,
    g_fc1,
    g_fc1_b,
    g_fc2,
    g_fc2_b,
    starts,
    stage,
    x_s,
    mid_s,
    e_s,
    n1_s,
    r1_s,
    a_s,
    q_s,
    k_s,
    v_s,
    eb_s,
    es_s,
    oat_s,
    rdn_s,
    o_s,
    n2_s,
    r2_s,
    m_s,
    g_s,
    gp_s,
    df_s,
    do_s,
    dqkv_s,
    lepb,
    leps,
    onesb,
    oness,
    vec,
    acc_gain1,
    acc_bias1,
    acc_lepe,
    acc_lepe_b,
    acc_proj_b,
    acc_gain2,
    acc_bias2,
    acc_fc1_b,
    acc_fc2_b,
):
    image = pl.program_id(0)
    images = pl.num_programs(0)
    layers = qkv_w.shape[0]
    dim = tokens.shape[2]
    tok = tokens.shape[1]
    crops = crop_side.shape[1]
    ff = fc1_w.shape[2]
    halves = dim // GROUP

    big_accs = (g_qkv, g_proj, g_fc1, g_fc2)
    small_accs = (
        acc_gain1,
        acc_bias1,
        acc_lepe,
        acc_lepe_b,
        acc_proj_b,
        acc_gain2,
        acc_bias2,
        acc_fc1_b,
        acc_fc2_b,
    )

    @pl.when(image == 0)
    def _():
        for ref in big_accs + small_accs:
            ref[...] = jnp.zeros(ref.shape, f32)
        lepb[...] = jnp.zeros(lepb.shape, f32)
        leps[...] = jnp.zeros(leps.shape, f32)
        stage[...] = jnp.zeros(stage.shape, f32)
        onesb[...] = ones_heads(GROUP)
        oness[...] = ones_heads(64)
        for l in range(layers):
            for i, ref in enumerate(
                (ln1_gain, ln1_bias, lepe_b, proj_b, ln2_gain, ln2_bias, fc1_b, fc2_b)
            ):
                vec[l, i : i + 1, : ref.shape[1]] = ref[l : l + 1, :]

    def place(j, carry):
        start, n_big, n_small = carry
        side = crop_side[image, j]
        is_big = side == BIG
        slot = jnp.where(is_big, n_big, BIG_CROPS + n_small)
        starts[slot] = start
        big_add = is_big.astype(jnp.int32)
        return (start + side * side, n_big + big_add, n_small + 1 - big_add)

    zero = jnp.int32(0)
    lax.fori_loop(0, crops, place, (zero, zero, zero))

    keep_lo = (iota((8, GROUP), 0) != 0).astype(f32)
    keep_hi = (iota((8, GROUP), 0) != 7).astype(f32)
    keep_small = (iota((8, GROUP), 0) < SMALL).astype(f32)

    def ingest(source, target):
        for half in range(halves):
            stage[half, 8 : 8 + tok, :] = source[0, :, half * GROUP : (half + 1) * GROUP].astype(f32)
        for c in range(BIG_CROPS):
            start = starts[c] + 7
            for r in range(BIG):
                for half in range(halves):
                    lanes = slice(half * GROUP, (half + 1) * GROUP)
                    base = c * BIG_ROWS + r * 16
                    lo = stage[half, pl.ds(start + r * BIG, 8), :]
                    hi = stage[half, pl.ds(start + r * BIG + 8, 8), :]
                    target[base : base + 8, lanes] = lo * keep_lo
                    target[base + 8 : base + 16, lanes] = hi * keep_hi
        for c in range(SMALL_CROPS):
            start = starts[BIG_CROPS + c] + 8
            for r in range(SMALL):
                for half in range(halves):
                    lanes = slice(half * GROUP, (half + 1) * GROUP)
                    base = SMALL_BASE + c * SMALL_ROWS + r * 8
                    lo = stage[half, pl.ds(start + r * SMALL, 8), :]
                    target[base : base + 8, lanes] = lo * keep_small

    def put(half, at, value, keep):
        old = stage[half, pl.ds(at, 8), :]
        stage[half, pl.ds(at, 8), :] = jnp.where(keep > 0, value, old)

    def emit(source, target):
        for c in range(BIG_CROPS):
            start = starts[c] + 7
            for r in range(BIG):
                for half in range(halves):
                    lanes = slice(half * GROUP, (half + 1) * GROUP)
                    base = c * BIG_ROWS + r * 16
                    put(half, start + r * BIG, source[base : base + 8, lanes], keep_lo)
                    put(half, start + r * BIG + 8, source[base + 8 : base + 16, lanes], keep_hi)
        for c in range(SMALL_CROPS):
            start = starts[BIG_CROPS + c] + 8
            for r in range(SMALL):
                for half in range(halves):
                    lanes = slice(half * GROUP, (half + 1) * GROUP)
                    base = SMALL_BASE + c * SMALL_ROWS + r * 8
                    put(half, start + r * SMALL, source[base : base + 8, lanes], keep_small)
        for half in range(halves):
            target[0, :, half * GROUP : (half + 1) * GROUP] = stage[half, 8 : 8 + tok, :].astype(
                target.dtype
            )

    def norm_stats(x):
        center = x - jnp.mean(x, axis=1, keepdims=True)
        r = lax.rsqrt(jnp.mean(center * center, axis=1, keepdims=True) + EPSILON)
        return center * r, r

    def project(l, base, rows, big):
        rows_at = pl.ds(base, rows)
        n, r = norm_stats(x_s[rows_at, :])
        n1_s[l, rows_at, :] = n
        r1_s[l, rows_at, :] = jnp.broadcast_to(r, (rows, GROUP))
        a = (n * vec[l, 0:1, :dim] + vec[l, 1:2, :dim]).astype(bf16)
        a_s[l, rows_at, :] = a
        qkv = mm(a, qkv_w[l])
        real = real_big() if big else real_small(rows)
        for grp in range(2):
            cols = [slice(s * dim + grp * GROUP, s * dim + (grp + 1) * GROUP) for s in range(3)]
            q = qkv[:, cols[0]] * (SCALE * LOG2E)
            k = qkv[:, cols[1]]
            v = qkv[:, cols[2]] * real
            if big and grp == 1:
                q, k, v = to_vertical(q), to_vertical(k), to_vertical(v)
            lanes = slice(grp * GROUP, (grp + 1) * GROUP)
            q_s[l, rows_at, lanes] = q.astype(bf16)
            k_s[l, rows_at, lanes] = k.astype(bf16)
            v_s[l, rows_at, lanes] = v.astype(bf16)

    def pad_row(grp, w):
        u = iota((1, HEADS_GROUP * GROUP), 1) % GROUP
        if grp == 0:
            bad = (u % 16 == 0) | (u % 16 == 15)
        elif w == 0:
            bad = u % 8 == 0
        else:
            bad = u % 8 == 7
        return jnp.where(bad | (u >= WIN), NEG, 0.0).astype(f32)

    def pad_row_small():
        u = iota((1, HEADS_GROUP * 64), 1) % 64
        return jnp.where((u % 8 >= SMALL) | (u >= SMALL_ROWS), NEG, 0.0).astype(f32)

    def shifted(buf, idx, margin, stride, rows):
        return [buf[idx, pl.ds(margin - stride + b, rows + 2 * stride), :] for b in (-1, 0, 1)]

    def conv(views, stride, rows, weights, flip):
        total = None
        for a in range(3):
            for b in range(3):
                k = 3 * a + b
                wk = weights[8 - k : 9 - k] if flip else weights[k : k + 1]
                term = views[b][a * stride : a * stride + rows] * wk
                total = term if total is None else total + term
        return total

    def windows_big(c):
        for grp in range(2):
            for w in range(2):
                yield grp, w, c * BIG_ROWS + w * WIN

    def attend_big(l, c):
        items = list(windows_big(c))
        scores = []
        for grp, w, base in items:
            lanes = slice(grp * GROUP, (grp + 1) * GROUP)
            q = q_s[l, pl.ds(base, WIN), lanes]
            kb = block_heads(k_s[l, pl.ds(base, WIN), lanes], GROUP)
            scores.append(mm(q, kb, NT) + pad_row(grp, w))
        for i, (grp, w, base) in enumerate(items):
            parts = []
            for h in range(HEADS_GROUP):
                s = scores[i][:, h * GROUP : (h + 1) * GROUP]
                parts.append(jnp.exp2(s - jnp.max(s, axis=1, keepdims=True)).astype(bf16))
            eb_s[l, 4 * c + 2 * grp + w] = jnp.concatenate(parts, axis=1)
        outs = []
        for i, (grp, w, base) in enumerate(items):
            lanes = slice(grp * GROUP, (grp + 1) * GROUP)
            v = v_s[l, pl.ds(base, WIN), lanes]
            vo = jnp.concatenate([block_heads(v, GROUP), onesb[...]], axis=1)
            both = mm(eb_s[l, 4 * c + 2 * grp + w], vo)
            rden = 1.0 / both[:, GROUP:]
            oat = both[:, :GROUP] * rden
            rdn_s[l, pl.ds(base, WIN), lanes] = rden
            oat_s[l, pl.ds(base, WIN), lanes] = oat
            stride = 16 if grp == 0 else 8
            lepb[i, pl.ds(24, WIN), :] = v.astype(f32)
            views = shifted(lepb, i, 24, stride, WIN)
            near = conv(views, stride, WIN, lepe_w[l, :, lanes], False)
            outs.append(oat + near + vec[l, 2:3, lanes])
        rows_at = pl.ds(c * BIG_ROWS, BIG_ROWS)
        o_s[l, rows_at, :GROUP] = jnp.concatenate(outs[:2], axis=0).astype(bf16)
        o_s[l, rows_at, GROUP:] = from_vertical(jnp.concatenate(outs[2:], axis=0)).astype(bf16)

    def attend_small(l, c0, count):
        items = [
            (grp, c0 + c, SMALL_BASE + (c0 + c) * SMALL_ROWS, 2 * c + grp)
            for c in range(count)
            for grp in range(2)
        ]
        low = iota((SMALL_ROWS, GROUP), 1) < 64
        scores = []
        for grp, c, base, i in items:
            lanes = slice(grp * GROUP, (grp + 1) * GROUP)
            q = q_s[l, pl.ds(base, SMALL_ROWS), lanes]
            kb = block_heads(k_s[l, pl.ds(base, SMALL_ROWS), lanes], 64)
            scores.append(mm(q, kb, NT) + pad_row_small())
        for j, (grp, c, base, i) in enumerate(items):
            parts = []
            for t in range(2):
                s = scores[j][:, t * GROUP : (t + 1) * GROUP]
                top_lo = jnp.max(jnp.where(low, s, 2 * NEG), axis=1, keepdims=True)
                top_hi = jnp.max(jnp.where(low, 2 * NEG, s), axis=1, keepdims=True)
                parts.append(jnp.exp2(s - jnp.where(low, top_lo, top_hi)).astype(bf16))
            es_s[l, 2 * c + grp] = jnp.concatenate(parts, axis=1)
        for grp, c, base, i in items:
            lanes = slice(grp * GROUP, (grp + 1) * GROUP)
            v = v_s[l, pl.ds(base, SMALL_ROWS), lanes]
            vo = jnp.concatenate([block_heads(v, 64), oness[...]], axis=1)
            both = mm(es_s[l, 2 * c + grp], vo)
            rden = 1.0 / both[:, GROUP:]
            oat = both[:, :GROUP] * rden
            rdn_s[l, pl.ds(base, SMALL_ROWS), lanes] = rden
            oat_s[l, pl.ds(base, SMALL_ROWS), lanes] = oat
            leps[i, pl.ds(16, SMALL_ROWS), :] = v.astype(f32)
            views = shifted(leps, i, 16, 8, SMALL_ROWS)
            near = conv(views, 8, SMALL_ROWS, lepe_w[l, :, lanes], False)
            o_s[l, pl.ds(base, SMALL_ROWS), lanes] = (oat + near + vec[l, 2:3, lanes]).astype(
                bf16
            )

    def feed(l, base):
        rows_at = pl.ds(base, CHUNK)
        mid = x_s[rows_at, :] + mm(o_s[l, rows_at, :], proj_w[l]) + vec[l, 3:4, :dim]
        n, r = norm_stats(mid)
        n2_s[l, rows_at, :] = n
        r2_s[l, rows_at, :] = jnp.broadcast_to(r, (CHUNK, GROUP))
        m = (n * vec[l, 4:5, :dim] + vec[l, 5:6, :dim]).astype(bf16)
        m_s[l, rows_at, :] = m
        total = mid + vec[l, 7:8, :dim]
        step = 256
        for j in range(ff // step):
            cols = slice(j * step, (j + 1) * step)
            f = mm(m, fc1_w[l, :, cols]) + vec[l, 6:7, cols]
            phi = 0.5 * lax.erf(f * np.float32(math.sqrt(0.5))) + 0.5
            dens = jnp.exp2(f * f * np.float32(-0.5 * LOG2E)) * np.float32(
                1.0 / math.sqrt(2.0 * math.pi)
            )
            g = (f * phi).astype(bf16)
            g_s[l, rows_at, cols] = g
            gp_s[l, rows_at, cols] = (phi + f * dens).astype(bf16)
            total = total + mm(g, fc2_w[l, cols, :])
        x_s[rows_at, :] = total

    def norm_back(dm, n, r, gain):
        dn = dm * gain
        mean_one = jnp.mean(dn, axis=1, keepdims=True)
        mean_two = jnp.mean(dn * n, axis=1, keepdims=True)
        rb = jnp.concatenate([r] * halves, axis=1)
        return rb * (dn - mean_one - n * mean_two)

    def feed_back(l, base):
        rows_at = pl.ds(base, CHUNK)
        e = e_s[rows_at, :]
        dz = e.astype(bf16)
        acc_fc2_b[l] += partial_rows(dz.astype(f32))
        dm = None
        step = 256
        for j in range(ff // step):
            cols = slice(j * step, (j + 1) * step)
            dg = mm(dz, fc2_w[l, cols, :], NT)
            df = (dg * gp_s[l, rows_at, cols].astype(f32)).astype(bf16)
            df_s[rows_at, cols] = df
            acc_fc1_b[l, :, cols] += partial_rows(df.astype(f32))
            part = mm(df, fc1_w[l, :, cols], NT)
            dm = part if dm is None else dm + part
        n = n2_s[l, rows_at, :]
        acc_gain2[l] += partial_rows(dm * n)
        acc_bias2[l] += partial_rows(dm)
        dmid = e + norm_back(dm, n, r2_s[l, rows_at, :], vec[l, 4:5, :dim])
        mid_s[rows_at, :] = dmid
        dy = dmid.astype(bf16)
        acc_proj_b[l] += partial_rows(dy.astype(f32))
        do_s[rows_at, :] = mm(dy, proj_w[l], NT).astype(bf16).astype(f32)

    def lepe_back(l, buf, idx, margin, stride, rows, lanes, v):
        views = [buf[idx, pl.ds(margin - stride + b, rows + 2 * stride), :] for b in (-1, 0, 1)]
        vf = v.astype(f32)
        for k in range(9):
            a, b = divmod(8 - k, 3)
            acc_lepe[l, k, :, lanes] += partial_rows(views[b][a * stride : a * stride + rows] * vf)
        acc_lepe_b[l, :, lanes] += partial_rows(views[1][stride : stride + rows])
        return conv(views, stride, rows, lepe_w[l, :, lanes], True)

    def attend_back(l, group_items, rows, keys, buf, margin, strides, e_ref, ones, unit):
        grads = []
        kbs = []
        ds_all = []
        dop_all = []
        for grp, base, e_at, lep_at, do in group_items:
            lanes = slice(grp * GROUP, (grp + 1) * GROUP)
            rows_at = pl.ds(base, rows)
            buf[lep_at, pl.ds(margin, rows), :] = do
            dop = do * rdn_s[l, rows_at, lanes]
            tail = -(dop * oat_s[l, rows_at, lanes])
            dop_all.append(dop.astype(bf16))
            left = jnp.concatenate([dop.astype(bf16), tail.astype(bf16)], axis=1)
            vo = jnp.concatenate([block_heads(v_s[l, rows_at, lanes], keys), ones[...]], axis=1)
            x = mm(left, vo, NT)
            ds_all.append((e_ref[l, e_at].astype(f32) * x).astype(bf16))
        for i, (grp, base, e_at, lep_at, do) in enumerate(group_items):
            lanes = slice(grp * GROUP, (grp + 1) * GROUP)
            kb = block_heads(k_s[l, pl.ds(base, rows), lanes], keys)
            grads.append([mm(ds_all[i], kb) * SCALE])
        zero_block = jnp.zeros((rows, GROUP), bf16)
        for i in range(0, len(group_items), 2):
            pair = group_items[i : i + 2]

            def spread(first, second):
                return jnp.concatenate(
                    [
                        jnp.concatenate([first, zero_block], axis=1),
                        jnp.concatenate([zero_block, second], axis=1),
                    ],
                    axis=0,
                )

            qs = [q_s[l, pl.ds(it[1], rows), it[0] * GROUP : (it[0] + 1) * GROUP] for it in pair]
            dk = mm(jnp.concatenate(ds_all[i : i + 2], axis=0), spread(*qs), TN)
            es = jnp.concatenate([e_ref[l, it[2]] for it in pair], axis=0)
            dv = mm(es, spread(*dop_all[i : i + 2]), TN)
            for j, (grp, base, e_at, lep_at, do) in enumerate(pair):
                lanes = slice(grp * GROUP, (grp + 1) * GROUP)
                cols = slice(j * GROUP, (j + 1) * GROUP)
                near = lepe_back(
                    l, buf, lep_at, margin, strides[grp], rows, lanes, v_s[l, pl.ds(base, rows), lanes]
                )
                grads[i + j].append(sum_heads(dk[:, cols], keys, rows) * (1.0 / LOG2E))
                grads[i + j].append(sum_heads(dv[:, cols], keys, rows) + near)
        return grads

    def attend_back_big(l, c):
        rows_at = pl.ds(c * BIG_ROWS, BIG_ROWS)
        do_h = do_s[rows_at, :GROUP]
        do_v = to_vertical(do_s[rows_at, GROUP:])
        items = []
        for i, (grp, w, base) in enumerate(windows_big(c)):
            do = (do_h if grp == 0 else do_v)[w * WIN : (w + 1) * WIN]
            items.append((grp, base, 4 * c + 2 * grp + w, i, do))
        grads = attend_back(l, items, WIN, GROUP, lepb, 24, (16, 8), eb_s, onesb, None)
        real = real_big()
        for s in range(3):
            left = jnp.concatenate([grads[0][s], grads[1][s]], axis=0)
            right = from_vertical(jnp.concatenate([grads[2][s], grads[3][s]], axis=0))
            if s == 2:
                left, right = left * real, right * real
            dqkv_s[rows_at, s * dim : s * dim + GROUP] = left.astype(bf16)
            dqkv_s[rows_at, s * dim + GROUP : (s + 1) * dim] = right.astype(bf16)

    def attend_back_small(l, c0, count):
        items = []
        for grp in range(2):
            for c in range(count):
                base = SMALL_BASE + (c0 + c) * SMALL_ROWS
                do = do_s[pl.ds(base, SMALL_ROWS), grp * GROUP : (grp + 1) * GROUP]
                items.append((grp, base, 2 * (c0 + c) + grp, 2 * c + grp, do))
        grads = attend_back(l, items, SMALL_ROWS, 64, leps, 16, (8, 8), es_s, oness, None)
        real = real_small(SMALL_ROWS)
        for (grp, base, e_at, lep_at, do), grad in zip(items, grads):
            for s in range(3):
                value = grad[s] * real if s == 2 else grad[s]
                at = s * dim + grp * GROUP
                dqkv_s[pl.ds(base, SMALL_ROWS), at : at + GROUP] = value.astype(bf16)

    def project_back(l, base):
        rows_at = pl.ds(base, CHUNK)
        da = mm(dqkv_s[rows_at, :], qkv_w[l], NT)
        n = n1_s[l, rows_at, :]
        acc_gain1[l] += partial_rows(da * n)
        acc_bias1[l] += partial_rows(da)
        e_s[rows_at, :] = mid_s[rows_at, :] + norm_back(
            da, n, r1_s[l, rows_at, :], vec[l, 0:1, :dim]
        )

    def loop(count, body):
        def step(i, carry):
            body(i)
            return carry

        lax.fori_loop(0, count, step, 0)

    ingest(tokens, x_s)

    def forward_layer(l):
        loop(BIG_CROPS, lambda c: project(l, pl.multiple_of(c * BIG_ROWS, 16), BIG_ROWS, True))
        project(l, SMALL_BASE, ROWS - SMALL_BASE, False)
        loop(BIG_CROPS, lambda c: attend_big(l, c))
        loop(SMALL_CROPS // 2, lambda c: attend_small(l, 2 * c, 2))
        loop(2, lambda c: feed(l, pl.multiple_of(c * CHUNK, 16)))

    loop(layers, forward_layer)
    emit(x_s, out)
    ingest(cotangent, e_s)

    def backward_layer(step):
        l = layers - 1 - step
        loop(2, lambda c: feed_back(l, pl.multiple_of(c * CHUNK, 16)))
        dz = e_s[...].astype(bf16)
        g_fc2[l] += mm(g_s[l], dz, TN)
        g_fc1[l] += mm(m_s[l], df_s[...], TN)
        g_proj[l] += mm(o_s[l], mid_s[...].astype(bf16), TN)
        loop(BIG_CROPS, lambda c: attend_back_big(l, c))
        loop(SMALL_CROPS // 2, lambda c: attend_back_small(l, 2 * c, 2))
        g_qkv[l] += mm(a_s[l], dqkv_s[...], TN)
        loop(2, lambda c: project_back(l, pl.multiple_of(c * CHUNK, 16)))

    loop(layers, backward_layer)
    emit(e_s, input_grad)

    @pl.when(image == images - 1)
    def _():
        for acc, target in (
            (acc_gain1, g_gain1),
            (acc_bias1, g_bias1),
            (acc_lepe_b, g_lepe_b),
            (acc_proj_b, g_proj_b),
            (acc_gain2, g_gain2),
            (acc_bias2, g_bias2),
            (acc_fc1_b, g_fc1_b),
            (acc_fc2_b, g_fc2_b),
        ):
            target[...] = jnp.sum(acc[...], axis=1)
        g_lepe_w[...] = jnp.sum(acc_lepe[...], axis=2)


def local(
    tokens,
    crop_side,
    cotangent,
    ln1_gain,
    ln1_bias,
    qkv_weight,
    lepe_weight,
    lepe_bias,
    proj_weight,
    proj_bias,
    ln2_gain,
    ln2_bias,
    fc1_weight,
    fc1_bias,
    fc2_weight,
    fc2_bias,
):
    images, tok, dim = tokens.shape
    layers = qkv_weight.shape[0]
    ff = fc1_weight.shape[2]
    weights = (
        ln1_gain,
        ln1_bias,
        qkv_weight,
        lepe_weight,
        lepe_bias,
        proj_weight,
        proj_bias,
        ln2_gain,
        ln2_bias,
        fc1_weight,
        fc1_bias,
        fc2_weight,
        fc2_bias,
    )
    block = pl.BlockSpec((1, tok, dim), lambda i: (i, 0, 0))
    whole = pl.BlockSpec(memory_space=pltpu.VMEM)
    results = pl.pallas_call(
        kernel,
        grid=(images,),
        out_shape=[
            jax.ShapeDtypeStruct(tokens.shape, bf16),
            jax.ShapeDtypeStruct(tokens.shape, f32),
        ]
        + [jax.ShapeDtypeStruct(w.shape, f32) for w in weights],
        in_specs=[pl.BlockSpec(memory_space=pltpu.SMEM), block, block] + [whole] * len(weights),
        out_specs=[block, block] + [whole] * len(weights),
        scratch_shapes=[
            pltpu.SMEM((BIG_CROPS + SMALL_CROPS,), jnp.int32),
            pltpu.VMEM((dim // GROUP, tok + 16, GROUP), f32),
            pltpu.VMEM((ROWS, dim), f32),
            pltpu.VMEM((ROWS, dim), f32),
            pltpu.VMEM((ROWS, dim), f32),
            pltpu.VMEM((layers, ROWS, dim), f32),
            pltpu.VMEM((layers, ROWS, GROUP), f32),
            pltpu.VMEM((layers, ROWS, dim), bf16),
            pltpu.VMEM((layers, ROWS, dim), bf16),
            pltpu.VMEM((layers, ROWS, dim), bf16),
            pltpu.VMEM((layers, ROWS, dim), bf16),
            pltpu.VMEM((layers, 4 * BIG_CROPS, WIN, 4 * GROUP), bf16),
            pltpu.VMEM((layers, 2 * SMALL_CROPS, SMALL_ROWS, 2 * GROUP), bf16),
            pltpu.VMEM((layers, ROWS, dim), f32),
            pltpu.VMEM((layers, ROWS, dim), f32),
            pltpu.VMEM((layers, ROWS, dim), bf16),
            pltpu.VMEM((layers, ROWS, dim), f32),
            pltpu.VMEM((layers, ROWS, GROUP), f32),
            pltpu.VMEM((layers, ROWS, dim), bf16),
            pltpu.VMEM((layers, ROWS, ff), bf16),
            pltpu.VMEM((layers, ROWS, ff), bf16),
            pltpu.VMEM((ROWS, ff), bf16),
            pltpu.VMEM((ROWS, dim), f32),
            pltpu.VMEM((ROWS, 3 * dim), bf16),
            pltpu.VMEM((4, WIN + 48, GROUP), f32),
            pltpu.VMEM((4, SMALL_ROWS + 32, GROUP), f32),
            pltpu.VMEM((4 * GROUP, GROUP), bf16),
            pltpu.VMEM((4 * 64, GROUP), bf16),
            pltpu.VMEM((layers, 8, ff), f32),
            pltpu.VMEM((layers, 8, dim), f32),
            pltpu.VMEM((layers, 8, dim), f32),
            pltpu.VMEM((layers, 9, 8, dim), f32),
            pltpu.VMEM((layers, 8, dim), f32),
            pltpu.VMEM((layers, 8, dim), f32),
            pltpu.VMEM((layers, 8, dim), f32),
            pltpu.VMEM((layers, 8, dim), f32),
            pltpu.VMEM((layers, 8, ff), f32),
            pltpu.VMEM((layers, 8, dim), f32),
        ],
        compiler_params=pltpu.CompilerParams(
            dimension_semantics=("arbitrary",), vmem_limit_bytes=62 * 1024 * 1024
        ),
    )(crop_side, tokens, cotangent, *weights)
    grads = lax.psum(tuple(results[2:]), ("dp", "head"))
    factor = 1.0 / math.sqrt(lax.axis_size("dp") * lax.axis_size("head") * images * tok)
    return (results[0], results[1]) + tuple(g * factor for g in grads)


def solution(mesh):
    sharded = P(("dp", "head"), None, None)
    return jax.shard_map(
        local,
        mesh=mesh,
        in_specs=(sharded, P(("dp", "head"), None), sharded) + (P(),) * 13,
        out_specs=(sharded, sharded) + (P(),) * 13,
        check_vma=False,
    )
```

```python
from functools import partial
import math

import jax
import jax.numpy as jnp
import numpy as np
from jax import lax
from jax.experimental import pallas as pl
from jax.experimental.pallas import tpu as pltpu
from jax.sharding import PartitionSpec as P

HEADS_GROUP = 4
HEAD_DIM = 32
SW = 7
BIG = 14
SMALL = 6
BIG_CROPS = 2
SMALL_CROPS = 6
GROUP = 128
EPSILON = 1e-05

BIG_ROWS = BIG * 16
WIN = SW * 16
SMALL_ROWS = SMALL * 8
SMALL_BASE = BIG_CROPS * BIG_ROWS
ROWS = SMALL_BASE + SMALL_CROPS * SMALL_ROWS
CHUNK = ROWS // 2

SCALE = HEAD_DIM**-0.5
LOG2E = math.log2(math.e)
NEG = -1e30

bf16 = jnp.bfloat16
f32 = jnp.float32

NN = (((1,), (0,)), ((), ()))
NT = (((1,), (1,)), ((), ()))
TN = (((0,), (0,)), ((), ()))


def mm(a, b, dims=NN):
    return lax.dot_general(a, b, dims, preferred_element_type=f32)


def iota(shape, dim):
    return lax.broadcasted_iota(jnp.int32, shape, dim)


def to_vertical(x):
    x4 = x.reshape(BIG, 2, 8, x.shape[1])
    return jnp.concatenate([x4[:, 0].reshape(WIN, -1), x4[:, 1].reshape(WIN, -1)], axis=0)


def from_vertical(y):
    y4 = y.reshape(2, BIG, 8, y.shape[1])
    return jnp.stack([y4[0], y4[1]], axis=1).reshape(BIG_ROWS, -1)


def real_big():
    sub = iota((BIG_ROWS, GROUP), 0) % 16
    return ((sub != 0) & (sub != 15)).astype(f32)


def real_small(rows):
    return ((iota((rows, GROUP), 0) % 8) < SMALL).astype(f32)


def partial_rows(x):
    return jnp.sum(x.reshape(x.shape[0] // 8, 8, x.shape[1]), axis=0)


def head_mask(h):
    lane = iota((1, GROUP), 1)
    return ((lane >= h * HEAD_DIM) & (lane < (h + 1) * HEAD_DIM)).astype(f32)


def block_heads(x, keys):
    rows = x.shape[0]
    parts = []
    for h in range(HEADS_GROUP):
        part = x * head_mask(h).astype(x.dtype)
        parts.append(part)
        if keys > rows:
            parts.append(jnp.zeros((keys - rows, GROUP), x.dtype))
    return jnp.concatenate(parts, axis=0)


def ones_heads(keys):
    row_head = iota((HEADS_GROUP * keys, GROUP), 0) // keys
    lane_head = iota((HEADS_GROUP * keys, GROUP), 1) // HEAD_DIM
    return (row_head == lane_head).astype(f32).astype(bf16)


def sum_heads(x, keys, rows):
    total = None
    for h in range(HEADS_GROUP):
        part = x[h * keys : h * keys + rows] * head_mask(h)
        total = part if total is None else total + part
    return total


def kernel(
    crop_side,
    tokens,
    cotangent,
    ln1_gain,
    ln1_bias,
    qkv_w,
    lepe_w,
    lepe_b,
    proj_w,
    proj_b,
    ln2_gain,
    ln2_bias,
    fc1_w,
    fc1_b,
    fc2_w,
    fc2_b,
    out,
    input_grad,
    packed,
    g_qkv,
    g_proj,
    g_fc1,
    g_fc2,
    starts,
    stage,
    x_s,
    mid_s,
    e_s,
    n1_s,
    r1_s,
    a_s,
    q_s,
    k_s,
    v_s,
    eb_s,
    es_s,
    oat_s,
    rdn_s,
    o_s,
    n2_s,
    r2_s,
    m_s,
    g_s,
    gp_s,
    df_s,
    do_s,
    dqkv_s,
    lepb,
    leps,
    onesb,
    oness,
    vec,
    acc_gain1,
    acc_bias1,
    acc_lepe,
    acc_lepe_b,
    acc_proj_b,
    acc_gain2,
    acc_bias2,
    acc_fc1_b,
    acc_fc2_b,
):
    image = pl.program_id(0)
    images = pl.num_programs(0)
    layers = qkv_w.shape[0]
    dim = tokens.shape[2]
    tok = tokens.shape[1]
    crops = crop_side.shape[1]
    ff = fc1_w.shape[2]
    halves = dim // GROUP

    big_accs = (g_qkv, g_proj, g_fc1, g_fc2)
    small_accs = (
        acc_gain1,
        acc_bias1,
        acc_lepe,
        acc_lepe_b,
        acc_proj_b,
        acc_gain2,
        acc_bias2,
        acc_fc1_b,
        acc_fc2_b,
    )

    @pl.when(image == 0)
    def _():
        for ref in big_accs + small_accs:
            ref[...] = jnp.zeros(ref.shape, f32)
        lepb[...] = jnp.zeros(lepb.shape, f32)
        leps[...] = jnp.zeros(leps.shape, f32)
        stage[...] = jnp.zeros(stage.shape, f32)
        onesb[...] = ones_heads(GROUP)
        oness[...] = ones_heads(64)
        for l in range(layers):
            for i, ref in enumerate(
                (ln1_gain, ln1_bias, lepe_b, proj_b, ln2_gain, ln2_bias, fc1_b, fc2_b)
            ):
                vec[l, i : i + 1, : ref.shape[1]] = ref[l : l + 1, :]

    def place(j, carry):
        start, n_big, n_small = carry
        side = crop_side[image, j]
        is_big = side == BIG
        slot = jnp.where(is_big, n_big, BIG_CROPS + n_small)
        starts[slot] = start
        big_add = is_big.astype(jnp.int32)
        return (start + side * side, n_big + big_add, n_small + 1 - big_add)

    zero = jnp.int32(0)
    lax.fori_loop(0, crops, place, (zero, zero, zero))

    keep_lo = (iota((8, GROUP), 0) != 0).astype(f32)
    keep_hi = (iota((8, GROUP), 0) != 7).astype(f32)
    keep_small = (iota((8, GROUP), 0) < SMALL).astype(f32)

    def ingest(source, target):
        for half in range(halves):
            stage[half, 8 : 8 + tok, :] = source[0, :, half * GROUP : (half + 1) * GROUP].astype(f32)
        for c in range(BIG_CROPS):
            start = starts[c] + 7
            for r in range(BIG):
                for half in range(halves):
                    lanes = slice(half * GROUP, (half + 1) * GROUP)
                    base = c * BIG_ROWS + r * 16
                    lo = stage[half, pl.ds(start + r * BIG, 8), :]
                    hi = stage[half, pl.ds(start + r * BIG + 8, 8), :]
                    target[base : base + 8, lanes] = lo * keep_lo
                    target[base + 8 : base + 16, lanes] = hi * keep_hi
        for c in range(SMALL_CROPS):
            start = starts[BIG_CROPS + c] + 8
            for r in range(SMALL):
                for half in range(halves):
                    lanes = slice(half * GROUP, (half + 1) * GROUP)
                    base = SMALL_BASE + c * SMALL_ROWS + r * 8
                    lo = stage[half, pl.ds(start + r * SMALL, 8), :]
                    target[base : base + 8, lanes] = lo * keep_small

    def put(half, at, value, keep):
        old = stage[half, pl.ds(at, 8), :]
        stage[half, pl.ds(at, 8), :] = jnp.where(keep > 0, value, old)

    def emit(source, target):
        for c in range(BIG_CROPS):
            start = starts[c] + 7
            for r in range(BIG):
                for half in range(halves):
                    lanes = slice(half * GROUP, (half + 1) * GROUP)
                    base = c * BIG_ROWS + r * 16
                    put(half, start + r * BIG, source[base : base + 8, lanes], keep_lo)
                    put(half, start + r * BIG + 8, source[base + 8 : base + 16, lanes], keep_hi)
        for c in range(SMALL_CROPS):
            start = starts[BIG_CROPS + c] + 8
            for r in range(SMALL):
                for half in range(halves):
                    lanes = slice(half * GROUP, (half + 1) * GROUP)
                    base = SMALL_BASE + c * SMALL_ROWS + r * 8
                    put(half, start + r * SMALL, source[base : base + 8, lanes], keep_small)
        for half in range(halves):
            target[0, :, half * GROUP : (half + 1) * GROUP] = stage[half, 8 : 8 + tok, :].astype(
                target.dtype
            )

    def norm_stats(x):
        center = x - jnp.mean(x, axis=1, keepdims=True)
        r = lax.rsqrt(jnp.mean(center * center, axis=1, keepdims=True) + EPSILON)
        return center * r, r

    def project(l, base, rows, big):
        rows_at = pl.ds(base, rows)
        n, r = norm_stats(x_s[rows_at, :])
        n1_s[l, rows_at, :] = n
        r1_s[l, rows_at, :] = jnp.broadcast_to(r, (rows, GROUP))
        a = (n * vec[l, 0:1, :dim] + vec[l, 1:2, :dim]).astype(bf16)
        a_s[l, rows_at, :] = a
        qkv = mm(a, qkv_w[l])
        real = real_big() if big else real_small(rows)
        for grp in range(2):
            cols = [slice(s * dim + grp * GROUP, s * dim + (grp + 1) * GROUP) for s in range(3)]
            q = qkv[:, cols[0]] * (SCALE * LOG2E)
            k = qkv[:, cols[1]]
            v = qkv[:, cols[2]] * real
            if big and grp == 1:
                q, k, v = to_vertical(q), to_vertical(k), to_vertical(v)
            lanes = slice(grp * GROUP, (grp + 1) * GROUP)
            q_s[l, rows_at, lanes] = q.astype(bf16)
            k_s[l, rows_at, lanes] = k.astype(bf16)
            v_s[l, rows_at, lanes] = v.astype(bf16)

    def pad_row(grp, w):
        u = iota((1, HEADS_GROUP * GROUP), 1) % GROUP
        if grp == 0:
            bad = (u % 16 == 0) | (u % 16 == 15)
        elif w == 0:
            bad = u % 8 == 0
        else:
            bad = u % 8 == 7
        return jnp.where(bad | (u >= WIN), NEG, 0.0).astype(f32)

    def pad_row_small():
        u = iota((1, HEADS_GROUP * 64), 1) % 64
        return jnp.where((u % 8 >= SMALL) | (u >= SMALL_ROWS), NEG, 0.0).astype(f32)

    def shifted(buf, idx, margin, stride, rows):
        return [buf[idx, pl.ds(margin - stride + b, rows + 2 * stride), :] for b in (-1, 0, 1)]

    def conv(views, stride, rows, weights, flip):
        total = None
        for a in range(3):
            for b in range(3):
                k = 3 * a + b
                wk = weights[8 - k : 9 - k] if flip else weights[k : k + 1]
                term = views[b][a * stride : a * stride + rows] * wk
                total = term if total is None else total + term
        return total

    def windows_big(c):
        for grp in range(2):
            for w in range(2):
                yield grp, w, c * BIG_ROWS + w * WIN

    def attend_big(l, c):
        items = list(windows_big(c))
        scores = []
        for grp, w, base in items:
            lanes = slice(grp * GROUP, (grp + 1) * GROUP)
            q = q_s[l, pl.ds(base, WIN), lanes]
            kb = block_heads(k_s[l, pl.ds(base, WIN), lanes], GROUP)
            scores.append(mm(q, kb, NT) + pad_row(grp, w))
        for i, (grp, w, base) in enumerate(items):
            parts = []
            for h in range(HEADS_GROUP):
                s = scores[i][:, h * GROUP : (h + 1) * GROUP]
                parts.append(jnp.exp2(s - jnp.max(s, axis=1, keepdims=True)).astype(bf16))
            eb_s[l, 4 * c + 2 * grp + w] = jnp.concatenate(parts, axis=1)
        outs = []
        for i, (grp, w, base) in enumerate(items):
            lanes = slice(grp * GROUP, (grp + 1) * GROUP)
            v = v_s[l, pl.ds(base, WIN), lanes]
            vo = jnp.concatenate([block_heads(v, GROUP), onesb[...]], axis=1)
            both = mm(eb_s[l, 4 * c + 2 * grp + w], vo)
            rden = 1.0 / both[:, GROUP:]
            oat = both[:, :GROUP] * rden
            rdn_s[l, pl.ds(base, WIN), lanes] = rden
            oat_s[l, pl.ds(base, WIN), lanes] = oat
            stride = 16 if grp == 0 else 8
            lepb[i, pl.ds(24, WIN), :] = v.astype(f32)
            views = shifted(lepb, i, 24, stride, WIN)
            near = conv(views, stride, WIN, lepe_w[l, :, lanes], False)
            outs.append(oat + near + vec[l, 2:3, lanes])
        rows_at = pl.ds(c * BIG_ROWS, BIG_ROWS)
        o_s[l, rows_at, :GROUP] = jnp.concatenate(outs[:2], axis=0).astype(bf16)
        o_s[l, rows_at, GROUP:] = from_vertical(jnp.concatenate(outs[2:], axis=0)).astype(bf16)

    def attend_small(l, c0, count):
        items = [
            (grp, c0 + c, SMALL_BASE + (c0 + c) * SMALL_ROWS, 2 * c + grp)
            for c in range(count)
            for grp in range(2)
        ]
        low = iota((SMALL_ROWS, GROUP), 1) < 64
        scores = []
        for grp, c, base, i in items:
            lanes = slice(grp * GROUP, (grp + 1) * GROUP)
            q = q_s[l, pl.ds(base, SMALL_ROWS), lanes]
            kb = block_heads(k_s[l, pl.ds(base, SMALL_ROWS), lanes], 64)
            scores.append(mm(q, kb, NT) + pad_row_small())
        for j, (grp, c, base, i) in enumerate(items):
            parts = []
            for t in range(2):
                s = scores[j][:, t * GROUP : (t + 1) * GROUP]
                top_lo = jnp.max(jnp.where(low, s, 2 * NEG), axis=1, keepdims=True)
                top_hi = jnp.max(jnp.where(low, 2 * NEG, s), axis=1, keepdims=True)
                parts.append(jnp.exp2(s - jnp.where(low, top_lo, top_hi)).astype(bf16))
            es_s[l, 2 * c + grp] = jnp.concatenate(parts, axis=1)
        for grp, c, base, i in items:
            lanes = slice(grp * GROUP, (grp + 1) * GROUP)
            v = v_s[l, pl.ds(base, SMALL_ROWS), lanes]
            vo = jnp.concatenate([block_heads(v, 64), oness[...]], axis=1)
            both = mm(es_s[l, 2 * c + grp], vo)
            rden = 1.0 / both[:, GROUP:]
            oat = both[:, :GROUP] * rden
            rdn_s[l, pl.ds(base, SMALL_ROWS), lanes] = rden
            oat_s[l, pl.ds(base, SMALL_ROWS), lanes] = oat
            leps[i, pl.ds(16, SMALL_ROWS), :] = v.astype(f32)
            views = shifted(leps, i, 16, 8, SMALL_ROWS)
            near = conv(views, 8, SMALL_ROWS, lepe_w[l, :, lanes], False)
            o_s[l, pl.ds(base, SMALL_ROWS), lanes] = (oat + near + vec[l, 2:3, lanes]).astype(
                bf16
            )

    def feed(l, base):
        rows_at = pl.ds(base, CHUNK)
        mid = x_s[rows_at, :] + mm(o_s[l, rows_at, :], proj_w[l]) + vec[l, 3:4, :dim]
        n, r = norm_stats(mid)
        n2_s[l, rows_at, :] = n
        r2_s[l, rows_at, :] = jnp.broadcast_to(r, (CHUNK, GROUP))
        m = (n * vec[l, 4:5, :dim] + vec[l, 5:6, :dim]).astype(bf16)
        m_s[l, rows_at, :] = m
        total = mid + vec[l, 7:8, :dim]
        step = 256
        for j in range(ff // step):
            cols = slice(j * step, (j + 1) * step)
            f = mm(m, fc1_w[l, :, cols]) + vec[l, 6:7, cols]
            phi = 0.5 * lax.erf(f * np.float32(math.sqrt(0.5))) + 0.5
            dens = jnp.exp2(f * f * np.float32(-0.5 * LOG2E)) * np.float32(
                1.0 / math.sqrt(2.0 * math.pi)
            )
            g = (f * phi).astype(bf16)
            g_s[l, rows_at, cols] = g
            gp_s[l, rows_at, cols] = (phi + f * dens).astype(bf16)
            total = total + mm(g, fc2_w[l, cols, :])
        x_s[rows_at, :] = total

    def norm_back(dm, n, r, gain):
        dn = dm * gain
        mean_one = jnp.mean(dn, axis=1, keepdims=True)
        mean_two = jnp.mean(dn * n, axis=1, keepdims=True)
        rb = jnp.concatenate([r] * halves, axis=1)
        return rb * (dn - mean_one - n * mean_two)

    def feed_back(l, base):
        rows_at = pl.ds(base, CHUNK)
        e = e_s[rows_at, :]
        dz = e.astype(bf16)
        acc_fc2_b[l] += partial_rows(dz.astype(f32))
        dm = None
        step = 256
        for j in range(ff // step):
            cols = slice(j * step, (j + 1) * step)
            dg = mm(dz, fc2_w[l, cols, :], NT)
            df = (dg * gp_s[l, rows_at, cols].astype(f32)).astype(bf16)
            df_s[rows_at, cols] = df
            acc_fc1_b[l, :, cols] += partial_rows(df.astype(f32))
            part = mm(df, fc1_w[l, :, cols], NT)
            dm = part if dm is None else dm + part
        n = n2_s[l, rows_at, :]
        acc_gain2[l] += partial_rows(dm * n)
        acc_bias2[l] += partial_rows(dm)
        dmid = e + norm_back(dm, n, r2_s[l, rows_at, :], vec[l, 4:5, :dim])
        mid_s[rows_at, :] = dmid
        dy = dmid.astype(bf16)
        acc_proj_b[l] += partial_rows(dy.astype(f32))
        do_s[rows_at, :] = mm(dy, proj_w[l], NT).astype(bf16).astype(f32)

    def lepe_back(l, buf, idx, margin, stride, rows, lanes, v):
        views = [buf[idx, pl.ds(margin - stride + b, rows + 2 * stride), :] for b in (-1, 0, 1)]
        vf = v.astype(f32)
        for k in range(9):
            a, b = divmod(8 - k, 3)
            acc_lepe[l, k, :, lanes] += partial_rows(views[b][a * stride : a * stride + rows] * vf)
        acc_lepe_b[l, :, lanes] += partial_rows(views[1][stride : stride + rows])
        return conv(views, stride, rows, lepe_w[l, :, lanes], True)

    def attend_back(l, group_items, rows, keys, buf, margin, strides, e_ref, ones, unit):
        grads = []
        kbs = []
        ds_all = []
        dop_all = []
        for grp, base, e_at, lep_at, do in group_items:
            lanes = slice(grp * GROUP, (grp + 1) * GROUP)
            rows_at = pl.ds(base, rows)
            buf[lep_at, pl.ds(margin, rows), :] = do
            dop = do * rdn_s[l, rows_at, lanes]
            tail = -(dop * oat_s[l, rows_at, lanes])
            dop_all.append(dop.astype(bf16))
            left = jnp.concatenate([dop.astype(bf16), tail.astype(bf16)], axis=1)
            vo = jnp.concatenate([block_heads(v_s[l, rows_at, lanes], keys), ones[...]], axis=1)
            x = mm(left, vo, NT)
            ds_all.append((e_ref[l, e_at].astype(f32) * x).astype(bf16))
        for i, (grp, base, e_at, lep_at, do) in enumerate(group_items):
            lanes = slice(grp * GROUP, (grp + 1) * GROUP)
            kb = block_heads(k_s[l, pl.ds(base, rows), lanes], keys)
            grads.append([mm(ds_all[i], kb) * SCALE])
        zero_block = jnp.zeros((rows, GROUP), bf16)
        for i in range(0, len(group_items), 2):
            pair = group_items[i : i + 2]

            def spread(first, second):
                return jnp.concatenate(
                    [
                        jnp.concatenate([first, zero_block], axis=1),
                        jnp.concatenate([zero_block, second], axis=1),
                    ],
                    axis=0,
                )

            qs = [q_s[l, pl.ds(it[1], rows), it[0] * GROUP : (it[0] + 1) * GROUP] for it in pair]
            dk = mm(jnp.concatenate(ds_all[i : i + 2], axis=0), spread(*qs), TN)
            es = jnp.concatenate([e_ref[l, it[2]] for it in pair], axis=0)
            dv = mm(es, spread(*dop_all[i : i + 2]), TN)
            for j, (grp, base, e_at, lep_at, do) in enumerate(pair):
                lanes = slice(grp * GROUP, (grp + 1) * GROUP)
                cols = slice(j * GROUP, (j + 1) * GROUP)
                near = lepe_back(
                    l, buf, lep_at, margin, strides[grp], rows, lanes, v_s[l, pl.ds(base, rows), lanes]
                )
                grads[i + j].append(sum_heads(dk[:, cols], keys, rows) * (1.0 / LOG2E))
                grads[i + j].append(sum_heads(dv[:, cols], keys, rows) + near)
        return grads

    def attend_back_big(l, c):
        rows_at = pl.ds(c * BIG_ROWS, BIG_ROWS)
        do_h = do_s[rows_at, :GROUP]
        do_v = to_vertical(do_s[rows_at, GROUP:])
        items = []
        for i, (grp, w, base) in enumerate(windows_big(c)):
            do = (do_h if grp == 0 else do_v)[w * WIN : (w + 1) * WIN]
            items.append((grp, base, 4 * c + 2 * grp + w, i, do))
        grads = attend_back(l, items, WIN, GROUP, lepb, 24, (16, 8), eb_s, onesb, None)
        real = real_big()
        for s in range(3):
            left = jnp.concatenate([grads[0][s], grads[1][s]], axis=0)
            right = from_vertical(jnp.concatenate([grads[2][s], grads[3][s]], axis=0))
            if s == 2:
                left, right = left * real, right * real
            dqkv_s[rows_at, s * dim : s * dim + GROUP] = left.astype(bf16)
            dqkv_s[rows_at, s * dim + GROUP : (s + 1) * dim] = right.astype(bf16)

    def attend_back_small(l, c0, count):
        items = []
        for grp in range(2):
            for c in range(count):
                base = SMALL_BASE + (c0 + c) * SMALL_ROWS
                do = do_s[pl.ds(base, SMALL_ROWS), grp * GROUP : (grp + 1) * GROUP]
                items.append((grp, base, 2 * (c0 + c) + grp, 2 * c + grp, do))
        grads = attend_back(l, items, SMALL_ROWS, 64, leps, 16, (8, 8), es_s, oness, None)
        real = real_small(SMALL_ROWS)
        for (grp, base, e_at, lep_at, do), grad in zip(items, grads):
            for s in range(3):
                value = grad[s] * real if s == 2 else grad[s]
                at = s * dim + grp * GROUP
                dqkv_s[pl.ds(base, SMALL_ROWS), at : at + GROUP] = value.astype(bf16)

    def project_back(l, base):
        rows_at = pl.ds(base, CHUNK)
        da = mm(dqkv_s[rows_at, :], qkv_w[l], NT)
        n = n1_s[l, rows_at, :]
        acc_gain1[l] += partial_rows(da * n)
        acc_bias1[l] += partial_rows(da)
        e_s[rows_at, :] = mid_s[rows_at, :] + norm_back(
            da, n, r1_s[l, rows_at, :], vec[l, 0:1, :dim]
        )

    def loop(count, body):
        def step(i, carry):
            body(i)
            return carry

        lax.fori_loop(0, count, step, 0)

    ingest(tokens, x_s)

    def forward_layer(l):
        loop(BIG_CROPS, lambda c: project(l, pl.multiple_of(c * BIG_ROWS, 16), BIG_ROWS, True))
        project(l, SMALL_BASE, ROWS - SMALL_BASE, False)
        loop(BIG_CROPS, lambda c: attend_big(l, c))
        loop(SMALL_CROPS // 2, lambda c: attend_small(l, 2 * c, 2))
        loop(2, lambda c: feed(l, pl.multiple_of(c * CHUNK, 16)))

    loop(layers, forward_layer)
    emit(x_s, out)
    ingest(cotangent, e_s)

    def backward_layer(step):
        l = layers - 1 - step
        loop(2, lambda c: feed_back(l, pl.multiple_of(c * CHUNK, 16)))
        dz = e_s[...].astype(bf16)
        g_fc2[l] += mm(g_s[l], dz, TN)
        g_fc1[l] += mm(m_s[l], df_s[...], TN)
        g_proj[l] += mm(o_s[l], mid_s[...].astype(bf16), TN)
        loop(BIG_CROPS, lambda c: attend_back_big(l, c))
        loop(SMALL_CROPS // 2, lambda c: attend_back_small(l, 2 * c, 2))
        g_qkv[l] += mm(a_s[l], dqkv_s[...], TN)
        loop(2, lambda c: project_back(l, pl.multiple_of(c * CHUNK, 16)))

    loop(layers, backward_layer)
    emit(e_s, input_grad)

    @pl.when(image == images - 1)
    def _():
        at = 0
        for l in range(layers):
            for ref in big_accs:
                rows, width = ref.shape[1:]
                for lane in range(0, width, GROUP):
                    packed[at : at + rows, :] = ref[l, :, lane : lane + GROUP].astype(bf16)
                    at += rows
        parts = []
        for l in range(layers):
            for acc in small_accs:
                value = acc[l]
                for k in range(value.size // (8 * value.shape[-1])):
                    row = jnp.sum(value[k] if value.ndim == 3 else value, axis=0, keepdims=True)
                    parts += [row[:, c : c + GROUP] for c in range(0, row.shape[1], GROUP)]
        rest = packed.shape[0] - at
        parts.append(jnp.zeros((rest - len(parts), GROUP), f32))
        packed[at:, :] = jnp.concatenate(parts, axis=0).astype(bf16)


def place_of(chip, core, heads):
    return (2 * (chip // heads) + core, lax.rem(chip, heads))


def reduce_kernel(chips, heads, mine, total, near, half, parts, own, sems):
    core = lax.rem(lax.axis_index("dp"), 2)
    chip = (lax.axis_index("dp") // 2) * heads + lax.axis_index("head")
    side = 1 - core
    rows = half.shape[0]
    chunk = rows // chips
    mesh_id = pl.DeviceIdType.MESH

    def other(k):
        return lax.rem(chip + k, chips)

    def signal(k, carry):
        pl.semaphore_signal(
            barrier, inc=1, device_id=place_of(other(k), core, heads), device_id_type=mesh_id
        )
        return carry

    barrier = pltpu.get_barrier_semaphore()
    pl.semaphore_signal(
        barrier, inc=1, device_id=place_of(chip, side, heads), device_id_type=mesh_id
    )
    lax.fori_loop(1, chips, signal, 0)
    pl.semaphore_wait(barrier, chips)

    def rows_of(ref, index, count):
        return ref.at[pl.ds(pl.multiple_of(index * count, 16), count)]

    swap = pltpu.make_async_remote_copy(
        src_ref=rows_of(mine, side, rows),
        dst_ref=near,
        send_sem=sems.at[0, 0],
        recv_sem=sems.at[1, 0],
        device_id=place_of(chip, side, heads),
        device_id_type=mesh_id,
    )
    swap.start()
    swap.wait()

    def add(k, carry):
        at = pl.multiple_of(k * chunk, 16)
        mine_at = pl.multiple_of(core * rows + k * chunk, 16)
        half[pl.ds(at, chunk), :] = (
            mine[pl.ds(mine_at, chunk), :].astype(f32) + near[pl.ds(at, chunk), :].astype(f32)
        ).astype(bf16)
        return carry

    lax.fori_loop(0, chips, add, 0)

    def scatter(k):
        return pltpu.make_async_remote_copy(
            src_ref=rows_of(half, other(k), chunk),
            dst_ref=parts.at[k],
            send_sem=sems.at[2, k],
            recv_sem=sems.at[3, k],
            device_id=place_of(other(k), core, heads),
            device_id_type=mesh_id,
        )

    def start_scatter(k, carry):
        scatter(k).start()
        return carry

    lax.fori_loop(1, chips, start_scatter, 0)

    def gather(k, acc):
        scatter(k).wait()
        return acc + parts[k].astype(f32)

    mine_sum = half[pl.ds(pl.multiple_of(chip * chunk, 16), chunk), :].astype(f32)
    mine_sum = lax.fori_loop(1, chips, gather, mine_sum)
    own[...] = mine_sum.astype(bf16)

    def spread(k):
        return pltpu.make_async_remote_copy(
            src_ref=own,
            dst_ref=rows_of(total, core * chips + chip, chunk),
            send_sem=sems.at[4, k],
            recv_sem=sems.at[5, k],
            device_id=place_of(other(k), core, heads),
            device_id_type=mesh_id,
        )

    def sent(k, source):
        at = core * chips + lax.rem(chip + chips - k, chips)
        return pltpu.make_async_remote_copy(
            src_ref=source if source is not None else rows_of(total, at, chunk),
            dst_ref=rows_of(total, at, chunk),
            send_sem=sems.at[6, k],
            recv_sem=sems.at[7, k],
            device_id=place_of(chip, side, heads),
            device_id_type=mesh_id,
        )

    def start_spread(k, carry):
        spread(k).start()
        return carry

    lax.fori_loop(1, chips, start_spread, 0)
    sent(0, own).start()
    total[pl.ds(pl.multiple_of((core * chips + chip) * chunk, 16), chunk), :] = own[...]

    def pass_on(k, carry):
        spread(k).wait()
        sent(k, None).start()
        return carry

    lax.fori_loop(1, chips, pass_on, 0)
    sent(0, own).wait()

    def finish(k, carry):
        sent(k, None).wait()
        return carry

    lax.fori_loop(1, chips, finish, 0)


def unpack_kernel(factor, packed, *refs):
    g_gain1, g_bias1, g_qkv, g_lepe, g_lepe_b, g_proj, g_proj_b = refs[:7]
    g_gain2, g_bias2, g_fc1, g_fc1_b, g_fc2, g_fc2_b = refs[7:]
    layers = g_qkv.shape[0]
    at = 0
    for l in range(layers):
        for ref in (g_qkv, g_proj, g_fc1, g_fc2):
            rows, width = ref.shape[1:]
            for lane in range(0, width, GROUP):
                ref[l, :, lane : lane + GROUP] = packed[at : at + rows, :].astype(f32) * factor
                at += rows
    rest = packed[at:, :].astype(f32) * factor
    row = 0
    for l in range(layers):
        for ref in (g_gain1, g_bias1, g_lepe, g_lepe_b, g_proj_b, g_gain2, g_bias2, g_fc1_b, g_fc2_b):
            width = ref.shape[-1]
            for k in range(ref.size // (layers * width)):
                for c in range(0, width, GROUP):
                    value = rest[row : row + 1]
                    if ref.ndim == 3:
                        ref[l, k : k + 1, c : c + GROUP] = value
                    else:
                        ref[l : l + 1, c : c + GROUP] = value
                    row += 1


def local(
    tokens,
    crop_side,
    cotangent,
    ln1_gain,
    ln1_bias,
    qkv_weight,
    lepe_weight,
    lepe_bias,
    proj_weight,
    proj_bias,
    ln2_gain,
    ln2_bias,
    fc1_weight,
    fc1_bias,
    fc2_weight,
    fc2_bias,
):
    images, tok, dim = tokens.shape
    layers = qkv_weight.shape[0]
    ff = fc1_weight.shape[2]
    weights = (
        ln1_gain,
        ln1_bias,
        qkv_weight,
        lepe_weight,
        lepe_bias,
        proj_weight,
        proj_bias,
        ln2_gain,
        ln2_bias,
        fc1_weight,
        fc1_bias,
        fc2_weight,
        fc2_bias,
    )
    block = pl.BlockSpec((1, tok, dim), lambda i: (i, 0, 0))
    whole = pl.BlockSpec(memory_space=pltpu.VMEM)
    heads = lax.axis_size("head")
    devices = lax.axis_size("dp") * heads
    chips = devices // 2
    packed_rows = sum(math.prod(w.shape) for w in weights) // GROUP
    packed_rows = -(-packed_rows // (16 * devices)) * 16 * devices
    out, input_grad, packed = pl.pallas_call(
        kernel,
        grid=(images,),
        out_shape=[
            jax.ShapeDtypeStruct(tokens.shape, bf16),
            jax.ShapeDtypeStruct(tokens.shape, f32),
            jax.ShapeDtypeStruct((packed_rows, GROUP), bf16),
        ],
        in_specs=[pl.BlockSpec(memory_space=pltpu.SMEM), block, block] + [whole] * len(weights),
        out_specs=[block, block, whole],
        scratch_shapes=[
            pltpu.VMEM(qkv_weight.shape, f32),
            pltpu.VMEM(proj_weight.shape, f32),
            pltpu.VMEM(fc1_weight.shape, f32),
            pltpu.VMEM(fc2_weight.shape, f32),
            pltpu.SMEM((BIG_CROPS + SMALL_CROPS,), jnp.int32),
            pltpu.VMEM((dim // GROUP, tok + 16, GROUP), f32),
            pltpu.VMEM((ROWS, dim), f32),
            pltpu.VMEM((ROWS, dim), f32),
            pltpu.VMEM((ROWS, dim), f32),
            pltpu.VMEM((layers, ROWS, dim), f32),
            pltpu.VMEM((layers, ROWS, GROUP), f32),
            pltpu.VMEM((layers, ROWS, dim), bf16),
            pltpu.VMEM((layers, ROWS, dim), bf16),
            pltpu.VMEM((layers, ROWS, dim), bf16),
            pltpu.VMEM((layers, ROWS, dim), bf16),
            pltpu.VMEM((layers, 4 * BIG_CROPS, WIN, 4 * GROUP), bf16),
            pltpu.VMEM((layers, 2 * SMALL_CROPS, SMALL_ROWS, 2 * GROUP), bf16),
            pltpu.VMEM((layers, ROWS, dim), f32),
            pltpu.VMEM((layers, ROWS, dim), f32),
            pltpu.VMEM((layers, ROWS, dim), bf16),
            pltpu.VMEM((layers, ROWS, dim), f32),
            pltpu.VMEM((layers, ROWS, GROUP), f32),
            pltpu.VMEM((layers, ROWS, dim), bf16),
            pltpu.VMEM((layers, ROWS, ff), bf16),
            pltpu.VMEM((layers, ROWS, ff), bf16),
            pltpu.VMEM((ROWS, ff), bf16),
            pltpu.VMEM((ROWS, dim), f32),
            pltpu.VMEM((ROWS, 3 * dim), bf16),
            pltpu.VMEM((4, WIN + 48, GROUP), f32),
            pltpu.VMEM((4, SMALL_ROWS + 32, GROUP), f32),
            pltpu.VMEM((4 * GROUP, GROUP), bf16),
            pltpu.VMEM((4 * 64, GROUP), bf16),
            pltpu.VMEM((layers, 8, ff), f32),
            pltpu.VMEM((layers, 8, dim), f32),
            pltpu.VMEM((layers, 8, dim), f32),
            pltpu.VMEM((layers, 9, 8, dim), f32),
            pltpu.VMEM((layers, 8, dim), f32),
            pltpu.VMEM((layers, 8, dim), f32),
            pltpu.VMEM((layers, 8, dim), f32),
            pltpu.VMEM((layers, 8, dim), f32),
            pltpu.VMEM((layers, 8, ff), f32),
            pltpu.VMEM((layers, 8, dim), f32),
        ],
        compiler_params=pltpu.CompilerParams(
            dimension_semantics=("arbitrary",), vmem_limit_bytes=62 * 1024 * 1024
        ),
    )(crop_side, tokens, cotangent, *weights)
    half_rows = packed_rows // 2
    chunk = half_rows // chips
    total = pl.pallas_call(
        partial(reduce_kernel, chips, heads),
        out_shape=jax.ShapeDtypeStruct((packed_rows, GROUP), bf16),
        in_specs=[whole],
        out_specs=whole,
        scratch_shapes=[
            pltpu.VMEM((half_rows, GROUP), bf16),
            pltpu.VMEM((half_rows, GROUP), bf16),
            pltpu.VMEM((chips, chunk, GROUP), bf16),
            pltpu.VMEM((chunk, GROUP), bf16),
            pltpu.SemaphoreType.DMA((8, chips)),
        ],
        compiler_params=pltpu.CompilerParams(
            collective_id=0, has_side_effects=True, vmem_limit_bytes=32 * 1024 * 1024
        ),
    )(packed)
    factor = 1.0 / math.sqrt(devices * images * tok)
    grads = pl.pallas_call(
        partial(unpack_kernel, factor),
        out_shape=[jax.ShapeDtypeStruct(w.shape, f32) for w in weights],
        in_specs=[whole],
        out_specs=[whole] * len(weights),
        compiler_params=pltpu.CompilerParams(vmem_limit_bytes=32 * 1024 * 1024),
    )(total)
    return (out, input_grad) + tuple(grads)


def solution(mesh):
    sharded = P(("dp", "head"), None, None)
    return jax.shard_map(
        local,
        mesh=mesh,
        in_specs=(sharded, P(("dp", "head"), None), sharded) + (P(),) * 13,
        out_specs=(sharded, sharded) + (P(),) * 13,
        check_vma=False,
    )
```

```python
from functools import partial
import math

import jax
import jax.numpy as jnp
import numpy as np
from jax import lax
from jax.experimental import pallas as pl
from jax.experimental.pallas import tpu as pltpu
from jax.sharding import PartitionSpec as P

HEADS_GROUP = 4
HEAD_DIM = 32
SW = 7
BIG = 14
SMALL = 6
BIG_CROPS = 2
SMALL_CROPS = 6
GROUP = 128
EPSILON = 1e-05

BIG_ROWS = BIG * 16
WIN = SW * 16
SMALL_ROWS = SMALL * 8
SMALL_BASE = BIG_CROPS * BIG_ROWS
ROWS = SMALL_BASE + SMALL_CROPS * SMALL_ROWS
CHUNK = ROWS // 2

SCALE = HEAD_DIM**-0.5
LOG2E = math.log2(math.e)
NEG = -1e30

bf16 = jnp.bfloat16
f32 = jnp.float32

NN = (((1,), (0,)), ((), ()))
NT = (((1,), (1,)), ((), ()))
TN = (((0,), (0,)), ((), ()))


def mm(a, b, dims=NN):
    return lax.dot_general(a, b, dims, preferred_element_type=f32)


def iota(shape, dim):
    return lax.broadcasted_iota(jnp.int32, shape, dim)


def to_vertical(x):
    x4 = x.reshape(BIG, 2, 8, x.shape[1])
    return jnp.concatenate([x4[:, 0].reshape(WIN, -1), x4[:, 1].reshape(WIN, -1)], axis=0)


def from_vertical(y):
    y4 = y.reshape(2, BIG, 8, y.shape[1])
    return jnp.stack([y4[0], y4[1]], axis=1).reshape(BIG_ROWS, -1)


def real_big():
    sub = iota((BIG_ROWS, GROUP), 0) % 16
    return ((sub != 0) & (sub != 15)).astype(f32)


def real_small(rows):
    return ((iota((rows, GROUP), 0) % 8) < SMALL).astype(f32)


def partial_rows(x):
    return jnp.sum(x.reshape(x.shape[0] // 8, 8, x.shape[1]), axis=0)


def head_mask(h):
    lane = iota((1, GROUP), 1)
    return ((lane >= h * HEAD_DIM) & (lane < (h + 1) * HEAD_DIM)).astype(f32)


def block_heads(x, keys):
    rows = x.shape[0]
    parts = []
    for h in range(HEADS_GROUP):
        part = x * head_mask(h).astype(x.dtype)
        parts.append(part)
        if keys > rows:
            parts.append(jnp.zeros((keys - rows, GROUP), x.dtype))
    return jnp.concatenate(parts, axis=0)


def ones_heads(keys):
    row_head = iota((HEADS_GROUP * keys, GROUP), 0) // keys
    lane_head = iota((HEADS_GROUP * keys, GROUP), 1) // HEAD_DIM
    return (row_head == lane_head).astype(f32).astype(bf16)


def sum_heads(x, keys, rows):
    total = None
    for h in range(HEADS_GROUP):
        part = x[h * keys : h * keys + rows] * head_mask(h)
        total = part if total is None else total + part
    return total


def kernel(
    crop_side,
    tokens,
    cotangent,
    ln1_gain,
    ln1_bias,
    qkv_w,
    lepe_w,
    lepe_b,
    proj_w,
    proj_b,
    ln2_gain,
    ln2_bias,
    fc1_w,
    fc1_b,
    fc2_w,
    fc2_b,
    out,
    input_grad,
    packed,
    g_qkv,
    g_proj,
    g_fc1,
    g_fc2,
    starts,
    stage,
    x_s,
    mid_s,
    e_s,
    n1_s,
    r1_s,
    a_s,
    q_s,
    k_s,
    v_s,
    eb_s,
    es_s,
    oat_s,
    rdn_s,
    o_s,
    n2_s,
    r2_s,
    m_s,
    g_s,
    gp_s,
    df_s,
    do_s,
    dqkv_s,
    lepb,
    leps,
    onesb,
    oness,
    vec,
    acc_gain1,
    acc_bias1,
    acc_lepe,
    acc_lepe_b,
    acc_proj_b,
    acc_gain2,
    acc_bias2,
    acc_fc1_b,
    acc_fc2_b,
):
    image = pl.program_id(0)
    images = pl.num_programs(0)
    layers = qkv_w.shape[0]
    dim = tokens.shape[2]
    tok = tokens.shape[1]
    crops = crop_side.shape[1]
    ff = fc1_w.shape[2]
    halves = dim // GROUP

    big_accs = (g_qkv, g_proj, g_fc1, g_fc2)
    small_accs = (
        acc_gain1,
        acc_bias1,
        acc_lepe,
        acc_lepe_b,
        acc_proj_b,
        acc_gain2,
        acc_bias2,
        acc_fc1_b,
        acc_fc2_b,
    )

    @pl.when(image == 0)
    def _():
        for ref in big_accs + small_accs:
            ref[...] = jnp.zeros(ref.shape, f32)
        lepb[...] = jnp.zeros(lepb.shape, f32)
        leps[...] = jnp.zeros(leps.shape, f32)
        stage[...] = jnp.zeros(stage.shape, f32)
        onesb[...] = ones_heads(GROUP)
        oness[...] = ones_heads(64)
        for l in range(layers):
            for i, ref in enumerate(
                (ln1_gain, ln1_bias, lepe_b, proj_b, ln2_gain, ln2_bias, fc1_b, fc2_b)
            ):
                vec[l, i : i + 1, : ref.shape[1]] = ref[l : l + 1, :]

    def place(j, carry):
        start, n_big, n_small = carry
        side = crop_side[image, j]
        is_big = side == BIG
        slot = jnp.where(is_big, n_big, BIG_CROPS + n_small)
        starts[slot] = start
        big_add = is_big.astype(jnp.int32)
        return (start + side * side, n_big + big_add, n_small + 1 - big_add)

    zero = jnp.int32(0)
    lax.fori_loop(0, crops, place, (zero, zero, zero))

    keep_lo = (iota((8, GROUP), 0) != 0).astype(f32)
    keep_hi = (iota((8, GROUP), 0) != 7).astype(f32)
    keep_small = (iota((8, GROUP), 0) < SMALL).astype(f32)

    def ingest(source, target):
        for half in range(halves):
            stage[half, 8 : 8 + tok, :] = source[0, :, half * GROUP : (half + 1) * GROUP].astype(f32)
        for c in range(BIG_CROPS):
            start = starts[c] + 7
            for r in range(BIG):
                for half in range(halves):
                    lanes = slice(half * GROUP, (half + 1) * GROUP)
                    base = c * BIG_ROWS + r * 16
                    lo = stage[half, pl.ds(start + r * BIG, 8), :]
                    hi = stage[half, pl.ds(start + r * BIG + 8, 8), :]
                    target[base : base + 8, lanes] = lo * keep_lo
                    target[base + 8 : base + 16, lanes] = hi * keep_hi
        for c in range(SMALL_CROPS):
            start = starts[BIG_CROPS + c] + 8
            for r in range(SMALL):
                for half in range(halves):
                    lanes = slice(half * GROUP, (half + 1) * GROUP)
                    base = SMALL_BASE + c * SMALL_ROWS + r * 8
                    lo = stage[half, pl.ds(start + r * SMALL, 8), :]
                    target[base : base + 8, lanes] = lo * keep_small

    def put(half, at, value, keep):
        old = stage[half, pl.ds(at, 8), :]
        stage[half, pl.ds(at, 8), :] = jnp.where(keep > 0, value, old)

    def emit(source, target):
        for c in range(BIG_CROPS):
            start = starts[c] + 7
            for r in range(BIG):
                for half in range(halves):
                    lanes = slice(half * GROUP, (half + 1) * GROUP)
                    base = c * BIG_ROWS + r * 16
                    put(half, start + r * BIG, source[base : base + 8, lanes], keep_lo)
                    put(half, start + r * BIG + 8, source[base + 8 : base + 16, lanes], keep_hi)
        for c in range(SMALL_CROPS):
            start = starts[BIG_CROPS + c] + 8
            for r in range(SMALL):
                for half in range(halves):
                    lanes = slice(half * GROUP, (half + 1) * GROUP)
                    base = SMALL_BASE + c * SMALL_ROWS + r * 8
                    put(half, start + r * SMALL, source[base : base + 8, lanes], keep_small)
        for half in range(halves):
            target[0, :, half * GROUP : (half + 1) * GROUP] = stage[half, 8 : 8 + tok, :].astype(
                target.dtype
            )

    def norm_stats(x):
        center = x - jnp.mean(x, axis=1, keepdims=True)
        r = lax.rsqrt(jnp.mean(center * center, axis=1, keepdims=True) + EPSILON)
        return center * r, r

    def project(l, base, rows, big):
        rows_at = pl.ds(base, rows)
        n, r = norm_stats(x_s[rows_at, :])
        n1_s[l, rows_at, :] = n
        r1_s[l, rows_at, :] = jnp.broadcast_to(r, (rows, GROUP))
        a = (n * vec[l, 0:1, :dim] + vec[l, 1:2, :dim]).astype(bf16)
        a_s[l, rows_at, :] = a
        qkv = mm(a, qkv_w[l])
        real = real_big() if big else real_small(rows)
        for grp in range(2):
            cols = [slice(s * dim + grp * GROUP, s * dim + (grp + 1) * GROUP) for s in range(3)]
            q = qkv[:, cols[0]] * (SCALE * LOG2E)
            k = qkv[:, cols[1]]
            v = qkv[:, cols[2]] * real
            if big and grp == 1:
                q, k, v = to_vertical(q), to_vertical(k), to_vertical(v)
            lanes = slice(grp * GROUP, (grp + 1) * GROUP)
            q_s[l, rows_at, lanes] = q.astype(bf16)
            k_s[l, rows_at, lanes] = k.astype(bf16)
            v_s[l, rows_at, lanes] = v.astype(bf16)

    def pad_row(grp, w):
        u = iota((1, HEADS_GROUP * GROUP), 1) % GROUP
        if grp == 0:
            bad = (u % 16 == 0) | (u % 16 == 15)
        elif w == 0:
            bad = u % 8 == 0
        else:
            bad = u % 8 == 7
        return jnp.where(bad | (u >= WIN), NEG, 0.0).astype(f32)

    def pad_row_small():
        u = iota((1, HEADS_GROUP * 64), 1) % 64
        return jnp.where((u % 8 >= SMALL) | (u >= SMALL_ROWS), NEG, 0.0).astype(f32)

    def shifted(buf, idx, margin, stride, rows):
        return [buf[idx, pl.ds(margin - stride + b, rows + 2 * stride), :] for b in (-1, 0, 1)]

    def conv(views, stride, rows, weights, flip):
        total = None
        for a in range(3):
            for b in range(3):
                k = 3 * a + b
                wk = weights[8 - k : 9 - k] if flip else weights[k : k + 1]
                term = views[b][a * stride : a * stride + rows] * wk
                total = term if total is None else total + term
        return total

    def windows_big(c):
        for grp in range(2):
            for w in range(2):
                yield grp, w, c * BIG_ROWS + w * WIN

    def attend_big(l, c):
        items = list(windows_big(c))
        scores = []
        for grp, w, base in items:
            lanes = slice(grp * GROUP, (grp + 1) * GROUP)
            q = q_s[l, pl.ds(base, WIN), lanes]
            kb = block_heads(k_s[l, pl.ds(base, WIN), lanes], GROUP)
            scores.append(mm(q, kb, NT) + pad_row(grp, w))
        for i, (grp, w, base) in enumerate(items):
            parts = []
            for h in range(HEADS_GROUP):
                s = scores[i][:, h * GROUP : (h + 1) * GROUP]
                parts.append(jnp.exp2(s - jnp.max(s, axis=1, keepdims=True)).astype(bf16))
            eb_s[l, 4 * c + 2 * grp + w] = jnp.concatenate(parts, axis=1)
        outs = []
        for i, (grp, w, base) in enumerate(items):
            lanes = slice(grp * GROUP, (grp + 1) * GROUP)
            v = v_s[l, pl.ds(base, WIN), lanes]
            vo = jnp.concatenate([block_heads(v, GROUP), onesb[...]], axis=1)
            both = mm(eb_s[l, 4 * c + 2 * grp + w], vo)
            rden = 1.0 / both[:, GROUP:]
            oat = both[:, :GROUP] * rden
            rdn_s[l, pl.ds(base, WIN), lanes] = rden
            oat_s[l, pl.ds(base, WIN), lanes] = oat
            stride = 16 if grp == 0 else 8
            lepb[i, pl.ds(24, WIN), :] = v.astype(f32)
            views = shifted(lepb, i, 24, stride, WIN)
            near = conv(views, stride, WIN, lepe_w[l, :, lanes], False)
            outs.append(oat + near + vec[l, 2:3, lanes])
        rows_at = pl.ds(c * BIG_ROWS, BIG_ROWS)
        o_s[l, rows_at, :GROUP] = jnp.concatenate(outs[:2], axis=0).astype(bf16)
        o_s[l, rows_at, GROUP:] = from_vertical(jnp.concatenate(outs[2:], axis=0)).astype(bf16)

    def attend_small(l, c0, count):
        items = [
            (grp, c0 + c, SMALL_BASE + (c0 + c) * SMALL_ROWS, 2 * c + grp)
            for c in range(count)
            for grp in range(2)
        ]
        low = iota((SMALL_ROWS, GROUP), 1) < 64
        scores = []
        for grp, c, base, i in items:
            lanes = slice(grp * GROUP, (grp + 1) * GROUP)
            q = q_s[l, pl.ds(base, SMALL_ROWS), lanes]
            kb = block_heads(k_s[l, pl.ds(base, SMALL_ROWS), lanes], 64)
            scores.append(mm(q, kb, NT) + pad_row_small())
        for j, (grp, c, base, i) in enumerate(items):
            parts = []
            for t in range(2):
                s = scores[j][:, t * GROUP : (t + 1) * GROUP]
                top_lo = jnp.max(jnp.where(low, s, 2 * NEG), axis=1, keepdims=True)
                top_hi = jnp.max(jnp.where(low, 2 * NEG, s), axis=1, keepdims=True)
                parts.append(jnp.exp2(s - jnp.where(low, top_lo, top_hi)).astype(bf16))
            es_s[l, 2 * c + grp] = jnp.concatenate(parts, axis=1)
        for grp, c, base, i in items:
            lanes = slice(grp * GROUP, (grp + 1) * GROUP)
            v = v_s[l, pl.ds(base, SMALL_ROWS), lanes]
            vo = jnp.concatenate([block_heads(v, 64), oness[...]], axis=1)
            both = mm(es_s[l, 2 * c + grp], vo)
            rden = 1.0 / both[:, GROUP:]
            oat = both[:, :GROUP] * rden
            rdn_s[l, pl.ds(base, SMALL_ROWS), lanes] = rden
            oat_s[l, pl.ds(base, SMALL_ROWS), lanes] = oat
            leps[i, pl.ds(16, SMALL_ROWS), :] = v.astype(f32)
            views = shifted(leps, i, 16, 8, SMALL_ROWS)
            near = conv(views, 8, SMALL_ROWS, lepe_w[l, :, lanes], False)
            o_s[l, pl.ds(base, SMALL_ROWS), lanes] = (oat + near + vec[l, 2:3, lanes]).astype(
                bf16
            )

    def feed(l, base):
        rows_at = pl.ds(base, CHUNK)
        mid = x_s[rows_at, :] + mm(o_s[l, rows_at, :], proj_w[l]) + vec[l, 3:4, :dim]
        n, r = norm_stats(mid)
        n2_s[l, rows_at, :] = n
        r2_s[l, rows_at, :] = jnp.broadcast_to(r, (CHUNK, GROUP))
        m = (n * vec[l, 4:5, :dim] + vec[l, 5:6, :dim]).astype(bf16)
        m_s[l, rows_at, :] = m
        total = mid + vec[l, 7:8, :dim]
        step = 256
        for j in range(ff // step):
            cols = slice(j * step, (j + 1) * step)
            f = mm(m, fc1_w[l, :, cols]) + vec[l, 6:7, cols]
            phi = 0.5 * lax.erf(f * np.float32(math.sqrt(0.5))) + 0.5
            dens = jnp.exp2(f * f * np.float32(-0.5 * LOG2E)) * np.float32(
                1.0 / math.sqrt(2.0 * math.pi)
            )
            g = (f * phi).astype(bf16)
            g_s[l, rows_at, cols] = g
            gp_s[l, rows_at, cols] = (phi + f * dens).astype(bf16)
            total = total + mm(g, fc2_w[l, cols, :])
        x_s[rows_at, :] = total

    def norm_back(dm, n, r, gain):
        dn = dm * gain
        mean_one = jnp.mean(dn, axis=1, keepdims=True)
        mean_two = jnp.mean(dn * n, axis=1, keepdims=True)
        rb = jnp.concatenate([r] * halves, axis=1)
        return rb * (dn - mean_one - n * mean_two)

    def feed_back(l, base):
        rows_at = pl.ds(base, CHUNK)
        e = e_s[rows_at, :]
        dz = e.astype(bf16)
        acc_fc2_b[l] += partial_rows(dz.astype(f32))
        dm = None
        step = 256
        for j in range(ff // step):
            cols = slice(j * step, (j + 1) * step)
            dg = mm(dz, fc2_w[l, cols, :], NT)
            df = (dg * gp_s[l, rows_at, cols].astype(f32)).astype(bf16)
            df_s[rows_at, cols] = df
            acc_fc1_b[l, :, cols] += partial_rows(df.astype(f32))
            part = mm(df, fc1_w[l, :, cols], NT)
            dm = part if dm is None else dm + part
        n = n2_s[l, rows_at, :]
        acc_gain2[l] += partial_rows(dm * n)
        acc_bias2[l] += partial_rows(dm)
        dmid = e + norm_back(dm, n, r2_s[l, rows_at, :], vec[l, 4:5, :dim])
        mid_s[rows_at, :] = dmid
        dy = dmid.astype(bf16)
        acc_proj_b[l] += partial_rows(dy.astype(f32))
        do_s[rows_at, :] = mm(dy, proj_w[l], NT).astype(bf16).astype(f32)

    def lepe_back(l, buf, idx, margin, stride, rows, lanes, v):
        views = [buf[idx, pl.ds(margin - stride + b, rows + 2 * stride), :] for b in (-1, 0, 1)]
        vf = v.astype(f32)
        for k in range(9):
            a, b = divmod(8 - k, 3)
            acc_lepe[l, k, :, lanes] += partial_rows(views[b][a * stride : a * stride + rows] * vf)
        acc_lepe_b[l, :, lanes] += partial_rows(views[1][stride : stride + rows])
        return conv(views, stride, rows, lepe_w[l, :, lanes], True)

    def attend_back(l, group_items, rows, keys, buf, margin, strides, e_ref, ones, unit):
        grads = []
        kbs = []
        ds_all = []
        dop_all = []
        for grp, base, e_at, lep_at, do in group_items:
            lanes = slice(grp * GROUP, (grp + 1) * GROUP)
            rows_at = pl.ds(base, rows)
            buf[lep_at, pl.ds(margin, rows), :] = do
            dop = do * rdn_s[l, rows_at, lanes]
            tail = -(dop * oat_s[l, rows_at, lanes])
            dop_all.append(dop.astype(bf16))
            left = jnp.concatenate([dop.astype(bf16), tail.astype(bf16)], axis=1)
            vo = jnp.concatenate([block_heads(v_s[l, rows_at, lanes], keys), ones[...]], axis=1)
            x = mm(left, vo, NT)
            ds_all.append((e_ref[l, e_at].astype(f32) * x).astype(bf16))
        for i, (grp, base, e_at, lep_at, do) in enumerate(group_items):
            lanes = slice(grp * GROUP, (grp + 1) * GROUP)
            kb = block_heads(k_s[l, pl.ds(base, rows), lanes], keys)
            grads.append([mm(ds_all[i], kb) * SCALE])
        zero_block = jnp.zeros((rows, GROUP), bf16)
        for i in range(0, len(group_items), 2):
            pair = group_items[i : i + 2]

            def spread(first, second):
                return jnp.concatenate(
                    [
                        jnp.concatenate([first, zero_block], axis=1),
                        jnp.concatenate([zero_block, second], axis=1),
                    ],
                    axis=0,
                )

            qs = [q_s[l, pl.ds(it[1], rows), it[0] * GROUP : (it[0] + 1) * GROUP] for it in pair]
            dk = mm(jnp.concatenate(ds_all[i : i + 2], axis=0), spread(*qs), TN)
            es = jnp.concatenate([e_ref[l, it[2]] for it in pair], axis=0)
            dv = mm(es, spread(*dop_all[i : i + 2]), TN)
            for j, (grp, base, e_at, lep_at, do) in enumerate(pair):
                lanes = slice(grp * GROUP, (grp + 1) * GROUP)
                cols = slice(j * GROUP, (j + 1) * GROUP)
                near = lepe_back(
                    l, buf, lep_at, margin, strides[grp], rows, lanes, v_s[l, pl.ds(base, rows), lanes]
                )
                grads[i + j].append(sum_heads(dk[:, cols], keys, rows) * (1.0 / LOG2E))
                grads[i + j].append(sum_heads(dv[:, cols], keys, rows) + near)
        return grads

    def attend_back_big(l, c):
        rows_at = pl.ds(c * BIG_ROWS, BIG_ROWS)
        do_h = do_s[rows_at, :GROUP]
        do_v = to_vertical(do_s[rows_at, GROUP:])
        items = []
        for i, (grp, w, base) in enumerate(windows_big(c)):
            do = (do_h if grp == 0 else do_v)[w * WIN : (w + 1) * WIN]
            items.append((grp, base, 4 * c + 2 * grp + w, i, do))
        grads = attend_back(l, items, WIN, GROUP, lepb, 24, (16, 8), eb_s, onesb, None)
        real = real_big()
        for s in range(3):
            left = jnp.concatenate([grads[0][s], grads[1][s]], axis=0)
            right = from_vertical(jnp.concatenate([grads[2][s], grads[3][s]], axis=0))
            if s == 2:
                left, right = left * real, right * real
            dqkv_s[rows_at, s * dim : s * dim + GROUP] = left.astype(bf16)
            dqkv_s[rows_at, s * dim + GROUP : (s + 1) * dim] = right.astype(bf16)

    def attend_back_small(l, c0, count):
        items = []
        for grp in range(2):
            for c in range(count):
                base = SMALL_BASE + (c0 + c) * SMALL_ROWS
                do = do_s[pl.ds(base, SMALL_ROWS), grp * GROUP : (grp + 1) * GROUP]
                items.append((grp, base, 2 * (c0 + c) + grp, 2 * c + grp, do))
        grads = attend_back(l, items, SMALL_ROWS, 64, leps, 16, (8, 8), es_s, oness, None)
        real = real_small(SMALL_ROWS)
        for (grp, base, e_at, lep_at, do), grad in zip(items, grads):
            for s in range(3):
                value = grad[s] * real if s == 2 else grad[s]
                at = s * dim + grp * GROUP
                dqkv_s[pl.ds(base, SMALL_ROWS), at : at + GROUP] = value.astype(bf16)

    def project_back(l, base):
        rows_at = pl.ds(base, CHUNK)
        da = mm(dqkv_s[rows_at, :], qkv_w[l], NT)
        n = n1_s[l, rows_at, :]
        acc_gain1[l] += partial_rows(da * n)
        acc_bias1[l] += partial_rows(da)
        e_s[rows_at, :] = mid_s[rows_at, :] + norm_back(
            da, n, r1_s[l, rows_at, :], vec[l, 0:1, :dim]
        )

    def loop(count, body):
        def step(i, carry):
            body(i)
            return carry

        lax.fori_loop(0, count, step, 0)

    ingest(tokens, x_s)

    def forward_layer(l):
        for c in range(BIG_CROPS): project(l, c*BIG_ROWS, BIG_ROWS, True)
        project(l, SMALL_BASE, ROWS - SMALL_BASE, False)
        for c in range(BIG_CROPS): attend_big(l, c)
        attend_small(l, 0, 6)
        for c in range(2): feed(l, c*CHUNK)

    for l in range(layers): forward_layer(l)
    emit(x_s, out)
    ingest(cotangent, e_s)

    def backward_layer(step):
        l = layers - 1 - step
        for c in range(2): feed_back(l, c*CHUNK)
        dz = e_s[...].astype(bf16)
        g_fc2[l] += mm(g_s[l], dz, TN)
        g_fc1[l] += mm(m_s[l], df_s[...], TN)
        g_proj[l] += mm(o_s[l], mid_s[...].astype(bf16), TN)
        for c in range(BIG_CROPS): attend_back_big(l, c)
        attend_back_small(l, 0, 6)
        g_qkv[l] += mm(a_s[l], dqkv_s[...], TN)
        for c in range(2): project_back(l, c*CHUNK)

    for l in range(layers): backward_layer(l)
    emit(e_s, input_grad)

    @pl.when(image == images - 1)
    def _():
        at = 0
        for l in range(layers):
            for ref in big_accs:
                rows, width = ref.shape[1:]
                for lane in range(0, width, GROUP):
                    packed[at : at + rows, :] = ref[l, :, lane : lane + GROUP].astype(bf16)
                    at += rows
        parts = []
        for l in range(layers):
            for acc in small_accs:
                value = acc[l]
                for k in range(value.size // (8 * value.shape[-1])):
                    row = jnp.sum(value[k] if value.ndim == 3 else value, axis=0, keepdims=True)
                    parts += [row[:, c : c + GROUP] for c in range(0, row.shape[1], GROUP)]
        rest = packed.shape[0] - at
        parts.append(jnp.zeros((rest - len(parts), GROUP), f32))
        packed[at:, :] = jnp.concatenate(parts, axis=0).astype(bf16)


class Grid:
    def __init__(self, dp, heads):
        chips = dp // 2
        self.heads = heads
        self.levels = next(n for n in (4, 2, 1) if chips % n == 0)
        self.low = chips // self.levels
        self.plane = self.low * heads
        self.chips = chips * heads

    def split(self, rows):
        units = max(2, -(-rows // (2 * 16 * self.chips)))
        first = max(1, (2 * units + 1) // 3)
        return 16 * first, 16 * (units - first)

    def packed_rows(self, rows):
        return 2 * self.chips * sum(self.split(rows))

    def scratch(self, rows):
        ca, cb = self.split(rows)
        half = self.chips * (ca + cb)
        return [
            pltpu.VMEM((half, GROUP), bf16),
            pltpu.VMEM((half, GROUP), bf16),
            pltpu.VMEM((self.plane, self.levels * ca, GROUP), bf16),
            pltpu.VMEM((self.levels, self.plane * cb, GROUP), bf16),
            pltpu.VMEM((1, self.levels * ca, GROUP), bf16),
            pltpu.VMEM((1, self.plane * cb, GROUP), bf16),
            pltpu.SemaphoreType.DMA((6, 2, self.plane)),
            pltpu.SemaphoreType.DMA((6, 2, self.levels)),
        ]


def each(first, last, body):
    def step(k, carry):
        body(k)
        return carry

    lax.fori_loop(first, last, step, 0)


class Here:
    def __init__(self, grid):
        self.grid = grid
        dp = lax.axis_index("dp")
        self.core = lax.rem(dp, 2)
        chip = dp // 2
        self.z = chip // grid.low
        self.p = lax.rem(chip, grid.low) * grid.heads + lax.axis_index("head")

    def device(self, z, p, core):
        low = p // self.grid.heads
        return (2 * (z * self.grid.low + low) + core, lax.rem(p, self.grid.heads))

    def sibling(self):
        return self.device(self.z, self.p, 1 - self.core)

    def in_plane(self, k):
        other = lax.rem(self.p + k, self.grid.plane)
        return other, self.device(self.z, other, self.core)

    def in_line(self, k):
        other = lax.rem(self.z + k, self.grid.levels)
        return other, self.device(other, self.p, self.core)

    def barrier(self):
        barrier = pltpu.get_barrier_semaphore()

        def signal(device):
            pl.semaphore_signal(
                barrier, inc=1, device_id=device, device_id_type=pl.DeviceIdType.MESH
            )

        signal(self.sibling())
        each(1, self.grid.plane, lambda k: signal(self.in_plane(k)[1]))
        each(1, self.grid.levels, lambda k: signal(self.in_line(k)[1]))
        pl.semaphore_wait(barrier, self.grid.plane + self.grid.levels - 1)


def send(source, target, sems, device):
    return pltpu.make_async_remote_copy(
        src_ref=source,
        dst_ref=target,
        send_sem=sems[0],
        recv_sem=sems[1],
        device_id=device,
        device_id_type=pl.DeviceIdType.MESH,
    )


class Total:
    def __init__(self, here, mine, total, scratch):
        self.here, self.mine, self.total = here, mine, total
        self.near, self.half, self.a1, self.b1, self.a2, self.b2, self.sa, self.sb = scratch
        grid = here.grid
        self.grid = grid
        self.ca = self.a1.shape[1] // grid.levels
        self.cb = self.b1.shape[1] // grid.plane
        self.rows_a = grid.chips * self.ca
        self.rows = self.half.shape[0]
        self.base = here.core * self.rows

    def rows_at(self, ref, start, count):
        return ref.at[pl.ds(pl.multiple_of(start, 16), count)]

    def sems(self, table, stage, k):
        return table.at[stage, 0, k], table.at[stage, 1, k]

    def plane_copy(self, stage, table, source, target):
        return lambda k: send(
            source(k), target(k), self.sems(table, stage, k), self.here.in_plane(k)[1]
        )

    def line_copy(self, stage, table, source, target):
        return lambda k: send(
            source(k), target(k), self.sems(table, stage, k), self.here.in_line(k)[1]
        )

    def swap(self):
        side = 1 - self.here.core
        return send(
            self.rows_at(self.mine, side * self.rows, self.rows),
            self.near,
            self.sems(self.sa, 0, 0),
            self.here.sibling(),
        )

    def out_copies(self):
        here, ca, cb = self.here, self.grid.levels * self.ca, self.grid.plane * self.cb
        first = self.plane_copy(
            1,
            self.sa,
            lambda k: self.rows_at(self.half, here.in_plane(k)[0] * ca, ca),
            lambda k: self.a1.at[k],
        )
        second = self.line_copy(
            1,
            self.sb,
            lambda k: self.rows_at(self.half, self.rows_a + here.in_line(k)[0] * cb, cb),
            lambda k: self.b1.at[k],
        )
        return first, second

    def in_copies(self):
        here, ca, cb = self.here, self.ca, self.cb
        first = self.line_copy(
            2,
            self.sb,
            lambda k: self.rows_at(self.a1.at[0], here.in_line(k)[0] * ca, ca),
            lambda k: self.rows_at(self.a2.at[0], k * ca, ca),
        )
        second = self.plane_copy(
            2,
            self.sa,
            lambda k: self.rows_at(self.b1.at[0], here.in_plane(k)[0] * cb, cb),
            lambda k: self.rows_at(self.b2.at[0], k * cb, cb),
        )
        return first, second

    def chunk_a(self):
        here = self.here
        return self.base + (here.p * self.grid.levels + here.z) * self.ca

    def chunk_b(self):
        here = self.here
        return self.base + self.rows_a + (here.z * self.grid.plane + here.p) * self.cb

    def back_copies(self):
        a = self.rows_at(self.total, self.chunk_a(), self.ca)
        b = self.rows_at(self.total, self.chunk_b(), self.cb)
        return (
            self.line_copy(3, self.sb, lambda k: a, lambda k: a),
            self.plane_copy(3, self.sa, lambda k: b, lambda k: b),
        )

    def block_a(self, p):
        size = self.grid.levels * self.ca
        return self.rows_at(self.total, self.base + p * size, size)

    def block_b(self, z):
        size = self.grid.plane * self.cb
        return self.rows_at(self.total, self.base + self.rows_a + z * size, size)

    def wide_copies(self):
        a, b = self.block_a(self.here.p), self.block_b(self.here.z)
        return (
            self.plane_copy(4, self.sa, lambda k: a, lambda k: a),
            self.line_copy(4, self.sb, lambda k: b, lambda k: b),
        )

    def last_copy_a(self, k):
        grid = self.grid
        block = self.block_a(lax.rem(self.here.p + grid.plane - k, grid.plane))
        return send(block, block, self.sems(self.sa, 5, k), self.here.sibling())

    def last_copy_b(self, k):
        grid = self.grid
        block = self.block_b(lax.rem(self.here.z + grid.levels - k, grid.levels))
        return send(block, block, self.sems(self.sb, 5, k), self.here.sibling())

    def start(self, copies, counts):
        for copy, count in zip(copies, counts):
            each(1, count, lambda k: copy(k).start())

    def wait(self, copies, counts):
        for copy, count in zip(copies, counts):
            each(1, count, lambda k: copy(k).wait())

    def step0(self):
        self.swap().start()

    def step1(self):
        self.swap().wait()
        size = self.ca + self.cb

        def add(k):
            at = pl.multiple_of(k * size, 16)
            mine_at = pl.multiple_of(self.base + k * size, 16)
            self.half[pl.ds(at, size), :] = (
                self.mine[pl.ds(mine_at, size), :].astype(f32)
                + self.near[pl.ds(at, size), :].astype(f32)
            ).astype(bf16)

        each(0, self.grid.chips, add)
        self.start(self.out_copies(), (self.grid.plane, self.grid.levels))

    def step2(self):
        grid, here = self.grid, self.here
        self.wait(self.out_copies(), (grid.plane, grid.levels))

        def add(slots, own, count, chunk, chunks):
            def body(j):
                rows = pl.ds(pl.multiple_of(j * chunk, 16), chunk)
                total = self.half[
                    pl.ds(pl.multiple_of(own + j * chunk, 16), chunk), :
                ].astype(f32)
                total = lax.fori_loop(
                    1, count, lambda k, acc: acc + slots[k, rows, :].astype(f32), total
                )
                slots[0, rows, :] = total.astype(bf16)

            each(0, chunks, body)

        add(self.a1, here.p * grid.levels * self.ca, grid.plane, self.ca, grid.levels)
        add(self.b1, self.rows_a + here.z * grid.plane * self.cb, grid.levels, self.cb, grid.plane)
        self.start(self.in_copies(), (grid.levels, grid.plane))

    def step3(self):
        grid, here = self.grid, self.here
        self.wait(self.in_copies(), (grid.levels, grid.plane))

        def add(blocks, own, slots, count, chunk, target):
            total = blocks[0, pl.ds(pl.multiple_of(own * chunk, 16), chunk), :].astype(f32)
            total = lax.fori_loop(
                1,
                count,
                lambda k, acc: acc
                + slots[0, pl.ds(pl.multiple_of(k * chunk, 16), chunk), :].astype(f32),
                total,
            )
            self.total[pl.ds(pl.multiple_of(target, 16), chunk), :] = total.astype(bf16)

        add(self.a1, here.z, self.a2, grid.levels, self.ca, self.chunk_a())
        add(self.b1, here.p, self.b2, grid.plane, self.cb, self.chunk_b())
        self.start(self.back_copies(), (grid.levels, grid.plane))

    def step4(self):
        grid = self.grid
        self.wait(self.back_copies(), (grid.levels, grid.plane))
        self.start(self.wide_copies(), (grid.plane, grid.levels))
        self.last_copy_a(0).start()
        self.last_copy_b(0).start()

    def step5(self):
        grid = self.grid
        wide_a, wide_b = self.wide_copies()

        def pass_a(k):
            wide_a(k).wait()
            self.last_copy_a(k).start()

        def pass_b(k):
            wide_b(k).wait()
            self.last_copy_b(k).start()

        each(1, grid.levels, pass_b)
        each(1, grid.plane, pass_a)

    def step6(self):
        each(0, self.grid.plane, lambda k: self.last_copy_a(k).wait())
        each(0, self.grid.levels, lambda k: self.last_copy_b(k).wait())


def reduce_kernel(grid, mine, total, *scratch):
    here = Here(grid)
    here.barrier()
    work = Total(here, mine, total, scratch)
    for step in (work.step0, work.step1, work.step2, work.step3, work.step4, work.step5, work.step6):
        step()


def unpack_kernel(factor, packed, *refs):
    g_gain1, g_bias1, g_qkv, g_lepe, g_lepe_b, g_proj, g_proj_b = refs[:7]
    g_gain2, g_bias2, g_fc1, g_fc1_b, g_fc2, g_fc2_b = refs[7:]
    layers = g_qkv.shape[0]
    at = 0
    for l in range(layers):
        for ref in (g_qkv, g_proj, g_fc1, g_fc2):
            rows, width = ref.shape[1:]
            for lane in range(0, width, GROUP):
                ref[l, :, lane : lane + GROUP] = packed[at : at + rows, :].astype(f32) * factor
                at += rows
    rest = packed[at:, :].astype(f32) * factor
    row = 0
    for l in range(layers):
        for ref in (g_gain1, g_bias1, g_lepe, g_lepe_b, g_proj_b, g_gain2, g_bias2, g_fc1_b, g_fc2_b):
            width = ref.shape[-1]
            for k in range(ref.size // (layers * width)):
                for c in range(0, width, GROUP):
                    value = rest[row : row + 1]
                    if ref.ndim == 3:
                        ref[l, k : k + 1, c : c + GROUP] = value
                    else:
                        ref[l : l + 1, c : c + GROUP] = value
                    row += 1


def compute(packed_rows, tokens, crop_side, cotangent, *weights):
    images, tok, dim = tokens.shape
    qkv_weight, proj_weight, fc1_weight, fc2_weight = (weights[i] for i in (2, 5, 9, 11))
    layers = qkv_weight.shape[0]
    ff = fc1_weight.shape[2]
    block = pl.BlockSpec((1, tok, dim), lambda i: (i, 0, 0))
    whole = pl.BlockSpec(memory_space=pltpu.VMEM)
    return pl.pallas_call(
        kernel,
        grid=(images,),
        out_shape=[
            jax.ShapeDtypeStruct(tokens.shape, bf16),
            jax.ShapeDtypeStruct(tokens.shape, f32),
            jax.ShapeDtypeStruct((packed_rows, GROUP), bf16),
        ],
        in_specs=[pl.BlockSpec(memory_space=pltpu.SMEM), block, block] + [whole] * len(weights),
        out_specs=[block, block, whole],
        scratch_shapes=[
            pltpu.VMEM(qkv_weight.shape, f32),
            pltpu.VMEM(proj_weight.shape, f32),
            pltpu.VMEM(fc1_weight.shape, f32),
            pltpu.VMEM(fc2_weight.shape, f32),
            pltpu.SMEM((BIG_CROPS + SMALL_CROPS,), jnp.int32),
            pltpu.VMEM((dim // GROUP, tok + 16, GROUP), f32),
            pltpu.VMEM((ROWS, dim), f32),
            pltpu.VMEM((ROWS, dim), f32),
            pltpu.VMEM((ROWS, dim), f32),
            pltpu.VMEM((layers, ROWS, dim), f32),
            pltpu.VMEM((layers, ROWS, GROUP), f32),
            pltpu.VMEM((layers, ROWS, dim), bf16),
            pltpu.VMEM((layers, ROWS, dim), bf16),
            pltpu.VMEM((layers, ROWS, dim), bf16),
            pltpu.VMEM((layers, ROWS, dim), bf16),
            pltpu.VMEM((layers, 4 * BIG_CROPS, WIN, 4 * GROUP), bf16),
            pltpu.VMEM((layers, 2 * SMALL_CROPS, SMALL_ROWS, 2 * GROUP), bf16),
            pltpu.VMEM((layers, ROWS, dim), f32),
            pltpu.VMEM((layers, ROWS, dim), f32),
            pltpu.VMEM((layers, ROWS, dim), bf16),
            pltpu.VMEM((layers, ROWS, dim), f32),
            pltpu.VMEM((layers, ROWS, GROUP), f32),
            pltpu.VMEM((layers, ROWS, dim), bf16),
            pltpu.VMEM((layers, ROWS, ff), bf16),
            pltpu.VMEM((layers, ROWS, ff), bf16),
            pltpu.VMEM((ROWS, ff), bf16),
            pltpu.VMEM((ROWS, dim), f32),
            pltpu.VMEM((ROWS, 3 * dim), bf16),
            pltpu.VMEM((4, WIN + 48, GROUP), f32),
            pltpu.VMEM((12, SMALL_ROWS + 32, GROUP), f32),
            pltpu.VMEM((4 * GROUP, GROUP), bf16),
            pltpu.VMEM((4 * 64, GROUP), bf16),
            pltpu.VMEM((layers, 8, ff), f32),
            pltpu.VMEM((layers, 8, dim), f32),
            pltpu.VMEM((layers, 8, dim), f32),
            pltpu.VMEM((layers, 9, 8, dim), f32),
            pltpu.VMEM((layers, 8, dim), f32),
            pltpu.VMEM((layers, 8, dim), f32),
            pltpu.VMEM((layers, 8, dim), f32),
            pltpu.VMEM((layers, 8, dim), f32),
            pltpu.VMEM((layers, 8, ff), f32),
            pltpu.VMEM((layers, 8, dim), f32),
        ],
        compiler_params=pltpu.CompilerParams(
            dimension_semantics=("arbitrary",), vmem_limit_bytes=62 * 1024 * 1024
        ),
    )(crop_side, tokens, cotangent, *weights)


def local(
    tokens,
    crop_side,
    cotangent,
    ln1_gain,
    ln1_bias,
    qkv_weight,
    lepe_weight,
    lepe_bias,
    proj_weight,
    proj_bias,
    ln2_gain,
    ln2_bias,
    fc1_weight,
    fc1_bias,
    fc2_weight,
    fc2_bias,
):
    images, tok = tokens.shape[:2]
    weights = (
        ln1_gain,
        ln1_bias,
        qkv_weight,
        lepe_weight,
        lepe_bias,
        proj_weight,
        proj_bias,
        ln2_gain,
        ln2_bias,
        fc1_weight,
        fc1_bias,
        fc2_weight,
        fc2_bias,
    )
    whole = pl.BlockSpec(memory_space=pltpu.VMEM)
    devices = lax.axis_size("dp") * lax.axis_size("head")
    grid = Grid(lax.axis_size("dp"), lax.axis_size("head"))
    grad_rows = sum(math.prod(w.shape) for w in weights) // GROUP
    packed_rows = grid.packed_rows(grad_rows)
    out, input_grad, packed = compute(packed_rows, tokens, crop_side, cotangent, *weights)
    total = pl.pallas_call(
        partial(reduce_kernel, grid),
        out_shape=jax.ShapeDtypeStruct((packed_rows, GROUP), bf16),
        in_specs=[whole],
        out_specs=whole,
        scratch_shapes=grid.scratch(grad_rows),
        compiler_params=pltpu.CompilerParams(
            collective_id=0, has_side_effects=True, vmem_limit_bytes=32 * 1024 * 1024
        ),
    )(packed)
    factor = 1.0 / math.sqrt(devices * images * tok)
    grads = pl.pallas_call(
        partial(unpack_kernel, factor),
        out_shape=[jax.ShapeDtypeStruct(w.shape, f32) for w in weights],
        in_specs=[whole],
        out_specs=[whole] * len(weights),
        compiler_params=pltpu.CompilerParams(vmem_limit_bytes=32 * 1024 * 1024),
    )(total)
    return (out, input_grad) + tuple(grads)


def solution(mesh):
    sharded = P(("dp", "head"), None, None)
    return jax.shard_map(
        local,
        mesh=mesh,
        in_specs=(sharded, P(("dp", "head"), None), sharded) + (P(),) * 13,
        out_specs=(sharded, sharded) + (P(),) * 13,
        check_vma=False,
    )
```

```python
from functools import partial
import math

import jax
import jax.numpy as jnp
import numpy as np
from jax import lax
from jax.experimental import pallas as pl
from jax.experimental.pallas import tpu as pltpu
from jax.sharding import PartitionSpec as P

HEADS_GROUP = 4
HEAD_DIM = 32
SW = 7
BIG = 14
SMALL = 6
BIG_CROPS = 2
SMALL_CROPS = 6
GROUP = 128
EPSILON = 1e-05

BIG_ROWS = BIG * 16
WIN = SW * 16
SMALL_ROWS = SMALL * 8
SMALL_BASE = BIG_CROPS * BIG_ROWS
ROWS = SMALL_BASE + SMALL_CROPS * SMALL_ROWS
CHUNK = ROWS // 2

SCALE = HEAD_DIM**-0.5
LOG2E = math.log2(math.e)
NEG = -1e30

PLANE_FIRST = 0.67
VMEM_LIMIT = 63 * 1024 * 1024
FWD_SMALL = 3
BWD_SMALL = 3
LAST_STEPS = (2, 0, 2, 1, 0, 2, 1, 0, 2, 1, 0, 2, 1, 2, 0, 1, 2)

bf16 = jnp.bfloat16
f32 = jnp.float32

NN = (((1,), (0,)), ((), ()))
NT = (((1,), (1,)), ((), ()))
TN = (((0,), (0,)), ((), ()))


def mm(a, b, dims=NN):
    return lax.dot_general(a, b, dims, preferred_element_type=f32)


def iota(shape, dim):
    return lax.broadcasted_iota(jnp.int32, shape, dim)


def to_vertical(x):
    x4 = x.reshape(BIG, 2, 8, x.shape[1])
    return jnp.concatenate([x4[:, 0].reshape(WIN, -1), x4[:, 1].reshape(WIN, -1)], axis=0)


def from_vertical(y):
    y4 = y.reshape(2, BIG, 8, y.shape[1])
    return jnp.stack([y4[0], y4[1]], axis=1).reshape(BIG_ROWS, -1)


def real_big():
    sub = iota((BIG_ROWS, GROUP), 0) % 16
    return ((sub != 0) & (sub != 15)).astype(f32)


def real_small(rows):
    return ((iota((rows, GROUP), 0) % 8) < SMALL).astype(f32)


def lockstep(streams):
    streams = list(streams)
    while streams:
        left = []
        for stream in streams:
            try:
                next(stream)
                left.append(stream)
            except StopIteration:
                pass
        streams = left


def partial_rows(x):
    return jnp.sum(x.reshape(x.shape[0] // 8, 8, x.shape[1]), axis=0)


def head_mask(h):
    lane = iota((1, GROUP), 1)
    return ((lane >= h * HEAD_DIM) & (lane < (h + 1) * HEAD_DIM)).astype(f32)


def block_heads(x, keys):
    rows = x.shape[0]
    parts = []
    for h in range(HEADS_GROUP):
        part = x * head_mask(h).astype(x.dtype)
        parts.append(part)
        if keys > rows:
            parts.append(jnp.zeros((keys - rows, GROUP), x.dtype))
    return jnp.concatenate(parts, axis=0)


def ones_heads(keys):
    row_head = iota((HEADS_GROUP * keys, GROUP), 0) // keys
    lane_head = iota((HEADS_GROUP * keys, GROUP), 1) // HEAD_DIM
    return (row_head == lane_head).astype(f32).astype(bf16)


def sum_heads(x, keys, rows):
    total = None
    for h in range(HEADS_GROUP):
        part = x[h * keys : h * keys + rows] * head_mask(h)
        total = part if total is None else total + part
    return total


def keeps():
    sub = iota((8, GROUP), 0)
    return [(part).astype(f32) for part in (sub != 0, sub != 7, sub < SMALL)]


def ingest(stage, starts, source, target):
    keep_lo, keep_hi, keep_small = keeps()
    tok = source.shape[1]
    halves = source.shape[2] // GROUP
    for half in range(halves):
        stage[half, 8 : 8 + tok, :] = source[0, :, half * GROUP : (half + 1) * GROUP].astype(f32)
    for c in range(BIG_CROPS):
        yield
        start = starts[c] + 7
        for r in range(BIG):
            for half in range(halves):
                lanes = slice(half * GROUP, (half + 1) * GROUP)
                base = c * BIG_ROWS + r * 16
                lo = stage[half, pl.ds(start + r * BIG, 8), :]
                hi = stage[half, pl.ds(start + r * BIG + 8, 8), :]
                target[base : base + 8, lanes] = lo * keep_lo
                target[base + 8 : base + 16, lanes] = hi * keep_hi
    for c in range(SMALL_CROPS):
        if c % 3 == 0:
            yield
        start = starts[BIG_CROPS + c] + 8
        for r in range(SMALL):
            for half in range(halves):
                lanes = slice(half * GROUP, (half + 1) * GROUP)
                base = SMALL_BASE + c * SMALL_ROWS + r * 8
                lo = stage[half, pl.ds(start + r * SMALL, 8), :]
                target[base : base + 8, lanes] = lo * keep_small

def put(stage, half, at, value, keep):
    old = stage[half, pl.ds(at, 8), :]
    stage[half, pl.ds(at, 8), :] = jnp.where(keep > 0, value, old)

def emit(stage, starts, source, target):
    keep_lo, keep_hi, keep_small = keeps()
    tok = target.shape[1]
    halves = target.shape[2] // GROUP
    for c in range(BIG_CROPS):
        yield
        start = starts[c] + 7
        for r in range(BIG):
            for half in range(halves):
                lanes = slice(half * GROUP, (half + 1) * GROUP)
                base = c * BIG_ROWS + r * 16
                put(stage, half, start + r * BIG, source[base : base + 8, lanes].astype(f32), keep_lo)
                put(stage, half, start + r * BIG + 8, source[base + 8 : base + 16, lanes].astype(f32), keep_hi)
    for c in range(SMALL_CROPS):
        if c % 3 == 0:
            yield
        start = starts[BIG_CROPS + c] + 8
        for r in range(SMALL):
            for half in range(halves):
                lanes = slice(half * GROUP, (half + 1) * GROUP)
                base = SMALL_BASE + c * SMALL_ROWS + r * 8
                put(stage, half, start + r * SMALL, source[base : base + 8, lanes].astype(f32), keep_small)
    for half in range(halves):
        target[0, :, half * GROUP : (half + 1) * GROUP] = stage[half, 8 : 8 + tok, :].astype(
            target.dtype
        )


def place_crops(crop_side, image):
    start, n_big, n_small = jnp.int32(0), jnp.int32(0), jnp.int32(0)
    starts = [jnp.int32(0)] * (BIG_CROPS + SMALL_CROPS)
    for j in range(crop_side.shape[1]):
        side = crop_side[image, j]
        is_big = side == BIG
        slot = jnp.where(is_big, n_big, BIG_CROPS + n_small)
        for i in range(len(starts)):
            starts[i] = jnp.where(slot == i, start, starts[i])
        big_add = jnp.where(is_big, 1, 0)
        start, n_big, n_small = start + side * side, n_big + big_add, n_small + 1 - big_add
    return starts


class Env:
    def __init__(self, **refs):
        self.__dict__.update(refs)


STATE = ("n1", "r1", "a", "q", "k", "v", "eb", "es", "oat", "rdn")
STATE_FEED = ("o", "n2", "r2", "m", "g", "gp")


def state_shapes(dim, ff):
    wide = (ROWS, dim)
    shapes = dict.fromkeys(STATE + STATE_FEED, (wide, bf16))
    shapes["r1"] = shapes["r2"] = ((ROWS, GROUP), f32)
    shapes["g"] = shapes["gp"] = ((ROWS, ff), bf16)
    shapes["eb"] = ((4 * BIG_CROPS, WIN, HEADS_GROUP * GROUP), bf16)
    shapes["es"] = ((2 * SMALL_CROPS, SMALL_ROWS, HEADS_GROUP * 64), bf16)
    return shapes


GRADS = ("qkv", "proj", "fc1", "fc2")
ACCS = ("gain1", "bias1", "lepe", "lepe_b", "proj_b", "gain2", "bias2", "fc1_b", "fc2_b")


def acc_scratch(dim, ff):
    shapes = dict.fromkeys(ACCS, (8, dim))
    shapes["lepe"] = (9, 8, dim)
    shapes["fc1_b"] = (8, ff)
    return [pltpu.VMEM(shapes[name], f32) for name in ACCS]


def grad_scratch(dim, ff):
    shapes = ((dim, 3 * dim), (dim, dim), (dim, ff), (ff, dim))
    return [pltpu.VMEM(shape, f32) for shape in shapes]


def shared_scratch(dim):
    return [
        pltpu.VMEM((ROWS, dim), bf16),
        pltpu.VMEM((ROWS, 3 * dim), bf16),
        pltpu.VMEM((4 * BIG_CROPS, WIN + 48, GROUP), f32),
        pltpu.VMEM((2 * SMALL_CROPS, SMALL_ROWS + 32, GROUP), f32),
        pltpu.VMEM((4 * GROUP, GROUP), bf16),
        pltpu.VMEM((4 * 64, GROUP), bf16),
    ]


def clear(env, l):
    for ref in [getattr(env.grad[l], name) for name in GRADS] + [
        getattr(env.acc[l], name) for name in ACCS
    ]:
        ref[...] = jnp.zeros(ref.shape, f32)
    env.lepb[...] = jnp.zeros(env.lepb.shape, f32)
    env.leps[...] = jnp.zeros(env.leps.shape, f32)
    env.onesb[...] = ones_heads(GROUP)
    env.oness[...] = ones_heads(64)


def fill(packed, refs, accs):
    at = 0
    for ref in refs:
        rows, width = ref.shape
        for lane in range(0, width, GROUP):
            packed[at : at + rows, :] = ref[:, lane : lane + GROUP].astype(bf16)
            at += rows
    parts = [small_rows(acc) for acc in accs or ()]
    rest = packed.shape[0] - at - sum(part.shape[0] for part in parts)
    if rest:
        parts.append(jnp.zeros((rest, GROUP), f32))
    if parts:
        packed[at:, :] = jnp.concatenate(parts, axis=0).astype(bf16)


def small_rows(acc):
    parts = []
    for name in ACCS:
        value = getattr(acc, name)[...]
        for k in range(value.size // (8 * value.shape[-1])):
            row = jnp.sum(value[k] if value.ndim == 3 else value, axis=0, keepdims=True)
            parts += [row[:, c : c + GROUP] for c in range(0, row.shape[1], GROUP)]
    return jnp.concatenate(parts, axis=0)


def stages(env):
    dim, ff = env.dim, env.ff
    halves = dim // GROUP

    def norm_stats(x):
        center = x - jnp.mean(x, axis=1, keepdims=True)
        r = lax.rsqrt(jnp.mean(center * center, axis=1, keepdims=True) + EPSILON)
        return center * r, r

    def project(l, base, rows, big):
        rows_at = pl.ds(base, rows)
        n, r = norm_stats(env.x[rows_at, :])
        env.state[l].n1[rows_at, :] = n.astype(bf16)
        env.state[l].r1[rows_at, :] = jnp.broadcast_to(r, (rows, GROUP))
        yield
        a = (n * env.vec[l, 0:1, :dim] + env.vec[l, 1:2, :dim]).astype(bf16)
        env.state[l].a[rows_at, :] = a
        qkv = mm(a, env.qkv_w[l])
        yield
        real = real_big() if big else real_small(rows)
        for grp in range(2):
            cols = [slice(s * dim + grp * GROUP, s * dim + (grp + 1) * GROUP) for s in range(3)]
            q = qkv[:, cols[0]] * (SCALE * LOG2E)
            k = qkv[:, cols[1]]
            v = qkv[:, cols[2]] * real
            if big and grp == 1:
                q, k, v = to_vertical(q), to_vertical(k), to_vertical(v)
            lanes = slice(grp * GROUP, (grp + 1) * GROUP)
            env.state[l].q[rows_at, lanes] = q.astype(bf16)
            env.state[l].k[rows_at, lanes] = k.astype(bf16)
            env.state[l].v[rows_at, lanes] = v.astype(bf16)

    def pad_row(grp, w):
        u = iota((1, HEADS_GROUP * GROUP), 1) % GROUP
        if grp == 0:
            bad = (u % 16 == 0) | (u % 16 == 15)
        elif w == 0:
            bad = u % 8 == 0
        else:
            bad = u % 8 == 7
        return jnp.where(bad | (u >= WIN), NEG, 0.0).astype(f32)

    def pad_row_small():
        u = iota((1, HEADS_GROUP * 64), 1) % 64
        return jnp.where((u % 8 >= SMALL) | (u >= SMALL_ROWS), NEG, 0.0).astype(f32)

    def shifted(buf, idx, margin, stride, rows):
        return [buf[idx, pl.ds(margin - stride + b, rows + 2 * stride), :] for b in (-1, 0, 1)]

    def conv(views, stride, rows, weights, flip):
        total = None
        for a in range(3):
            for b in range(3):
                k = 3 * a + b
                wk = weights[8 - k : 9 - k] if flip else weights[k : k + 1]
                term = views[b][a * stride : a * stride + rows] * wk
                total = term if total is None else total + term
        return total

    def windows_big(c):
        for grp in range(2):
            for w in range(2):
                yield grp, w, c * BIG_ROWS + w * WIN

    def attend_big(l, c):
        items = list(windows_big(c))
        scores = []
        for grp, w, base in items:
            lanes = slice(grp * GROUP, (grp + 1) * GROUP)
            q = env.state[l].q[pl.ds(base, WIN), lanes]
            kb = block_heads(env.state[l].k[pl.ds(base, WIN), lanes], GROUP)
            scores.append(mm(q, kb, NT) + pad_row(grp, w))
        yield
        for i, (grp, w, base) in enumerate(items):
            parts = []
            for h in range(HEADS_GROUP):
                s = scores[i][:, h * GROUP : (h + 1) * GROUP]
                parts.append(jnp.exp2(s - jnp.max(s, axis=1, keepdims=True)).astype(bf16))
            env.state[l].eb[4 * c + 2 * grp + w] = jnp.concatenate(parts, axis=1)
        yield
        outs = []
        for i, (grp, w, base) in enumerate(items):
            lanes = slice(grp * GROUP, (grp + 1) * GROUP)
            v = env.state[l].v[pl.ds(base, WIN), lanes]
            vo = jnp.concatenate([block_heads(v, GROUP), env.onesb[...]], axis=1)
            both = mm(env.state[l].eb[4 * c + 2 * grp + w], vo)
            rden = 1.0 / both[:, GROUP:]
            oat = both[:, :GROUP] * rden
            env.state[l].rdn[pl.ds(base, WIN), lanes] = rden.astype(bf16)
            env.state[l].oat[pl.ds(base, WIN), lanes] = oat.astype(bf16)
            stride = 16 if grp == 0 else 8
            env.lepb[4 * c + i, pl.ds(24, WIN), :] = v.astype(f32)
            views = shifted(env.lepb, 4 * c + i, 24, stride, WIN)
            near = conv(views, stride, WIN, env.lepe_w[l, :, lanes], False)
            outs.append(oat + near + env.vec[l, 2:3, lanes])
            if w == 1:
                yield
        rows_at = pl.ds(c * BIG_ROWS, BIG_ROWS)
        env.state[l].o[rows_at, :GROUP] = jnp.concatenate(outs[:2], axis=0).astype(bf16)
        env.state[l].o[rows_at, GROUP:] = from_vertical(jnp.concatenate(outs[2:], axis=0)).astype(bf16)

    def attend_small(l, c0, count):
        items = [
            (grp, c0 + c, SMALL_BASE + (c0 + c) * SMALL_ROWS, 2 * (c0 + c) + grp)
            for c in range(count)
            for grp in range(2)
        ]
        low = iota((SMALL_ROWS, GROUP), 1) < 64
        scores = []
        for grp, c, base, i in items:
            lanes = slice(grp * GROUP, (grp + 1) * GROUP)
            q = env.state[l].q[pl.ds(base, SMALL_ROWS), lanes]
            kb = block_heads(env.state[l].k[pl.ds(base, SMALL_ROWS), lanes], 64)
            scores.append(mm(q, kb, NT) + pad_row_small())
        yield
        for j, (grp, c, base, i) in enumerate(items):
            parts = []
            for t in range(2):
                s = scores[j][:, t * GROUP : (t + 1) * GROUP]
                top_lo = jnp.max(jnp.where(low, s, 2 * NEG), axis=1, keepdims=True)
                top_hi = jnp.max(jnp.where(low, 2 * NEG, s), axis=1, keepdims=True)
                parts.append(jnp.exp2(s - jnp.where(low, top_lo, top_hi)).astype(bf16))
            env.state[l].es[2 * c + grp] = jnp.concatenate(parts, axis=1)
        yield
        for grp, c, base, i in items:
            lanes = slice(grp * GROUP, (grp + 1) * GROUP)
            v = env.state[l].v[pl.ds(base, SMALL_ROWS), lanes]
            vo = jnp.concatenate([block_heads(v, 64), env.oness[...]], axis=1)
            both = mm(env.state[l].es[2 * c + grp], vo)
            rden = 1.0 / both[:, GROUP:]
            oat = both[:, :GROUP] * rden
            env.state[l].rdn[pl.ds(base, SMALL_ROWS), lanes] = rden.astype(bf16)
            env.state[l].oat[pl.ds(base, SMALL_ROWS), lanes] = oat.astype(bf16)
            env.leps[i, pl.ds(16, SMALL_ROWS), :] = v.astype(f32)
            views = shifted(env.leps, i, 16, 8, SMALL_ROWS)
            near = conv(views, 8, SMALL_ROWS, env.lepe_w[l, :, lanes], False)
            env.state[l].o[pl.ds(base, SMALL_ROWS), lanes] = (oat + near + env.vec[l, 2:3, lanes]).astype(
                bf16
            )

    def feed(l, base):
        rows_at = pl.ds(base, CHUNK)
        mid = env.x[rows_at, :] + mm(env.state[l].o[rows_at, :], env.proj_w[l]) + env.vec[l, 3:4, :dim]
        yield
        n, r = norm_stats(mid)
        env.state[l].n2[rows_at, :] = n.astype(bf16)
        env.state[l].r2[rows_at, :] = jnp.broadcast_to(r, (CHUNK, GROUP))
        m = (n * env.vec[l, 4:5, :dim] + env.vec[l, 5:6, :dim]).astype(bf16)
        env.state[l].m[rows_at, :] = m
        yield
        step = 256
        for j in range(ff // step):
            cols = slice(j * step, (j + 1) * step)
            f = mm(m, env.fc1_w[l, :, cols]) + env.vec[l, 6:7, cols]
            phi = 0.5 * lax.erf(f * np.float32(math.sqrt(0.5))) + 0.5
            dens = jnp.exp2(f * f * np.float32(-0.5 * LOG2E)) * np.float32(
                1.0 / math.sqrt(2.0 * math.pi)
            )
            env.state[l].g[rows_at, cols] = (f * phi).astype(bf16)
            env.state[l].gp[rows_at, cols] = (phi + f * dens).astype(bf16)
            yield
        env.x[rows_at, :] = mid + env.vec[l, 7:8, :dim] + mm(env.state[l].g[rows_at, :], env.fc2_w[l])

    def norm_back(dm, n, r, gain):
        dn = dm * gain
        mean_one = jnp.mean(dn, axis=1, keepdims=True)
        mean_two = jnp.mean(dn * n, axis=1, keepdims=True)
        rb = jnp.concatenate([r] * halves, axis=1)
        return rb * (dn - mean_one - n * mean_two)

    def feed_back(l, base):
        rows_at = pl.ds(base, CHUNK)
        e = env.e[rows_at, :]
        dz = e.astype(bf16)
        env.dz[rows_at, :] = dz
        env.acc[l].fc2_b[...] += partial_rows(dz.astype(f32))
        yield
        step = 256
        for j in range(ff // step):
            cols = slice(j * step, (j + 1) * step)
            df = mm(dz, env.fc2_w[l, cols, :], NT) * env.state[l].gp[rows_at, cols].astype(f32)
            env.state[l].gp[rows_at, cols] = df.astype(bf16)
            env.acc[l].fc1_b[:, cols] += partial_rows(df)
            yield
        dm = mm(env.state[l].gp[rows_at, :], env.fc1_w[l], NT)
        yield
        n = env.state[l].n2[rows_at, :].astype(f32)
        env.acc[l].gain2[...] += partial_rows(dm * n)
        env.acc[l].bias2[...] += partial_rows(dm)
        dmid = e + norm_back(dm, n, env.state[l].r2[rows_at, :], env.vec[l, 4:5, :dim])
        env.mid[rows_at, :] = dmid
        yield
        dy = dmid.astype(bf16)
        env.acc[l].proj_b[...] += partial_rows(dy.astype(f32))
        env.do[rows_at, :] = mm(dy, env.proj_w[l], NT).astype(bf16).astype(f32)

    def lepe_back(l, buf, idx, margin, stride, rows, lanes, v):
        views = [buf[idx, pl.ds(margin - stride + b, rows + 2 * stride), :] for b in (-1, 0, 1)]
        vf = v.astype(f32)
        for k in range(9):
            a, b = divmod(8 - k, 3)
            env.acc[l].lepe[k, :, lanes] += partial_rows(views[b][a * stride : a * stride + rows] * vf)
        env.acc[l].lepe_b[:, lanes] += partial_rows(views[1][stride : stride + rows])
        return conv(views, stride, rows, env.lepe_w[l, :, lanes], True)

    def attend_back(l, group_items, rows, keys, buf, margin, strides, e_ref, ones, unit):
        grads = []
        kbs = []
        ds_all = []
        dop_all = []
        for grp, base, e_at, lep_at, do in group_items:
            lanes = slice(grp * GROUP, (grp + 1) * GROUP)
            rows_at = pl.ds(base, rows)
            buf[lep_at, pl.ds(margin, rows), :] = do
            dop = do * env.state[l].rdn[rows_at, lanes].astype(f32)
            tail = -(dop * env.state[l].oat[rows_at, lanes].astype(f32))
            dop_all.append(dop.astype(bf16))
            left = jnp.concatenate([dop.astype(bf16), tail.astype(bf16)], axis=1)
            vo = jnp.concatenate([block_heads(env.state[l].v[rows_at, lanes], keys), ones[...]], axis=1)
            x = mm(left, vo, NT)
            ds_all.append((e_ref[e_at].astype(f32) * x).astype(bf16))
        yield
        for i, (grp, base, e_at, lep_at, do) in enumerate(group_items):
            lanes = slice(grp * GROUP, (grp + 1) * GROUP)
            kb = block_heads(env.state[l].k[pl.ds(base, rows), lanes], keys)
            grads.append([mm(ds_all[i], kb) * SCALE])
        yield
        zero_block = jnp.zeros((rows, GROUP), bf16)
        for i in range(0, len(group_items), 2):
            pair = group_items[i : i + 2]

            def spread(first, second):
                return jnp.concatenate(
                    [
                        jnp.concatenate([first, zero_block], axis=1),
                        jnp.concatenate([zero_block, second], axis=1),
                    ],
                    axis=0,
                )

            qs = [env.state[l].q[pl.ds(it[1], rows), it[0] * GROUP : (it[0] + 1) * GROUP] for it in pair]
            dk = mm(jnp.concatenate(ds_all[i : i + 2], axis=0), spread(*qs), TN)
            es = jnp.concatenate([e_ref[it[2]] for it in pair], axis=0)
            dv = mm(es, spread(*dop_all[i : i + 2]), TN)
            for j, (grp, base, e_at, lep_at, do) in enumerate(pair):
                lanes = slice(grp * GROUP, (grp + 1) * GROUP)
                cols = slice(j * GROUP, (j + 1) * GROUP)
                near = lepe_back(
                    l, buf, lep_at, margin, strides[grp], rows, lanes, env.state[l].v[pl.ds(base, rows), lanes]
                )
                grads[i + j].append(sum_heads(dk[:, cols], keys, rows) * (1.0 / LOG2E))
                grads[i + j].append(sum_heads(dv[:, cols], keys, rows) + near)
            yield
        return grads

    def attend_back_big(l, c):
        rows_at = pl.ds(c * BIG_ROWS, BIG_ROWS)
        do_h = env.do[rows_at, :GROUP]
        do_v = to_vertical(env.do[rows_at, GROUP:])
        items = []
        for i, (grp, w, base) in enumerate(windows_big(c)):
            do = (do_h if grp == 0 else do_v)[w * WIN : (w + 1) * WIN]
            items.append((grp, base, 4 * c + 2 * grp + w, 4 * c + i, do))
        grads = yield from attend_back(l, items, WIN, GROUP, env.lepb, 24, (16, 8), env.state[l].eb, env.onesb, None)
        real = real_big()
        for s in range(3):
            left = jnp.concatenate([grads[0][s], grads[1][s]], axis=0)
            right = from_vertical(jnp.concatenate([grads[2][s], grads[3][s]], axis=0))
            if s == 2:
                left, right = left * real, right * real
            env.dqkv[rows_at, s * dim : s * dim + GROUP] = left.astype(bf16)
            env.dqkv[rows_at, s * dim + GROUP : (s + 1) * dim] = right.astype(bf16)

    def attend_back_small(l, c0, count):
        items = []
        for grp in range(2):
            for c in range(count):
                base = SMALL_BASE + (c0 + c) * SMALL_ROWS
                do = env.do[pl.ds(base, SMALL_ROWS), grp * GROUP : (grp + 1) * GROUP]
                items.append((grp, base, 2 * (c0 + c) + grp, 2 * (c0 + c) + grp, do))
        grads = yield from attend_back(l, items, SMALL_ROWS, 64, env.leps, 16, (8, 8), env.state[l].es, env.oness, None)
        real = real_small(SMALL_ROWS)
        for (grp, base, e_at, lep_at, do), grad in zip(items, grads):
            for s in range(3):
                value = grad[s] * real if s == 2 else grad[s]
                at = s * dim + grp * GROUP
                env.dqkv[pl.ds(base, SMALL_ROWS), at : at + GROUP] = value.astype(bf16)

    def project_back(l, base):
        rows_at = pl.ds(base, CHUNK)
        da = mm(env.dqkv[rows_at, :], env.qkv_w[l], NT)
        yield
        n = env.state[l].n1[rows_at, :].astype(f32)
        env.acc[l].gain1[...] += partial_rows(da * n)
        env.acc[l].bias1[...] += partial_rows(da)
        env.e_out[rows_at, :] = env.mid[rows_at, :] + norm_back(
            da, n, env.state[l].r1[rows_at, :], env.vec[l, 0:1, :dim]
        )

    def feed_grads(l):
        dz = env.dz[...]
        for j in range(0, ff, 256):
            cols = slice(j, j + 256)
            env.grad[l].fc2[cols, :] += mm(env.state[l].g[:, cols], dz, TN)
            yield
            env.grad[l].fc1[:, cols] += mm(env.state[l].m[...], env.state[l].gp[:, cols], TN)
            yield
        env.grad[l].proj[...] += mm(env.state[l].o[...], env.mid[...].astype(bf16), TN)

    def qkv_grads(l):
        for j in range(0, 3 * dim, 256):
            cols = slice(j, j + 256)
            env.grad[l].qkv[:, cols] += mm(env.state[l].a[...], env.dqkv[:, cols], TN)
            yield

    return Env(
        project=project,
        attend_big=attend_big,
        attend_small=attend_small,
        feed=feed,
        feed_back=feed_back,
        feed_grads=feed_grads,
        attend_back_big=attend_back_big,
        attend_back_small=attend_back_small,
        project_back=project_back,
        qkv_grads=qkv_grads,
    )


class Grid:
    def __init__(self, dp, heads):
        chips = dp // 2
        self.heads = heads
        self.levels = next(n for n in (4, 2, 1) if chips % n == 0)
        self.low = chips // self.levels
        self.plane = self.low * heads
        self.chips = chips * heads

    def split(self, rows):
        units = max(2, -(-rows // (2 * 16 * self.chips)))
        first = min(units - 1, max(1, round(PLANE_FIRST * units)))
        return 16 * first, 16 * (units - first)

    def packed_rows(self, rows):
        return 2 * self.chips * sum(self.split(rows))

    def scratch(self, rows):
        ca, cb = self.split(rows)
        half = self.chips * (ca + cb)
        return [
            pltpu.VMEM((half, GROUP), bf16),
            pltpu.VMEM((half, GROUP), bf16),
            pltpu.VMEM((self.plane, self.levels * ca, GROUP), bf16),
            pltpu.VMEM((self.levels, self.plane * cb, GROUP), bf16),
            pltpu.VMEM((1, self.levels * ca, GROUP), bf16),
            pltpu.VMEM((1, self.plane * cb, GROUP), bf16),
            pltpu.SemaphoreType.DMA((6, 2, self.plane)),
            pltpu.SemaphoreType.DMA((6, 2, self.levels)),
            pltpu.SemaphoreType.REGULAR,
        ]


def each(first, last, body):
    def step(k, carry):
        body(k)
        return carry

    lax.fori_loop(first, last, step, 0)


class Here:
    def __init__(self, grid):
        self.grid = grid
        dp = lax.axis_index("dp")
        self.core = lax.rem(dp, 2)
        chip = dp // 2
        self.z = chip // grid.low
        self.p = lax.rem(chip, grid.low) * grid.heads + lax.axis_index("head")

    def device(self, z, p, core):
        low = p // self.grid.heads
        return (2 * (z * self.grid.low + low) + core, lax.rem(p, self.grid.heads))

    def sibling(self):
        return self.device(self.z, self.p, 1 - self.core)

    def in_plane(self, k):
        other = lax.rem(self.p + k, self.grid.plane)
        return other, self.device(self.z, other, self.core)

    def in_line(self, k):
        other = lax.rem(self.z + k, self.grid.levels)
        return other, self.device(other, self.p, self.core)

    def greet(self):
        barrier = pltpu.get_barrier_semaphore()

        def signal(device):
            pl.semaphore_signal(
                barrier, inc=1, device_id=device, device_id_type=pl.DeviceIdType.MESH
            )

        signal(self.sibling())
        each(1, self.grid.plane, lambda k: signal(self.in_plane(k)[1]))
        each(1, self.grid.levels, lambda k: signal(self.in_line(k)[1]))

    def wait(self):
        pl.semaphore_wait(
            pltpu.get_barrier_semaphore(), self.grid.plane + self.grid.levels - 1
        )


def send(source, target, sems, device):
    return pltpu.make_async_remote_copy(
        src_ref=source,
        dst_ref=target,
        send_sem=sems[0],
        recv_sem=sems[1],
        device_id=device,
        device_id_type=pl.DeviceIdType.MESH,
    )


class Total:
    def __init__(self, here, mine, total, scratch):
        self.here, self.mine, self.total = here, mine, total
        self.near, self.half, self.a1, self.b1, self.a2, self.b2 = scratch[:6]
        self.sa, self.sb, self.free = scratch[6:]
        grid = here.grid
        self.grid = grid
        self.ca = self.a1.shape[1] // grid.levels
        self.cb = self.b1.shape[1] // grid.plane
        self.rows_a = grid.chips * self.ca
        self.rows = self.half.shape[0]
        self.base = here.core * self.rows

    def rows_at(self, ref, start, count):
        return ref.at[pl.ds(pl.multiple_of(start, 16), count)]

    def sems(self, table, stage, k):
        return table.at[stage, 0, k], table.at[stage, 1, k]

    def plane_copy(self, stage, table, source, target):
        return lambda k: send(
            source(k), target(k), self.sems(table, stage, k), self.here.in_plane(k)[1]
        )

    def line_copy(self, stage, table, source, target):
        return lambda k: send(
            source(k), target(k), self.sems(table, stage, k), self.here.in_line(k)[1]
        )

    def swap(self):
        side = 1 - self.here.core
        return send(
            self.rows_at(self.mine, side * self.rows, self.rows),
            self.near,
            self.sems(self.sa, 0, 0),
            self.here.sibling(),
        )

    def out_copies(self):
        here, ca, cb = self.here, self.grid.levels * self.ca, self.grid.plane * self.cb
        first = self.plane_copy(
            1,
            self.sa,
            lambda k: self.rows_at(self.half, here.in_plane(k)[0] * ca, ca),
            lambda k: self.a1.at[k],
        )
        second = self.line_copy(
            1,
            self.sb,
            lambda k: self.rows_at(self.half, self.rows_a + here.in_line(k)[0] * cb, cb),
            lambda k: self.b1.at[k],
        )
        return first, second

    def in_copies(self):
        here, ca, cb = self.here, self.ca, self.cb
        first = self.line_copy(
            2,
            self.sb,
            lambda k: self.rows_at(self.a1.at[0], here.in_line(k)[0] * ca, ca),
            lambda k: self.rows_at(self.a2.at[0], k * ca, ca),
        )
        second = self.plane_copy(
            2,
            self.sa,
            lambda k: self.rows_at(self.b1.at[0], here.in_plane(k)[0] * cb, cb),
            lambda k: self.rows_at(self.b2.at[0], k * cb, cb),
        )
        return first, second

    def chunk_a(self):
        here = self.here
        return self.base + (here.p * self.grid.levels + here.z) * self.ca

    def chunk_b(self):
        here = self.here
        return self.base + self.rows_a + (here.z * self.grid.plane + here.p) * self.cb

    def back_copies(self):
        a = self.rows_at(self.total, self.chunk_a(), self.ca)
        b = self.rows_at(self.total, self.chunk_b(), self.cb)
        return (
            self.line_copy(3, self.sb, lambda k: a, lambda k: a),
            self.plane_copy(3, self.sa, lambda k: b, lambda k: b),
        )

    def block_a(self, p):
        size = self.grid.levels * self.ca
        return self.rows_at(self.total, self.base + p * size, size)

    def block_b(self, z):
        size = self.grid.plane * self.cb
        return self.rows_at(self.total, self.base + self.rows_a + z * size, size)

    def wide_copies(self):
        a, b = self.block_a(self.here.p), self.block_b(self.here.z)
        return (
            self.plane_copy(4, self.sa, lambda k: a, lambda k: a),
            self.line_copy(4, self.sb, lambda k: b, lambda k: b),
        )

    def last_copy_a(self, k):
        grid = self.grid
        block = self.block_a(lax.rem(self.here.p + grid.plane - k, grid.plane))
        return send(block, block, self.sems(self.sa, 5, k), self.here.sibling())

    def last_copy_b(self, k):
        grid = self.grid
        block = self.block_b(lax.rem(self.here.z + grid.levels - k, grid.levels))
        return send(block, block, self.sems(self.sb, 5, k), self.here.sibling())

    def start(self, copies, counts):
        for copy, count in zip(copies, counts):
            each(1, count, lambda k: copy(k).start())

    def wait(self, copies, counts):
        for copy, count in zip(copies, counts):
            each(1, count, lambda k: copy(k).wait())

    def steps(self):
        return (
            self.step0,
            self.step1,
            self.step2,
            self.step3,
            self.step4,
            self.step5,
            self.step6,
        )

    def step0(self):
        self.swap().start()

    def step1(self):
        self.swap().wait()
        pl.semaphore_signal(
            self.free,
            inc=1,
            device_id=self.here.sibling(),
            device_id_type=pl.DeviceIdType.MESH,
        )
        size = self.ca + self.cb

        def add(k):
            at = pl.multiple_of(k * size, 16)
            mine_at = pl.multiple_of(self.base + k * size, 16)
            self.half[pl.ds(at, size), :] = (
                self.mine[pl.ds(mine_at, size), :].astype(f32)
                + self.near[pl.ds(at, size), :].astype(f32)
            ).astype(bf16)

        each(0, self.grid.chips, add)
        self.start(self.out_copies(), (self.grid.plane, self.grid.levels))

    def step2(self):
        grid, here = self.grid, self.here
        self.wait(self.out_copies(), (grid.plane, grid.levels))

        def add(slots, own, count, chunk, chunks):
            def body(j):
                rows = pl.ds(pl.multiple_of(j * chunk, 16), chunk)
                total = self.half[
                    pl.ds(pl.multiple_of(own + j * chunk, 16), chunk), :
                ].astype(f32)
                total = lax.fori_loop(
                    1, count, lambda k, acc: acc + slots[k, rows, :].astype(f32), total
                )
                slots[0, rows, :] = total.astype(bf16)

            each(0, chunks, body)

        add(self.a1, here.p * grid.levels * self.ca, grid.plane, self.ca, grid.levels)
        add(self.b1, self.rows_a + here.z * grid.plane * self.cb, grid.levels, self.cb, grid.plane)
        self.start(self.in_copies(), (grid.levels, grid.plane))

    def step3(self):
        grid, here = self.grid, self.here
        self.wait(self.in_copies(), (grid.levels, grid.plane))

        def add(blocks, own, slots, count, chunk, target):
            total = blocks[0, pl.ds(pl.multiple_of(own * chunk, 16), chunk), :].astype(f32)
            total = lax.fori_loop(
                1,
                count,
                lambda k, acc: acc
                + slots[0, pl.ds(pl.multiple_of(k * chunk, 16), chunk), :].astype(f32),
                total,
            )
            self.total[pl.ds(pl.multiple_of(target, 16), chunk), :] = total.astype(bf16)

        add(self.a1, here.z, self.a2, grid.levels, self.ca, self.chunk_a())
        add(self.b1, here.p, self.b2, grid.plane, self.cb, self.chunk_b())
        self.start(self.back_copies(), (grid.levels, grid.plane))

    def step4(self):
        grid = self.grid
        self.wait(self.back_copies(), (grid.levels, grid.plane))
        self.start(self.wide_copies(), (grid.plane, grid.levels))
        pl.semaphore_wait(self.free, 1)
        self.last_copy_a(0).start()
        self.last_copy_b(0).start()

    def step5(self):
        grid = self.grid
        wide_a, wide_b = self.wide_copies()

        def pass_a(k):
            wide_a(k).wait()
            self.last_copy_a(k).start()

        def pass_b(k):
            wide_b(k).wait()
            self.last_copy_b(k).start()

        each(1, grid.levels, pass_b)
        each(1, grid.plane, pass_a)

    def step6(self):
        each(0, self.grid.plane, lambda k: self.last_copy_a(k).wait())
        each(0, self.grid.levels, lambda k: self.last_copy_b(k).wait())


def main_kernel(
    grid,
    crop_side,
    tokens,
    cotangent,
    ln1_gain,
    ln1_bias,
    qkv_w,
    lepe_w,
    lepe_b,
    proj_w,
    proj_b,
    ln2_gain,
    ln2_bias,
    fc1_w,
    fc1_b,
    fc2_w,
    fc2_b,
    out,
    e_out,
    *refs,
):
    names = STATE + STATE_FEED
    totals, packed, sem_out, refs = refs[:3], refs[3:6], refs[6], refs[7:]
    layers = qkv_w.shape[0]
    state, grad, acc = {}, {}, {}
    for l in range(layers):
        state[l], refs = Env(**dict(zip(names, refs))), refs[len(names) :]
        grad[l], refs = Env(**dict(zip(GRADS, refs))), refs[len(GRADS) :]
        acc[l], refs = Env(**dict(zip(ACCS, refs))), refs[len(ACCS) :]
    dz, dqkv, lepb, leps, onesb, oness, stage, x, mid, do, vec = refs[:11]
    refs = refs[11:]
    e = x
    count = len(refs) // 3
    here = Here(grid)
    sums = [
        Total(here, ref, ref, refs[i * count : (i + 1) * count]) for i, ref in enumerate(packed)
    ]
    image = pl.program_id(0)
    env = Env(
        dim=tokens.shape[2],
        ff=fc1_w.shape[2],
        state=state,
        grad=grad,
        acc=acc,
        dz=dz,
        dqkv=dqkv,
        lepb=lepb,
        leps=leps,
        onesb=onesb,
        oness=oness,
        x=x,
        mid=mid,
        e=e,
        do=do,
        vec=vec,
        e_out=e,
        qkv_w=qkv_w,
        proj_w=proj_w,
        fc1_w=fc1_w,
        fc2_w=fc2_w,
        lepe_w=lepe_w,
    )

    @pl.when(image == 0)
    def _():
        here.greet()
        for l in range(layers):
            clear(env, l)
            for i, ref in enumerate(
                (ln1_gain, ln1_bias, lepe_b, proj_b, ln2_gain, ln2_bias, fc1_b, fc2_b)
            ):
                vec[l, i : i + 1, : ref.shape[1]] = ref[l : l + 1, :]
        stage[...] = jnp.zeros(stage.shape, f32)

    def last_image(body):
        pl.when(image == pl.num_programs(0) - 1)(body)

    starts = place_crops(crop_side, image)
    run = stages(env)
    lockstep([ingest(stage, starts, tokens, x)])
    for l in range(layers):
        units = [run.project(l, c * BIG_ROWS, BIG_ROWS, True) for c in range(BIG_CROPS)]
        units.append(run.project(l, SMALL_BASE, ROWS - SMALL_BASE, False))
        lockstep(units)
        lockstep(
            [run.attend_big(l, c) for c in range(BIG_CROPS)]
            + [run.attend_small(l, c, FWD_SMALL) for c in range(0, SMALL_CROPS, FWD_SMALL)]
        )
        lockstep(run.feed(l, c * CHUNK) for c in range(2))
    out[0] = x[...].astype(bf16)
    lockstep([ingest(stage, starts, cotangent, e)])

    def attend_back(l):
        return [run.attend_back_big(l, c) for c in range(BIG_CROPS)] + [
            run.attend_back_small(l, c, BWD_SMALL) for c in range(0, SMALL_CROPS, BWD_SMALL)
        ]

    def project_back(l):
        return [run.project_back(l, c * CHUNK) for c in range(2)]

    for l in reversed(range(1, layers)):
        lockstep([run.feed_back(l, c * CHUNK) for c in range(2)])
        lockstep(attend_back(l) + [run.feed_grads(l)])
        lockstep(project_back(l) + [run.qkv_grads(l)])

    @last_image
    def _():
        refs = [getattr(grad[l], name) for l in range(1, layers) for name in GRADS]
        fill(packed[0], refs, None)
        here.wait()
        sums[0].step0()

    lockstep([run.feed_back(0, c * CHUNK) for c in range(2)])

    @last_image
    def _():
        sums[0].step1()

    lockstep([run.feed_grads(0)])

    @last_image
    def _():
        fill(packed[1], [grad[0].fc1, grad[0].fc2, grad[0].proj], None)
        sums[1].step0()

    lockstep(attend_back(0))

    @last_image
    def _():
        sums[1].step1()

    lockstep(project_back(0) + [run.qkv_grads(0)])
    e_out[0] = e[...]

    @last_image
    def _():
        fill(packed[2], [grad[0].qkv], [acc[l] for l in range(layers)])
        done = [2, 2, 0]
        for which in LAST_STEPS:
            sums[which].steps()[done[which]]()
            done[which] += 1
            if done[which] == 7:
                pltpu.make_async_copy(packed[which], totals[which], sem_out.at[which]).start()
        for which in range(3):
            pltpu.make_async_copy(packed[which], totals[which], sem_out.at[which]).wait()


def last_kernel(factor, crop_side, x, e, total1, total2, total3, out, input_grad, *refs):
    g_gain1, g_bias1, g_qkv, g_lepe, g_lepe_b, g_proj, g_proj_b = refs[:7]
    g_gain2, g_bias2, g_fc1, g_fc1_b, g_fc2, g_fc2_b = refs[7:13]
    stage, held1, held2, held3, w_qkv, w_proj, w_fc1, w_fc2, sem_in, sem_out = refs[13:]
    layers = g_qkv.shape[0]
    image = pl.program_id(0)
    loads = [
        pltpu.make_async_copy(total, held, sem_in.at[i])
        for i, (total, held) in enumerate(
            ((total1, held1), (total2, held2), (total3, held3))
        )
    ]
    big = ((w_qkv, g_qkv), (w_proj, g_proj), (w_fc1, g_fc1), (w_fc2, g_fc2))
    stores = [
        [
            pltpu.make_async_copy(made.at[l], target.at[l], sem_out.at[i, l])
            for i, (made, target) in enumerate(big)
        ]
        for l in range(layers)
    ]

    def unpack(packed, l, which):
        at = 0
        for i in which:
            ref = big[i][0]
            rows, width = ref.shape[1:]
            for lane in range(0, width, GROUP):
                ref[l, :, lane : lane + GROUP] = packed[at : at + rows, :].astype(f32) * factor
                at += rows
            stores[l][i].start()
        return at

    @pl.when(image == 0)
    def _():
        for load in loads:
            load.start()

    starts = place_crops(crop_side, image)
    lockstep(
        [emit(stage.at[0], starts, x.at[0], out), emit(stage.at[1], starts, e.at[0], input_grad)]
    )

    @pl.when(image == 0)
    def _():
        loads[0].wait()
        at = 0
        for l in range(1, layers):
            at += unpack(held1.at[at:] if at else held1, l, range(4))
        loads[1].wait()
        unpack(held2, 0, (2, 3, 1))
        loads[2].wait()
        at = unpack(held3, 0, (0,))
        rest = held3[at:, :].astype(f32) * factor
        row = 0
        for l in range(layers):
            for ref in (
                g_gain1,
                g_bias1,
                g_lepe,
                g_lepe_b,
                g_proj_b,
                g_gain2,
                g_bias2,
                g_fc1_b,
                g_fc2_b,
            ):
                width = ref.shape[-1]
                for k in range(ref.size // (layers * width)):
                    for c in range(0, width, GROUP):
                        value = rest[row : row + 1]
                        if ref.ndim == 3:
                            ref[l, k : k + 1, c : c + GROUP] = value
                        else:
                            ref[l : l + 1, c : c + GROUP] = value
                        row += 1

    @pl.when(image == pl.num_programs(0) - 1)
    def _():
        for layer in stores:
            for store in layer:
                store.wait()


def local(tokens, crop_side, cotangent, *weights):
    images, tok, dim = tokens.shape
    qkv_w, proj_w, fc1_w, fc2_w = (weights[i] for i in (2, 5, 9, 11))
    layers = qkv_w.shape[0]
    ff = fc1_w.shape[2]
    devices = lax.axis_size("dp") * lax.axis_size("head")
    grid = Grid(lax.axis_size("dp"), lax.axis_size("head"))
    grad_rows = [w.size // (layers * GROUP) for w in (qkv_w, proj_w, fc1_w, fc2_w)]
    small_rows_all = sum(w.size for w in weights) // GROUP - layers * sum(grad_rows)
    parts = [
        (layers - 1) * sum(grad_rows),
        sum(grad_rows[1:]),
        grad_rows[0] + small_rows_all,
    ]
    packed_rows = [grid.packed_rows(rows) for rows in parts]

    whole = pl.BlockSpec(memory_space=pltpu.VMEM)
    smem = pl.BlockSpec(memory_space=pltpu.SMEM)
    anywhere = pl.BlockSpec(memory_space=pl.ANY)
    block = pl.BlockSpec((1, tok, dim), lambda i: (i, 0, 0))
    canonical = pl.BlockSpec((1, ROWS, dim), lambda i: (i, 0, 0))
    shapes = state_shapes(dim, ff)
    packed_types = [jax.ShapeDtypeStruct((rows, GROUP), bf16) for rows in packed_rows]
    out, e, *totals = pl.pallas_call(
        partial(main_kernel, grid),
        grid=(images,),
        out_shape=[
            jax.ShapeDtypeStruct((images, ROWS, dim), bf16),
            jax.ShapeDtypeStruct((images, ROWS, dim), f32),
        ]
        + packed_types,
        in_specs=[smem, block, block] + [whole] * len(weights),
        out_specs=[canonical, canonical] + [anywhere] * len(packed_rows),
        scratch_shapes=[pltpu.VMEM(part.shape, bf16) for part in packed_types]
        + [pltpu.SemaphoreType.DMA((3,))]
        + layers
        * (
            [pltpu.VMEM(*shapes[name]) for name in STATE + STATE_FEED]
            + grad_scratch(dim, ff)
            + acc_scratch(dim, ff)
        )
        + shared_scratch(dim)
        + [
            pltpu.VMEM((dim // GROUP, tok + 16, GROUP), f32),
            pltpu.VMEM((ROWS, dim), f32),
            pltpu.VMEM((ROWS, dim), f32),
            pltpu.VMEM((ROWS, dim), f32),
            pltpu.VMEM((layers, 8, ff), f32),
        ]
        + [scratch for rows in parts for scratch in grid.scratch(rows)],
        compiler_params=pltpu.CompilerParams(
            dimension_semantics=("arbitrary",),
            collective_id=0,
            has_side_effects=True,
            vmem_limit_bytes=VMEM_LIMIT,
        ),
    )(crop_side, tokens, cotangent, *weights)

    factor = 1.0 / math.sqrt(devices * images * tok)
    big = (2, 5, 9, 11)
    return pl.pallas_call(
        partial(last_kernel, factor),
        grid=(images,),
        out_shape=[
            jax.ShapeDtypeStruct(tokens.shape, bf16),
            jax.ShapeDtypeStruct(tokens.shape, f32),
        ]
        + [jax.ShapeDtypeStruct(w.shape, f32) for w in weights],
        in_specs=[smem, canonical, canonical] + [anywhere] * len(totals),
        out_specs=[block, block]
        + [anywhere if i in big else whole for i in range(len(weights))],
        scratch_shapes=[pltpu.VMEM((2, dim // GROUP, tok + 16, GROUP), f32)]
        + [pltpu.VMEM(part.shape, bf16) for part in packed_types]
        + [pltpu.VMEM(weights[i].shape, f32) for i in big]
        + [pltpu.SemaphoreType.DMA((3,)), pltpu.SemaphoreType.DMA((4, layers))],
        compiler_params=pltpu.CompilerParams(
            dimension_semantics=("arbitrary",), vmem_limit_bytes=VMEM_LIMIT
        ),
    )(crop_side, out, e, *totals)


def solution(mesh):
    sharded = P(("dp", "head"), None, None)
    return jax.shard_map(
        local,
        mesh=mesh,
        in_specs=(sharded, P(("dp", "head"), None), sharded) + (P(),) * 13,
        out_specs=(sharded, sharded) + (P(),) * 13,
        check_vma=False,
    )
```

```python
from functools import partial
import math

import jax
import jax.numpy as jnp
import numpy as np
from jax import lax
from jax.experimental import pallas as pl
from jax.experimental.pallas import tpu as pltpu
from jax.sharding import PartitionSpec as P

HEADS_GROUP = 4
HEAD_DIM = 32
SW = 7
BIG = 14
SMALL = 6
BIG_CROPS = 2
SMALL_CROPS = 6
GROUP = 128
EPSILON = 1e-05

BIG_ROWS = BIG * 16
WIN = SW * 16
SMALL_ROWS = SMALL * 8
SMALL_BASE = BIG_CROPS * BIG_ROWS
ROWS = SMALL_BASE + SMALL_CROPS * SMALL_ROWS
CHUNK = ROWS // 2

SCALE = HEAD_DIM**-0.5
LOG2E = math.log2(math.e)
NEG = -1e30
ROOT_HALF = math.sqrt(0.5)

PLANE_FIRST = 0.67
VMEM_LIMIT = 63 * 1024 * 1024
FWD_SMALL = 3
BWD_SMALL = 3
LAST_STEPS = (2, 2, 0, 1, 2, 0, 1, 2, 0, 1, 2, 0, 1, 2, 0, 1, 2)

bf16 = jnp.bfloat16
f32 = jnp.float32

NN = (((1,), (0,)), ((), ()))
NT = (((1,), (1,)), ((), ()))
TN = (((0,), (0,)), ((), ()))


def mm(a, b, dims=NN):
    return lax.dot_general(a, b, dims, preferred_element_type=f32)


def iota(shape, dim):
    return lax.broadcasted_iota(jnp.int32, shape, dim)


def to_vertical(x):
    x4 = x.reshape(BIG, 2, 8, x.shape[1])
    return jnp.concatenate([x4[:, 0].reshape(WIN, -1), x4[:, 1].reshape(WIN, -1)], axis=0)


def from_vertical(y):
    y4 = y.reshape(2, BIG, 8, y.shape[1])
    return jnp.stack([y4[0], y4[1]], axis=1).reshape(BIG_ROWS, -1)


def real_big():
    sub = iota((BIG_ROWS, GROUP), 0) % 16
    return ((sub != 0) & (sub != 15)).astype(f32)


def real_small(rows):
    return ((iota((rows, GROUP), 0) % 8) < SMALL).astype(f32)


def lockstep(streams):
    streams = list(streams)
    while streams:
        left = []
        for stream in streams:
            try:
                next(stream)
                left.append(stream)
            except StopIteration:
                pass
        streams = left


def partial_rows(x):
    return jnp.sum(x.reshape(x.shape[0] // 8, 8, x.shape[1]), axis=0)


def head_mask(h):
    lane = iota((1, GROUP), 1)
    return ((lane >= h * HEAD_DIM) & (lane < (h + 1) * HEAD_DIM)).astype(f32)


def block_heads(x, keys):
    rows = x.shape[0]
    parts = []
    for h in range(HEADS_GROUP):
        part = x * head_mask(h).astype(x.dtype)
        parts.append(part)
        if keys > rows:
            parts.append(jnp.zeros((keys - rows, GROUP), x.dtype))
    return jnp.concatenate(parts, axis=0)


def ones_heads(keys):
    row_head = iota((HEADS_GROUP * keys, GROUP), 0) // keys
    lane_head = iota((HEADS_GROUP * keys, GROUP), 1) // HEAD_DIM
    return (row_head == lane_head).astype(f32).astype(bf16)


def sum_heads(x, keys, rows):
    lane = iota((1, GROUP), 1)
    total = x[:rows]
    for h in range(1, HEADS_GROUP):
        total = jnp.where(lane >= h * HEAD_DIM, x[h * keys : h * keys + rows], total)
    return total


def keeps():
    sub = iota((8, GROUP), 0)
    return [(part).astype(f32) for part in (sub != 0, sub != 7, sub < SMALL)]


def ingest(stage, starts, source, target):
    keep_lo, keep_hi, keep_small = keeps()
    tok = source.shape[1]
    halves = source.shape[2] // GROUP
    for half in range(halves):
        stage[half, 8 : 8 + tok, :] = source[0, :, half * GROUP : (half + 1) * GROUP].astype(f32)
    for c in range(BIG_CROPS):
        yield
        start = starts[c] + 7
        for r in range(BIG):
            for half in range(halves):
                lanes = slice(half * GROUP, (half + 1) * GROUP)
                base = c * BIG_ROWS + r * 16
                lo = stage[half, pl.ds(start + r * BIG, 8), :]
                hi = stage[half, pl.ds(start + r * BIG + 8, 8), :]
                target[base : base + 8, lanes] = lo * keep_lo
                target[base + 8 : base + 16, lanes] = hi * keep_hi
    for c in range(SMALL_CROPS):
        if c % 3 == 0:
            yield
        start = starts[BIG_CROPS + c] + 8
        for r in range(SMALL):
            for half in range(halves):
                lanes = slice(half * GROUP, (half + 1) * GROUP)
                base = SMALL_BASE + c * SMALL_ROWS + r * 8
                lo = stage[half, pl.ds(start + r * SMALL, 8), :]
                target[base : base + 8, lanes] = lo * keep_small

def put(stage, half, at, value, keep):
    old = stage[half, pl.ds(at, 8), :]
    stage[half, pl.ds(at, 8), :] = jnp.where(keep > 0, value, old)

def emit(stage, starts, source, target):
    keep_lo, keep_hi, keep_small = keeps()
    tok = target.shape[1]
    halves = target.shape[2] // GROUP
    for c in range(BIG_CROPS):
        yield
        start = starts[c] + 7
        for r in range(BIG):
            for half in range(halves):
                lanes = slice(half * GROUP, (half + 1) * GROUP)
                base = c * BIG_ROWS + r * 16
                put(stage, half, start + r * BIG, source[base : base + 8, lanes].astype(f32), keep_lo)
                put(stage, half, start + r * BIG + 8, source[base + 8 : base + 16, lanes].astype(f32), keep_hi)
    for c in range(SMALL_CROPS):
        if c % 3 == 0:
            yield
        start = starts[BIG_CROPS + c] + 8
        for r in range(SMALL):
            for half in range(halves):
                lanes = slice(half * GROUP, (half + 1) * GROUP)
                base = SMALL_BASE + c * SMALL_ROWS + r * 8
                put(stage, half, start + r * SMALL, source[base : base + 8, lanes].astype(f32), keep_small)
    for half in range(halves):
        target[0, :, half * GROUP : (half + 1) * GROUP] = stage[half, 8 : 8 + tok, :].astype(
            target.dtype
        )


def place_crops(crop_side, image):
    start, n_big, n_small = jnp.int32(0), jnp.int32(0), jnp.int32(0)
    starts = [jnp.int32(0)] * (BIG_CROPS + SMALL_CROPS)
    for j in range(crop_side.shape[1]):
        side = crop_side[image, j]
        is_big = side == BIG
        slot = jnp.where(is_big, n_big, BIG_CROPS + n_small)
        for i in range(len(starts)):
            starts[i] = jnp.where(slot == i, start, starts[i])
        big_add = jnp.where(is_big, 1, 0)
        start, n_big, n_small = start + side * side, n_big + big_add, n_small + 1 - big_add
    return starts


class Env:
    def __init__(self, **refs):
        self.__dict__.update(refs)


STATE = ("n1", "r1", "a", "q", "k", "v", "eb", "es", "oat", "rdn")
STATE_FEED = ("o", "n2", "r2", "m", "g", "gp")


def state_shapes(dim, ff):
    wide = (ROWS, dim)
    shapes = dict.fromkeys(STATE + STATE_FEED, (wide, bf16))
    shapes["r1"] = shapes["r2"] = ((ROWS, GROUP), f32)
    shapes["g"] = shapes["gp"] = ((ROWS, ff), bf16)
    shapes["eb"] = ((4 * BIG_CROPS, WIN, HEADS_GROUP * GROUP), bf16)
    shapes["es"] = ((2 * SMALL_CROPS, SMALL_ROWS, HEADS_GROUP * 64), bf16)
    return shapes


GRADS = ("qkv", "proj", "fc1", "fc2")
ACCS = ("gain1", "bias1", "lepe", "lepe_b", "proj_b", "gain2", "bias2", "fc1_b", "fc2_b")


def acc_scratch(dim, ff):
    shapes = dict.fromkeys(ACCS, (8, dim))
    shapes["lepe"] = (9, 8, dim)
    shapes["fc1_b"] = (8, ff)
    return [pltpu.VMEM(shapes[name], f32) for name in ACCS]


def grad_scratch(dim, ff):
    shapes = ((dim, 3 * dim), (dim, dim), (dim, ff), (ff, dim))
    return [pltpu.VMEM(shape, f32) for shape in shapes]


def shared_scratch(dim):
    return [
        pltpu.VMEM((ROWS, dim), bf16),
        pltpu.VMEM((ROWS, 3 * dim), bf16),
        pltpu.VMEM((4 * BIG_CROPS, WIN + 48, GROUP), f32),
        pltpu.VMEM((2 * SMALL_CROPS, SMALL_ROWS + 32, GROUP), f32),
        pltpu.VMEM((4 * GROUP, GROUP), bf16),
        pltpu.VMEM((4 * 64, GROUP), bf16),
    ]


def clear(env, l):
    for ref in [getattr(env.grad[l], name) for name in GRADS] + [
        getattr(env.acc[l], name) for name in ACCS
    ]:
        ref[...] = jnp.zeros(ref.shape, f32)
    env.lepb[...] = jnp.zeros(env.lepb.shape, f32)
    env.leps[...] = jnp.zeros(env.leps.shape, f32)
    env.onesb[...] = ones_heads(GROUP)
    env.oness[...] = ones_heads(64)


def fill(packed, refs, accs):
    at = 0
    for ref in refs:
        rows, width = ref.shape
        for lane in range(0, width, GROUP):
            packed[at : at + rows, :] = ref[:, lane : lane + GROUP].astype(bf16)
            at += rows
    parts = [small_rows(acc) for acc in accs or ()]
    rest = packed.shape[0] - at - sum(part.shape[0] for part in parts)
    if rest:
        parts.append(jnp.zeros((rest, GROUP), f32))
    if parts:
        packed[at:, :] = jnp.concatenate(parts, axis=0).astype(bf16)


def small_rows(acc):
    parts = []
    for name in ACCS:
        value = getattr(acc, name)[...]
        for k in range(value.size // (8 * value.shape[-1])):
            row = jnp.sum(value[k] if value.ndim == 3 else value, axis=0, keepdims=True)
            parts += [row[:, c : c + GROUP] for c in range(0, row.shape[1], GROUP)]
    return jnp.concatenate(parts, axis=0)


def stages(env):
    dim, ff = env.dim, env.ff
    halves = dim // GROUP

    def norm_stats(x):
        center = x - jnp.mean(x, axis=1, keepdims=True)
        r = lax.rsqrt(jnp.mean(center * center, axis=1, keepdims=True) + EPSILON)
        return center * r, r

    def project(l, base, rows, big):
        rows_at = pl.ds(base, rows)
        n, r = norm_stats(env.x[rows_at, :])
        env.state[l].n1[rows_at, :] = n.astype(bf16)
        env.state[l].r1[rows_at, :] = jnp.broadcast_to(r, (rows, GROUP))
        yield
        a = (n * env.vec[l, 0:1, :dim] + env.vec[l, 1:2, :dim]).astype(bf16)
        env.state[l].a[rows_at, :] = a
        qkv = mm(a, env.qkv_w[l])
        yield
        real = real_big() if big else real_small(rows)
        for grp in range(2):
            cols = [slice(s * dim + grp * GROUP, s * dim + (grp + 1) * GROUP) for s in range(3)]
            q = qkv[:, cols[0]] * (SCALE * LOG2E)
            k = qkv[:, cols[1]]
            v = qkv[:, cols[2]] * real
            if big and grp == 1:
                q, k, v = to_vertical(q), to_vertical(k), to_vertical(v)
            lanes = slice(grp * GROUP, (grp + 1) * GROUP)
            env.state[l].q[rows_at, lanes] = q.astype(bf16)
            env.state[l].k[rows_at, lanes] = k.astype(bf16)
            env.state[l].v[rows_at, lanes] = v.astype(bf16)

    def pad_row(grp, w):
        u = iota((1, HEADS_GROUP * GROUP), 1) % GROUP
        if grp == 0:
            bad = (u % 16 == 0) | (u % 16 == 15)
        elif w == 0:
            bad = u % 8 == 0
        else:
            bad = u % 8 == 7
        return jnp.where(bad | (u >= WIN), NEG, 0.0).astype(f32)

    def pad_row_small():
        u = iota((1, HEADS_GROUP * 64), 1) % 64
        return jnp.where((u % 8 >= SMALL) | (u >= SMALL_ROWS), NEG, 0.0).astype(f32)

    def shifted(buf, idx, margin, stride, rows):
        return [buf[idx, pl.ds(margin - stride + b, rows + 2 * stride), :] for b in (-1, 0, 1)]

    def conv(views, stride, rows, weights, flip):
        total = None
        for a in range(3):
            for b in range(3):
                k = 3 * a + b
                wk = weights[8 - k : 9 - k] if flip else weights[k : k + 1]
                term = views[b][a * stride : a * stride + rows] * wk
                total = term if total is None else total + term
        return total

    def windows_big(c):
        for grp in range(2):
            for w in range(2):
                yield grp, w, c * BIG_ROWS + w * WIN

    def attend_big(l, c):
        items = list(windows_big(c))
        scores = []
        for grp, w, base in items:
            lanes = slice(grp * GROUP, (grp + 1) * GROUP)
            q = env.state[l].q[pl.ds(base, WIN), lanes]
            kb = block_heads(env.state[l].k[pl.ds(base, WIN), lanes], GROUP)
            scores.append(mm(q, kb, NT) + pad_row(grp, w))
        yield
        for i, (grp, w, base) in enumerate(items):
            parts = []
            for h in range(HEADS_GROUP):
                s = scores[i][:, h * GROUP : (h + 1) * GROUP]
                parts.append(jnp.exp2(s - jnp.max(s, axis=1, keepdims=True)).astype(bf16))
            env.state[l].eb[4 * c + 2 * grp + w] = jnp.concatenate(parts, axis=1)
        yield
        outs = []
        for i, (grp, w, base) in enumerate(items):
            lanes = slice(grp * GROUP, (grp + 1) * GROUP)
            v = env.state[l].v[pl.ds(base, WIN), lanes]
            vo = jnp.concatenate([block_heads(v, GROUP), env.onesb[...]], axis=1)
            both = mm(env.state[l].eb[4 * c + 2 * grp + w], vo)
            rden = 1.0 / both[:, GROUP:]
            oat = both[:, :GROUP] * rden
            env.state[l].rdn[pl.ds(base, WIN), lanes] = rden.astype(bf16)
            env.state[l].oat[pl.ds(base, WIN), lanes] = oat.astype(bf16)
            stride = 16 if grp == 0 else 8
            env.lepb[4 * c + i, pl.ds(24, WIN), :] = v.astype(f32)
            views = shifted(env.lepb, 4 * c + i, 24, stride, WIN)
            near = conv(views, stride, WIN, env.lepe_w[l, :, lanes], False)
            outs.append(oat + near + env.vec[l, 2:3, lanes])
            if w == 1:
                yield
        rows_at = pl.ds(c * BIG_ROWS, BIG_ROWS)
        env.state[l].o[rows_at, :GROUP] = jnp.concatenate(outs[:2], axis=0).astype(bf16)
        env.state[l].o[rows_at, GROUP:] = from_vertical(jnp.concatenate(outs[2:], axis=0)).astype(bf16)

    def attend_small(l, c0, count):
        items = [
            (grp, c0 + c, SMALL_BASE + (c0 + c) * SMALL_ROWS, 2 * (c0 + c) + grp)
            for c in range(count)
            for grp in range(2)
        ]
        low = iota((SMALL_ROWS, GROUP), 1) < 64
        scores = []
        for grp, c, base, i in items:
            lanes = slice(grp * GROUP, (grp + 1) * GROUP)
            q = env.state[l].q[pl.ds(base, SMALL_ROWS), lanes]
            kb = block_heads(env.state[l].k[pl.ds(base, SMALL_ROWS), lanes], 64)
            scores.append(mm(q, kb, NT) + pad_row_small())
        yield
        for j, (grp, c, base, i) in enumerate(items):
            parts = []
            for t in range(2):
                s = scores[j][:, t * GROUP : (t + 1) * GROUP]
                top_lo = jnp.max(jnp.where(low, s, 2 * NEG), axis=1, keepdims=True)
                top_hi = jnp.max(jnp.where(low, 2 * NEG, s), axis=1, keepdims=True)
                parts.append(jnp.exp2(s - jnp.where(low, top_lo, top_hi)).astype(bf16))
            env.state[l].es[2 * c + grp] = jnp.concatenate(parts, axis=1)
        yield
        for grp, c, base, i in items:
            lanes = slice(grp * GROUP, (grp + 1) * GROUP)
            v = env.state[l].v[pl.ds(base, SMALL_ROWS), lanes]
            vo = jnp.concatenate([block_heads(v, 64), env.oness[...]], axis=1)
            both = mm(env.state[l].es[2 * c + grp], vo)
            rden = 1.0 / both[:, GROUP:]
            oat = both[:, :GROUP] * rden
            env.state[l].rdn[pl.ds(base, SMALL_ROWS), lanes] = rden.astype(bf16)
            env.state[l].oat[pl.ds(base, SMALL_ROWS), lanes] = oat.astype(bf16)
            env.leps[i, pl.ds(16, SMALL_ROWS), :] = v.astype(f32)
            views = shifted(env.leps, i, 16, 8, SMALL_ROWS)
            near = conv(views, 8, SMALL_ROWS, env.lepe_w[l, :, lanes], False)
            env.state[l].o[pl.ds(base, SMALL_ROWS), lanes] = (oat + near + env.vec[l, 2:3, lanes]).astype(
                bf16
            )

    def feed(l, base):
        rows_at = pl.ds(base, CHUNK)
        mid = env.x[rows_at, :] + mm(env.state[l].o[rows_at, :], env.proj_w[l]) + env.vec[l, 3:4, :dim]
        yield
        n, r = norm_stats(mid)
        env.state[l].n2[rows_at, :] = n.astype(bf16)
        env.state[l].r2[rows_at, :] = jnp.broadcast_to(r, (CHUNK, GROUP))
        m = (n * env.vec[l, 8:9, :dim] + env.vec[l, 5:6, :dim]).astype(bf16)
        env.state[l].m[rows_at, :] = m
        yield
        step = 256
        for j in range(ff // step):
            cols = slice(j * step, (j + 1) * step)
            f = mm(m, env.fc1_w[l, :, cols]) + env.vec[l, 6:7, cols]
            twice = lax.erf(f) + 1.0
            dens = jnp.exp2(f * f * np.float32(-LOG2E)) * np.float32(2.0 / math.sqrt(math.pi))
            env.state[l].g[rows_at, cols] = (f * twice).astype(bf16)
            env.state[l].gp[rows_at, cols] = (twice + f * dens).astype(bf16)
            yield
        env.x[rows_at, :] = (
            mid
            + env.vec[l, 7:8, :dim]
            + mm(env.state[l].g[rows_at, :], env.fc2_w[l]) * np.float32(ROOT_HALF)
        )

    def norm_back(dm, n, r, gain):
        dn = dm * gain
        mean_one = jnp.mean(dn, axis=1, keepdims=True)
        mean_two = jnp.mean(dn * n, axis=1, keepdims=True)
        rb = jnp.concatenate([r] * halves, axis=1)
        return rb * (dn - mean_one - n * mean_two)

    def feed_back(l, base):
        rows_at = pl.ds(base, CHUNK)
        e = env.e[rows_at, :]
        dz = e.astype(bf16)
        env.dz[rows_at, :] = dz
        half_dz = (0.5 * e).astype(bf16)
        env.acc[l].fc2_b[...] += partial_rows(dz.astype(f32))
        yield
        step = 256
        for j in range(ff // step):
            cols = slice(j * step, (j + 1) * step)
            df = mm(half_dz, env.fc2_w[l, cols, :], NT) * env.state[l].gp[rows_at, cols].astype(f32)
            env.state[l].gp[rows_at, cols] = df.astype(bf16)
            env.acc[l].fc1_b[:, cols] += partial_rows(df)
            yield
        dm = mm(env.state[l].gp[rows_at, :], env.fc1_w[l], NT)
        yield
        n = env.state[l].n2[rows_at, :].astype(f32)
        env.acc[l].gain2[...] += partial_rows(dm * n)
        env.acc[l].bias2[...] += partial_rows(dm)
        dmid = e + norm_back(dm, n, env.state[l].r2[rows_at, :], env.vec[l, 4:5, :dim])
        env.mid[rows_at, :] = dmid
        yield
        dy = dmid.astype(bf16)
        env.acc[l].proj_b[...] += partial_rows(dy.astype(f32))
        env.do[rows_at, :] = mm(dy, env.proj_w[l], NT).astype(bf16).astype(f32)

    def lepe_back(l, buf, idx, margin, stride, rows, lanes, v):
        views = [buf[idx, pl.ds(margin - stride + b, rows + 2 * stride), :] for b in (-1, 0, 1)]
        vf = v.astype(f32)
        for k in range(9):
            a, b = divmod(8 - k, 3)
            env.acc[l].lepe[k, :, lanes] += partial_rows(views[b][a * stride : a * stride + rows] * vf)
        env.acc[l].lepe_b[:, lanes] += partial_rows(views[1][stride : stride + rows])
        return conv(views, stride, rows, env.lepe_w[l, :, lanes], True)

    def attend_back(l, group_items, rows, keys, buf, margin, strides, e_ref, ones, unit):
        grads = []
        kbs = []
        ds_all = []
        dop_all = []
        for grp, base, e_at, lep_at, do in group_items:
            lanes = slice(grp * GROUP, (grp + 1) * GROUP)
            rows_at = pl.ds(base, rows)
            buf[lep_at, pl.ds(margin, rows), :] = do
            dop = do * env.state[l].rdn[rows_at, lanes].astype(f32)
            tail = -(dop * env.state[l].oat[rows_at, lanes].astype(f32))
            dop_all.append(dop.astype(bf16))
            left = jnp.concatenate([dop.astype(bf16), tail.astype(bf16)], axis=1)
            vo = jnp.concatenate([block_heads(env.state[l].v[rows_at, lanes], keys), ones[...]], axis=1)
            x = mm(left, vo, NT)
            ds_all.append((e_ref[e_at].astype(f32) * x).astype(bf16))
        yield
        for i, (grp, base, e_at, lep_at, do) in enumerate(group_items):
            lanes = slice(grp * GROUP, (grp + 1) * GROUP)
            kb = block_heads(env.state[l].k[pl.ds(base, rows), lanes], keys)
            grads.append([mm(ds_all[i], kb) * SCALE])
        yield
        zero_block = jnp.zeros((rows, GROUP), bf16)
        for i in range(0, len(group_items), 2):
            pair = group_items[i : i + 2]

            def spread(first, second):
                return jnp.concatenate(
                    [
                        jnp.concatenate([first, zero_block], axis=1),
                        jnp.concatenate([zero_block, second], axis=1),
                    ],
                    axis=0,
                )

            qs = [env.state[l].q[pl.ds(it[1], rows), it[0] * GROUP : (it[0] + 1) * GROUP] for it in pair]
            dk = mm(jnp.concatenate(ds_all[i : i + 2], axis=0), spread(*qs), TN)
            es = jnp.concatenate([e_ref[it[2]] for it in pair], axis=0)
            dv = mm(es, spread(*dop_all[i : i + 2]), TN)
            for j, (grp, base, e_at, lep_at, do) in enumerate(pair):
                lanes = slice(grp * GROUP, (grp + 1) * GROUP)
                cols = slice(j * GROUP, (j + 1) * GROUP)
                near = lepe_back(
                    l, buf, lep_at, margin, strides[grp], rows, lanes, env.state[l].v[pl.ds(base, rows), lanes]
                )
                grads[i + j].append(sum_heads(dk[:, cols], keys, rows) * (1.0 / LOG2E))
                grads[i + j].append(sum_heads(dv[:, cols], keys, rows) + near)
            yield
        return grads

    def attend_back_big(l, c):
        rows_at = pl.ds(c * BIG_ROWS, BIG_ROWS)
        do_h = env.do[rows_at, :GROUP]
        do_v = to_vertical(env.do[rows_at, GROUP:])
        items = []
        for i, (grp, w, base) in enumerate(windows_big(c)):
            do = (do_h if grp == 0 else do_v)[w * WIN : (w + 1) * WIN]
            items.append((grp, base, 4 * c + 2 * grp + w, 4 * c + i, do))
        grads = yield from attend_back(l, items, WIN, GROUP, env.lepb, 24, (16, 8), env.state[l].eb, env.onesb, None)
        real = real_big()
        for s in range(3):
            left = jnp.concatenate([grads[0][s], grads[1][s]], axis=0)
            right = from_vertical(jnp.concatenate([grads[2][s], grads[3][s]], axis=0))
            if s == 2:
                left, right = left * real, right * real
            env.dqkv[rows_at, s * dim : s * dim + GROUP] = left.astype(bf16)
            env.dqkv[rows_at, s * dim + GROUP : (s + 1) * dim] = right.astype(bf16)

    def attend_back_small(l, c0, count):
        items = []
        for grp in range(2):
            for c in range(count):
                base = SMALL_BASE + (c0 + c) * SMALL_ROWS
                do = env.do[pl.ds(base, SMALL_ROWS), grp * GROUP : (grp + 1) * GROUP]
                items.append((grp, base, 2 * (c0 + c) + grp, 2 * (c0 + c) + grp, do))
        grads = yield from attend_back(l, items, SMALL_ROWS, 64, env.leps, 16, (8, 8), env.state[l].es, env.oness, None)
        real = real_small(SMALL_ROWS)
        for (grp, base, e_at, lep_at, do), grad in zip(items, grads):
            for s in range(3):
                value = grad[s] * real if s == 2 else grad[s]
                at = s * dim + grp * GROUP
                env.dqkv[pl.ds(base, SMALL_ROWS), at : at + GROUP] = value.astype(bf16)

    def project_back(l, base):
        rows_at = pl.ds(base, CHUNK)
        da = mm(env.dqkv[rows_at, :], env.qkv_w[l], NT)
        yield
        n = env.state[l].n1[rows_at, :].astype(f32)
        env.acc[l].gain1[...] += partial_rows(da * n)
        env.acc[l].bias1[...] += partial_rows(da)
        env.e_out[rows_at, :] = env.mid[rows_at, :] + norm_back(
            da, n, env.state[l].r1[rows_at, :], env.vec[l, 0:1, :dim]
        )

    def feed_grads(l):
        dz = env.dz[...]
        for j in range(0, ff, 256):
            cols = slice(j, j + 256)
            env.grad[l].fc2[cols, :] += mm(env.state[l].g[:, cols], dz, TN)
            yield
            env.grad[l].fc1[:, cols] += mm(env.state[l].m[...], env.state[l].gp[:, cols], TN)
            yield
        env.grad[l].proj[...] += mm(env.state[l].o[...], env.mid[...].astype(bf16), TN)

    def qkv_grads(l):
        for j in range(0, 3 * dim, 256):
            cols = slice(j, j + 256)
            env.grad[l].qkv[:, cols] += mm(env.state[l].a[...], env.dqkv[:, cols], TN)
            yield

    return Env(
        project=project,
        attend_big=attend_big,
        attend_small=attend_small,
        feed=feed,
        feed_back=feed_back,
        feed_grads=feed_grads,
        attend_back_big=attend_back_big,
        attend_back_small=attend_back_small,
        project_back=project_back,
        qkv_grads=qkv_grads,
    )


class Grid:
    def __init__(self, dp, heads):
        chips = dp // 2
        self.heads = heads
        self.levels = next(n for n in (4, 2, 1) if chips % n == 0)
        self.low = chips // self.levels
        self.plane = self.low * heads
        self.chips = chips * heads

    def split(self, rows):
        units = max(2, -(-rows // (2 * 16 * self.chips)))
        first = min(units - 1, max(1, round(PLANE_FIRST * units)))
        return 16 * first, 16 * (units - first)

    def packed_rows(self, rows):
        return 2 * self.chips * sum(self.split(rows))

    def scratch(self, rows):
        ca, cb = self.split(rows)
        half = self.chips * (ca + cb)
        return [
            pltpu.VMEM((half, GROUP), bf16),
            pltpu.VMEM((half, GROUP), bf16),
            pltpu.VMEM((self.plane, self.levels * ca, GROUP), bf16),
            pltpu.VMEM((self.levels, self.plane * cb, GROUP), bf16),
            pltpu.VMEM((1, self.levels * ca, GROUP), bf16),
            pltpu.VMEM((1, self.plane * cb, GROUP), bf16),
            pltpu.SemaphoreType.DMA((6, 2, self.plane)),
            pltpu.SemaphoreType.DMA((6, 2, self.levels)),
            pltpu.SemaphoreType.REGULAR,
        ]


def aligned(start):
    return start if isinstance(start, int) else pl.multiple_of(start, 16)


def each(first, last, body):
    if last - first <= 4:
        for k in range(first, last):
            body(k)
        return

    def step(k, carry):
        body(k)
        return carry

    lax.fori_loop(first, last, step, 0)


def add_up(first, last, total, term):
    if last - first <= 4:
        for k in range(first, last):
            total = total + term(k)
        return total
    return lax.fori_loop(first, last, lambda k, acc: acc + term(k), total)


class Here:
    def __init__(self, grid):
        self.grid = grid
        dp = lax.axis_index("dp")
        self.core = lax.rem(dp, 2)
        chip = dp // 2
        self.z = chip // grid.low
        self.p = lax.rem(chip, grid.low) * grid.heads + lax.axis_index("head")

    def device(self, z, p, core):
        low = p // self.grid.heads
        return (2 * (z * self.grid.low + low) + core, lax.rem(p, self.grid.heads))

    def sibling(self):
        return self.device(self.z, self.p, 1 - self.core)

    def in_plane(self, k):
        other = lax.rem(self.p + k, self.grid.plane)
        return other, self.device(self.z, other, self.core)

    def in_line(self, k):
        other = lax.rem(self.z + k, self.grid.levels)
        return other, self.device(other, self.p, self.core)

    def greet(self):
        barrier = pltpu.get_barrier_semaphore()

        def signal(device):
            pl.semaphore_signal(
                barrier, inc=1, device_id=device, device_id_type=pl.DeviceIdType.MESH
            )

        signal(self.sibling())
        each(1, self.grid.plane, lambda k: signal(self.in_plane(k)[1]))
        each(1, self.grid.levels, lambda k: signal(self.in_line(k)[1]))

    def wait(self):
        pl.semaphore_wait(
            pltpu.get_barrier_semaphore(), self.grid.plane + self.grid.levels - 1
        )


def send(source, target, sems, device):
    return pltpu.make_async_remote_copy(
        src_ref=source,
        dst_ref=target,
        send_sem=sems[0],
        recv_sem=sems[1],
        device_id=device,
        device_id_type=pl.DeviceIdType.MESH,
    )


class Total:
    def __init__(self, here, mine, total, scratch):
        self.here, self.mine, self.total = here, mine, total
        self.near, self.half, self.a1, self.b1, self.a2, self.b2 = scratch[:6]
        self.sa, self.sb, self.free = scratch[6:]
        grid = here.grid
        self.grid = grid
        self.ca = self.a1.shape[1] // grid.levels
        self.cb = self.b1.shape[1] // grid.plane
        self.rows_a = grid.chips * self.ca
        self.rows = self.half.shape[0]
        self.base = here.core * self.rows

    def rows_at(self, ref, start, count):
        return ref.at[pl.ds(aligned(start), count)]

    def sems(self, table, stage, k):
        return table.at[stage, 0, k], table.at[stage, 1, k]

    def plane_copy(self, stage, table, source, target):
        return lambda k: send(
            source(k), target(k), self.sems(table, stage, k), self.here.in_plane(k)[1]
        )

    def line_copy(self, stage, table, source, target):
        return lambda k: send(
            source(k), target(k), self.sems(table, stage, k), self.here.in_line(k)[1]
        )

    def swap(self):
        side = 1 - self.here.core
        return send(
            self.rows_at(self.mine, side * self.rows, self.rows),
            self.near,
            self.sems(self.sa, 0, 0),
            self.here.sibling(),
        )

    def out_copies(self):
        here, ca, cb = self.here, self.grid.levels * self.ca, self.grid.plane * self.cb
        first = self.plane_copy(
            1,
            self.sa,
            lambda k: self.rows_at(self.half, here.in_plane(k)[0] * ca, ca),
            lambda k: self.a1.at[k],
        )
        second = self.line_copy(
            1,
            self.sb,
            lambda k: self.rows_at(self.half, self.rows_a + here.in_line(k)[0] * cb, cb),
            lambda k: self.b1.at[k],
        )
        return first, second

    def in_copies(self):
        here, ca, cb = self.here, self.ca, self.cb
        first = self.line_copy(
            2,
            self.sb,
            lambda k: self.rows_at(self.a1.at[0], here.in_line(k)[0] * ca, ca),
            lambda k: self.rows_at(self.a2.at[0], k * ca, ca),
        )
        second = self.plane_copy(
            2,
            self.sa,
            lambda k: self.rows_at(self.b1.at[0], here.in_plane(k)[0] * cb, cb),
            lambda k: self.rows_at(self.b2.at[0], k * cb, cb),
        )
        return first, second

    def chunk_a(self):
        here = self.here
        return self.base + (here.p * self.grid.levels + here.z) * self.ca

    def chunk_b(self):
        here = self.here
        return self.base + self.rows_a + (here.z * self.grid.plane + here.p) * self.cb

    def back_copies(self):
        a = self.rows_at(self.total, self.chunk_a(), self.ca)
        b = self.rows_at(self.total, self.chunk_b(), self.cb)
        return (
            self.line_copy(3, self.sb, lambda k: a, lambda k: a),
            self.plane_copy(3, self.sa, lambda k: b, lambda k: b),
        )

    def block_a(self, p):
        size = self.grid.levels * self.ca
        return self.rows_at(self.total, self.base + p * size, size)

    def block_b(self, z):
        size = self.grid.plane * self.cb
        return self.rows_at(self.total, self.base + self.rows_a + z * size, size)

    def wide_copies(self):
        a, b = self.block_a(self.here.p), self.block_b(self.here.z)
        return (
            self.plane_copy(4, self.sa, lambda k: a, lambda k: a),
            self.line_copy(4, self.sb, lambda k: b, lambda k: b),
        )

    def last_copy_a(self, k):
        grid = self.grid
        block = self.block_a(lax.rem(self.here.p + grid.plane - k, grid.plane))
        return send(block, block, self.sems(self.sa, 5, k), self.here.sibling())

    def last_copy_b(self, k):
        grid = self.grid
        block = self.block_b(lax.rem(self.here.z + grid.levels - k, grid.levels))
        return send(block, block, self.sems(self.sb, 5, k), self.here.sibling())

    def start(self, copies, counts):
        for copy, count in zip(copies, counts):
            each(1, count, lambda k: copy(k).start())

    def wait(self, copies, counts):
        for copy, count in zip(copies, counts):
            each(1, count, lambda k: copy(k).wait())

    def steps(self):
        return (
            self.step0,
            self.step1,
            self.step2,
            self.step3,
            self.step4,
            self.step5,
            self.step6,
        )

    def step0(self):
        self.swap().start()

    def step1(self):
        self.swap().wait()
        pl.semaphore_signal(
            self.free,
            inc=1,
            device_id=self.here.sibling(),
            device_id_type=pl.DeviceIdType.MESH,
        )
        slabs = 4 if self.grid.chips % 4 == 0 else 1
        size = (self.ca + self.cb) * self.grid.chips // slabs

        def add(k):
            at = aligned(k * size)
            mine_at = pl.multiple_of(self.base + k * size, 16)
            self.half[pl.ds(at, size), :] = (
                self.mine[pl.ds(mine_at, size), :].astype(f32)
                + self.near[pl.ds(at, size), :].astype(f32)
            ).astype(bf16)

        each(0, slabs, add)
        self.start(self.out_copies(), (self.grid.plane, self.grid.levels))

    def step2(self):
        grid, here = self.grid, self.here
        self.wait(self.out_copies(), (grid.plane, grid.levels))

        def add(slots, own, count, chunk, chunks):
            def body(j):
                rows = pl.ds(aligned(j * chunk), chunk)
                total = self.half[
                    pl.ds(pl.multiple_of(own + j * chunk, 16), chunk), :
                ].astype(f32)
                total = add_up(1, count, total, lambda k: slots[k, rows, :].astype(f32))
                slots[0, rows, :] = total.astype(bf16)

            each(0, chunks, body)

        add(self.a1, here.p * grid.levels * self.ca, grid.plane, self.ca, grid.levels)
        add(self.b1, self.rows_a + here.z * grid.plane * self.cb, grid.levels, self.cb, grid.plane)
        self.start(self.in_copies(), (grid.levels, grid.plane))

    def step3(self):
        grid, here = self.grid, self.here
        self.wait(self.in_copies(), (grid.levels, grid.plane))

        def add(blocks, own, slots, count, chunk, target):
            total = blocks[0, pl.ds(pl.multiple_of(own * chunk, 16), chunk), :].astype(f32)
            total = add_up(
                1,
                count,
                total,
                lambda k: slots[0, pl.ds(aligned(k * chunk), chunk), :].astype(f32),
            )
            self.total[pl.ds(pl.multiple_of(target, 16), chunk), :] = total.astype(bf16)

        add(self.a1, here.z, self.a2, grid.levels, self.ca, self.chunk_a())
        add(self.b1, here.p, self.b2, grid.plane, self.cb, self.chunk_b())
        self.start(self.back_copies(), (grid.levels, grid.plane))

    def step4(self):
        grid = self.grid
        self.wait(self.back_copies(), (grid.levels, grid.plane))
        self.start(self.wide_copies(), (grid.plane, grid.levels))
        pl.semaphore_wait(self.free, 1)
        self.last_copy_a(0).start()
        self.last_copy_b(0).start()

    def step5(self):
        grid = self.grid
        wide_a, wide_b = self.wide_copies()

        def pass_a(k):
            wide_a(k).wait()
            self.last_copy_a(k).start()

        def pass_b(k):
            wide_b(k).wait()
            self.last_copy_b(k).start()

        each(1, grid.levels, pass_b)
        each(1, grid.plane, pass_a)

    def step6(self):
        each(0, self.grid.plane, lambda k: self.last_copy_a(k).wait())
        each(0, self.grid.levels, lambda k: self.last_copy_b(k).wait())


def main_kernel(
    grid,
    crop_side,
    tokens,
    cotangent,
    ln1_gain,
    ln1_bias,
    qkv_w,
    lepe_w,
    lepe_b,
    proj_w,
    proj_b,
    ln2_gain,
    ln2_bias,
    fc1_w,
    fc1_b,
    fc2_w,
    fc2_b,
    out,
    e_out,
    *refs,
):
    names = STATE + STATE_FEED
    totals, packed, sem_out, refs = refs[:3], refs[3:6], refs[6], refs[7:]
    layers = qkv_w.shape[0]
    state, grad, acc = {}, {}, {}
    for l in range(layers):
        state[l], refs = Env(**dict(zip(names, refs))), refs[len(names) :]
        grad[l], refs = Env(**dict(zip(GRADS, refs))), refs[len(GRADS) :]
        acc[l], refs = Env(**dict(zip(ACCS, refs))), refs[len(ACCS) :]
    dz, dqkv, lepb, leps, onesb, oness, stage, x, mid, do, vec = refs[:11]
    refs = refs[11:]
    e = x
    count = len(refs) // 3
    here = Here(grid)
    sums = [
        Total(here, ref, ref, refs[i * count : (i + 1) * count]) for i, ref in enumerate(packed)
    ]
    image = pl.program_id(0)
    env = Env(
        dim=tokens.shape[2],
        ff=fc1_w.shape[2],
        state=state,
        grad=grad,
        acc=acc,
        dz=dz,
        dqkv=dqkv,
        lepb=lepb,
        leps=leps,
        onesb=onesb,
        oness=oness,
        x=x,
        mid=mid,
        e=e,
        do=do,
        vec=vec,
        e_out=e,
        qkv_w=qkv_w,
        proj_w=proj_w,
        fc1_w=fc1_w,
        fc2_w=fc2_w,
        lepe_w=lepe_w,
    )

    @pl.when(image == 0)
    def _():
        here.greet()
        for l in range(layers):
            clear(env, l)
            for i, ref in enumerate(
                (ln1_gain, ln1_bias, lepe_b, proj_b, ln2_gain, ln2_bias, fc1_b, fc2_b, ln2_gain)
            ):
                scale = ROOT_HALF if i in (5, 6, 8) else 1.0
                vec[l, i : i + 1, : ref.shape[1]] = ref[l : l + 1, :] * np.float32(scale)
        stage[...] = jnp.zeros(stage.shape, f32)

    def last_image(body):
        pl.when(image == pl.num_programs(0) - 1)(body)

    starts = place_crops(crop_side, image)
    run = stages(env)
    lockstep([ingest(stage, starts, tokens, x)])
    for l in range(layers):
        units = [run.project(l, c * BIG_ROWS, BIG_ROWS, True) for c in range(BIG_CROPS)]
        units.append(run.project(l, SMALL_BASE, ROWS - SMALL_BASE, False))
        lockstep(units)
        lockstep(
            [run.attend_big(l, c) for c in range(BIG_CROPS)]
            + [run.attend_small(l, c, FWD_SMALL) for c in range(0, SMALL_CROPS, FWD_SMALL)]
        )
        lockstep(run.feed(l, c * CHUNK) for c in range(2))
    out[0] = x[...].astype(bf16)
    lockstep([ingest(stage, starts, cotangent, e)])

    def attend_back(l):
        return [run.attend_back_big(l, c) for c in range(BIG_CROPS)] + [
            run.attend_back_small(l, c, BWD_SMALL) for c in range(0, SMALL_CROPS, BWD_SMALL)
        ]

    def project_back(l):
        return [run.project_back(l, c * CHUNK) for c in range(2)]

    for l in reversed(range(1, layers)):
        lockstep([run.feed_back(l, c * CHUNK) for c in range(2)])
        lockstep(attend_back(l) + [run.feed_grads(l)])
        lockstep(project_back(l) + [run.qkv_grads(l)])

    @last_image
    def _():
        refs = [getattr(grad[l], name) for l in range(1, layers) for name in GRADS]
        fill(packed[0], refs, None)
        here.wait()
        sums[0].step0()

    lockstep([run.feed_back(0, c * CHUNK) for c in range(2)])

    @last_image
    def _():
        sums[0].step1()

    lockstep([run.feed_grads(0)])

    @last_image
    def _():
        fill(packed[1], [grad[0].fc1, grad[0].fc2, grad[0].proj], None)
        sums[1].step0()

    lockstep(attend_back(0))

    @last_image
    def _():
        sums[1].step1()

    lockstep(project_back(0) + [run.qkv_grads(0)])
    e_out[0] = e[...]

    @last_image
    def _():
        fill(packed[2], [grad[0].qkv], [acc[l] for l in range(layers)])
        done = [2, 2, 0]
        for which in LAST_STEPS:
            sums[which].steps()[done[which]]()
            done[which] += 1
            if done[which] == 7:
                pltpu.make_async_copy(packed[which], totals[which], sem_out.at[which]).start()
        for which in range(3):
            pltpu.make_async_copy(packed[which], totals[which], sem_out.at[which]).wait()


def last_kernel(factor, images, crop_side, x, e, total1, total2, total3, out, input_grad, *refs):
    g_gain1, g_bias1, g_qkv, g_lepe, g_lepe_b, g_proj, g_proj_b = refs[:7]
    g_gain2, g_bias2, g_fc1, g_fc1_b, g_fc2, g_fc2_b = refs[7:13]
    stage, held1, held2, held3, w_qkv, w_proj, w_fc1, w_fc2, sem_in, sem_out = refs[13:]
    layers = g_qkv.shape[0]
    image = pl.program_id(0)
    loads = [
        pltpu.make_async_copy(total, held, sem_in.at[i])
        for i, (total, held) in enumerate(
            ((total1, held1), (total2, held2), (total3, held3))
        )
    ]
    big = ((w_qkv, g_qkv), (w_proj, g_proj), (w_fc1, g_fc1), (w_fc2, g_fc2))
    stores = [
        [
            pltpu.make_async_copy(made.at[l], target.at[l], sem_out.at[i, l])
            for i, (made, target) in enumerate(big)
        ]
        for l in range(layers)
    ]

    def unpack(packed, l, which):
        at = 0
        for i in which:
            ref = big[i][0]
            scale = factor * (1.0, 1.0, 1.0 / ROOT_HALF, ROOT_HALF)[i]
            rows, width = ref.shape[1:]
            for lane in range(0, width, GROUP):
                ref[l, :, lane : lane + GROUP] = packed[at : at + rows, :].astype(f32) * scale
                at += rows
            stores[l][i].start()
        return at

    @pl.when(image == 0)
    def _():
        for load in loads:
            load.start()

    starts = place_crops(crop_side, image)
    lockstep(
        [emit(stage.at[0], starts, x.at[0], out), emit(stage.at[1], starts, e.at[0], input_grad)]
    )

    @pl.when(image == 0)
    def _():
        loads[0].wait()
        at = 0
        for l in range(1, layers):
            at += unpack(held1.at[at:] if at else held1, l, range(4))

    @pl.when(image == min(1, images - 1))
    def _():
        loads[1].wait()
        unpack(held2, 0, (2, 3, 1))
        loads[2].wait()
        at = unpack(held3, 0, (0,))
        rest = held3[at:, :].astype(f32) * factor
        row = 0
        for l in range(layers):
            for ref in (
                g_gain1,
                g_bias1,
                g_lepe,
                g_lepe_b,
                g_proj_b,
                g_gain2,
                g_bias2,
                g_fc1_b,
                g_fc2_b,
            ):
                width = ref.shape[-1]
                for k in range(ref.size // (layers * width)):
                    for c in range(0, width, GROUP):
                        value = rest[row : row + 1]
                        if ref.ndim == 3:
                            ref[l, k : k + 1, c : c + GROUP] = value
                        else:
                            ref[l : l + 1, c : c + GROUP] = value
                        row += 1

    @pl.when(image == pl.num_programs(0) - 1)
    def _():
        for layer in stores:
            for store in layer:
                store.wait()


def local(tokens, crop_side, cotangent, *weights):
    images, tok, dim = tokens.shape
    qkv_w, proj_w, fc1_w, fc2_w = (weights[i] for i in (2, 5, 9, 11))
    layers = qkv_w.shape[0]
    ff = fc1_w.shape[2]
    devices = lax.axis_size("dp") * lax.axis_size("head")
    grid = Grid(lax.axis_size("dp"), lax.axis_size("head"))
    grad_rows = [w.size // (layers * GROUP) for w in (qkv_w, proj_w, fc1_w, fc2_w)]
    small_rows_all = sum(w.size for w in weights) // GROUP - layers * sum(grad_rows)
    parts = [
        (layers - 1) * sum(grad_rows),
        sum(grad_rows[1:]),
        grad_rows[0] + small_rows_all,
    ]
    packed_rows = [grid.packed_rows(rows) for rows in parts]

    whole = pl.BlockSpec(memory_space=pltpu.VMEM)
    smem = pl.BlockSpec(memory_space=pltpu.SMEM)
    anywhere = pl.BlockSpec(memory_space=pl.ANY)
    block = pl.BlockSpec((1, tok, dim), lambda i: (i, 0, 0))
    canonical = pl.BlockSpec((1, ROWS, dim), lambda i: (i, 0, 0))
    shapes = state_shapes(dim, ff)
    packed_types = [jax.ShapeDtypeStruct((rows, GROUP), bf16) for rows in packed_rows]
    out, e, *totals = pl.pallas_call(
        partial(main_kernel, grid),
        grid=(images,),
        out_shape=[
            jax.ShapeDtypeStruct((images, ROWS, dim), bf16),
            jax.ShapeDtypeStruct((images, ROWS, dim), f32),
        ]
        + packed_types,
        in_specs=[smem, block, block] + [whole] * len(weights),
        out_specs=[canonical, canonical] + [anywhere] * len(packed_rows),
        scratch_shapes=[pltpu.VMEM(part.shape, bf16) for part in packed_types]
        + [pltpu.SemaphoreType.DMA((3,))]
        + layers
        * (
            [pltpu.VMEM(*shapes[name]) for name in STATE + STATE_FEED]
            + grad_scratch(dim, ff)
            + acc_scratch(dim, ff)
        )
        + shared_scratch(dim)
        + [
            pltpu.VMEM((dim // GROUP, tok + 16, GROUP), f32),
            pltpu.VMEM((ROWS, dim), f32),
            pltpu.VMEM((ROWS, dim), f32),
            pltpu.VMEM((ROWS, dim), f32),
            pltpu.VMEM((layers, 16, ff), f32),
        ]
        + [scratch for rows in parts for scratch in grid.scratch(rows)],
        compiler_params=pltpu.CompilerParams(
            dimension_semantics=("arbitrary",),
            collective_id=0,
            has_side_effects=True,
            vmem_limit_bytes=VMEM_LIMIT,
        ),
    )(crop_side, tokens, cotangent, *weights)

    factor = 1.0 / math.sqrt(devices * images * tok)
    big = (2, 5, 9, 11)
    return pl.pallas_call(
        partial(last_kernel, factor, images),
        grid=(images,),
        out_shape=[
            jax.ShapeDtypeStruct(tokens.shape, bf16),
            jax.ShapeDtypeStruct(tokens.shape, f32),
        ]
        + [jax.ShapeDtypeStruct(w.shape, f32) for w in weights],
        in_specs=[smem, canonical, canonical] + [anywhere] * len(totals),
        out_specs=[block, block]
        + [anywhere if i in big else whole for i in range(len(weights))],
        scratch_shapes=[pltpu.VMEM((2, dim // GROUP, tok + 16, GROUP), f32)]
        + [pltpu.VMEM(part.shape, bf16) for part in packed_types]
        + [pltpu.VMEM(weights[i].shape, f32) for i in big]
        + [pltpu.SemaphoreType.DMA((3,)), pltpu.SemaphoreType.DMA((4, layers))],
        compiler_params=pltpu.CompilerParams(
            dimension_semantics=("arbitrary",), vmem_limit_bytes=VMEM_LIMIT
        ),
    )(crop_side, out, e, *totals)


def solution(mesh):
    sharded = P(("dp", "head"), None, None)
    return jax.shard_map(
        local,
        mesh=mesh,
        in_specs=(sharded, P(("dp", "head"), None), sharded) + (P(),) * 13,
        out_specs=(sharded, sharded) + (P(),) * 13,
        check_vma=False,
    )
```
